32 devices in a mesh: gx: 4 (over x, core), gy: 4 (over z), gz: 2 (over y).
Axes of the slice: x: 2, y: 2, z: 4, core: 2. Of those that a mesh axis runs over, the one named last changes fastest.
Arguments:
- e_forward: float32 [3, 64, 128, 256], P(None, 'gx', 'gy', 'gz'), may hold values from -6 to 6
- h_forward: float32 [3, 64, 128, 256], P(None, 'gx', 'gy', 'gz'), may hold values from -6 to 6
- e_adjoint: float32 [3, 64, 128, 256], P(None, 'gx', 'gy', 'gz'), may hold values from -6 to 6
- h_adjoint: float32 [3, 64, 128, 256], P(None, 'gx', 'gy', 'gz'), may hold values from -6 to 6
- material: int32 [64, 128, 256], P('gx', 'gy', 'gz'), may hold values from 0 to 3
- dft_forward: float32 [3, 2, 3, 96, 64, 128], P(None, None, None, 'gz', 'gx', 'gy'), may hold values from -6 to 6
- dft_adjoint: float32 [3, 2, 3, 96, 64, 128], P(None, None, None, 'gz', 'gx', 'gy'), may hold values from -6 to 6
- angular_freq: float32 [3], replicated, may hold values from 0.05 to 0.6
- layer_map: int32 [96], replicated, may hold values from 0 to 15, as said below
Outputs:
- e_forward_new: float32 [3, 64, 128, 256], P(None, 'gx', 'gy', 'gz')
- h_forward_new: float32 [3, 64, 128, 256], P(None, 'gx', 'gy', 'gz')
- e_adjoint_new: float32 [3, 64, 128, 256], P(None, 'gx', 'gy', 'gz')
- h_adjoint_new: float32 [3, 64, 128, 256], P(None, 'gx', 'gy', 'gz')
- gradient: float32 [16, 64, 128], P('gz', 'gx', 'gy')
The draws below stay inside these ranges and needn't reach their ends.
Inputs may be any that keep to these rules, and one draw needn't show every extreme that they name: `layer_map`: every design layer owns one contiguous nonempty run of the 96 slab cells; the runs' order along the slab is arbitrary.
All inputs are finite; a program needn't handle non-finite values.
Results may differ from the reference program's by a relative error of at most 0.000073.
Values sent between devices are 32-bit elements; how exact they have to be, the bound alone decides.
No kernel may reach another device: no remote copies, remote signals or barrier semaphores. Data moves between devices by JAX's collectives and lax.ppermute only.
A program may use at most 128 MiB of HBM per device.

```python
import math
import jax
import jax.numpy as jnp
from jax import lax

SLAB = 96
LAYERS = 16
FREQS = 3
STEP = 40
NX = 64
NY = 128
NZ = 256


def draw_layer_map(key, part):
    first_key, second_key = jax.random.split(jax.random.fold_in(key, 11))
    picks = jax.random.permutation(first_key, SLAB - 1)[:LAYERS - 1] + 1
    cuts = jnp.sort(picks)
    run_number = jnp.sum(jnp.arange(SLAB)[:, None] >= cuts[None, :], axis=1)
    ordering = jax.random.permutation(second_key, LAYERS)
    return ordering[run_number].astype(jnp.int32)


def place_ends(array, rng, least, top_value):
    longest = array.shape.index(max(array.shape))
    spots = []
    for shift in (0, 1):
        where = [jax.random.randint(jax.random.fold_in(rng, axis), (), 0, length) for axis, length in enumerate(array.shape)]
        where[longest] = (where[longest] + shift) % array.shape[longest]
        spots.append(tuple(where))
    return array.at[spots[0]].set(least).at[spots[1]].set(top_value)


def block_levels(rng, dims, cuts, low, largest):
    loudness, own = 1.0, jax.random.fold_in(rng, 6)
    for position, shards_of in cuts:
        draws = jnp.exp(jax.random.uniform(jax.random.fold_in(own, position), (shards_of,), jnp.float32, low / len(cuts), largest / len(cuts)))
        loudness = loudness * jnp.repeat(draws, dims[position] // shards_of).reshape([-1 if axis == position else 1 for axis in range(len(dims))])
    return loudness


def noise(own_key, dims, scale, most, cuts=(), kind=jnp.bfloat16):
    drawn = jax.random.normal(own_key, dims, jnp.float32) * scale
    if len(cuts) > 0:
        drawn = block_levels(own_key, dims, cuts, -0.22, 0.18) * drawn
    return jnp.clip(drawn, min=-most, max=most).astype(kind)


def setup_inputs(seed: int = 0) -> dict:
    key_of = jax.random.split(jax.random.key(seed), 10)
    e_forward = noise(key_of[0], (3, NX, NY, NZ), 1.0, 6.0, ((1, 4), (2, 4), (3, 2)), jnp.float32)
    h_forward = noise(key_of[1], (3, NX, NY, NZ), 1.0, 6.0, ((1, 4), (2, 4), (3, 2)), jnp.float32)
    e_adjoint = noise(key_of[2], (3, NX, NY, NZ), 1.0, 6.0, ((1, 4), (2, 4), (3, 2)), jnp.float32)
    h_adjoint = noise(key_of[3], (3, NX, NY, NZ), 1.0, 6.0, ((1, 4), (2, 4), (3, 2)), jnp.float32)
    material = place_ends(jax.random.randint(key_of[4], (NX, NY, NZ), 0, 4), jax.random.fold_in(key_of[4], 1), 0, 3).astype(jnp.int32)
    dft_forward = noise(key_of[5], (FREQS, 2, 3, SLAB, NX, NY), 1.0, 6.0, ((3, 2), (4, 4), (5, 4)), jnp.float32)
    dft_adjoint = noise(key_of[6], (FREQS, 2, 3, SLAB, NX, NY), 1.0, 6.0, ((3, 2), (4, 4), (5, 4)), jnp.float32)
    angular_freq = jnp.clip(jnp.exp(jax.random.uniform(key_of[7], (FREQS,), jnp.float32, math.log(0.05), math.log(0.6))), 0.05, 0.6)
    layer_map = draw_layer_map(jax.random.fold_in(key_of[9], 71), 0)
    return dict(e_forward=e_forward, h_forward=h_forward, e_adjoint=e_adjoint, h_adjoint=h_adjoint, material=material, dft_forward=dft_forward, dft_adjoint=dft_adjoint, angular_freq=angular_freq, layer_map=layer_map)


PERMITTIVITIES = (1.0, 2.1, 4.0, 12.0)
COURANT = 0.5


def update_coefficient(material):
    result = jnp.zeros(material.shape, jnp.float32)
    for material_id, value_eps in enumerate(PERMITTIVITIES):
        result = result + jnp.where(material == material_id, COURANT / value_eps, 0.0).astype(jnp.float32)
    return result


def curl_forward(field_e, uppers):
    above_x, above_y, above_z = uppers
    comp_x = (above_y[..., 2, :, :, :] - field_e[..., 2, :, :, :]) - (above_z[..., 1, :, :, :] - field_e[..., 1, :, :, :])
    comp_y = (above_z[..., 0, :, :, :] - field_e[..., 0, :, :, :]) - (above_x[..., 2, :, :, :] - field_e[..., 2, :, :, :])
    comp_z = (above_x[..., 1, :, :, :] - field_e[..., 1, :, :, :]) - (above_y[..., 0, :, :, :] - field_e[..., 0, :, :, :])
    return jnp.stack([comp_x, comp_y, comp_z], axis=-4)


def curl_backward(field_h, lowers):
    below_x, below_y, below_z = lowers
    comp_x = (field_h[..., 2, :, :, :] - below_y[..., 2, :, :, :]) - (field_h[..., 1, :, :, :] - below_z[..., 1, :, :, :])
    comp_y = (field_h[..., 0, :, :, :] - below_z[..., 0, :, :, :]) - (field_h[..., 2, :, :, :] - below_x[..., 2, :, :, :])
    comp_z = (field_h[..., 1, :, :, :] - below_x[..., 1, :, :, :]) - (field_h[..., 0, :, :, :] - below_y[..., 0, :, :, :])
    return jnp.stack([comp_x, comp_y, comp_z], axis=-4)


def upper_cells(source, direction):
    if direction == 3:
        return jnp.concatenate([source[..., 1:], jnp.zeros_like(source[..., :1])], axis=3)
    return jnp.roll(source, -1, axis=direction)


def lower_cells(source, direction):
    if direction == 3:
        return jnp.concatenate([jnp.zeros_like(source[..., :1]), source[..., :-1]], axis=3)
    return jnp.roll(source, 1, axis=direction)


def advance(field_e, field_h, coefficient):
    uppers = tuple(upper_cells(field_e, direction) for direction in (1, 2, 3))
    new_h = field_h - COURANT * curl_forward(field_e, uppers)
    lowers = tuple(lower_cells(new_h, direction) for direction in (1, 2, 3))
    new_e = field_e + coefficient * curl_backward(new_h, lowers)
    return new_e, new_h


def reference(e_forward, h_forward, e_adjoint, h_adjoint, material, dft_forward, dft_adjoint, angular_freq, layer_map):
    coefficient = update_coefficient(material)
    e_fwd_new, h_fwd_new = advance(e_forward, h_forward, coefficient)
    e_adj_new, h_adj_new = advance(e_adjoint, h_adjoint, coefficient)
    slab_start = NZ // 2 - SLAB // 2
    phases = angular_freq * STEP
    cosine = jnp.cos(phases)[:, None, None, None, None]
    sine_term = jnp.sin(phases)[:, None, None, None, None]
    slab_fwd = jnp.transpose(e_fwd_new[:, :, :, slab_start:slab_start + SLAB], (0, 3, 1, 2))
    slab_adj = jnp.transpose(e_adj_new[:, :, :, slab_start:slab_start + SLAB], (0, 3, 1, 2))
    real_fwd = dft_forward[:, 0] + cosine * slab_fwd[None]
    imag_fwd = dft_forward[:, 1] - sine_term * slab_fwd[None]
    real_adj = dft_adjoint[:, 0] + cosine * slab_adj[None]
    imag_adj = dft_adjoint[:, 1] - sine_term * slab_adj[None]
    products = jnp.sum(real_fwd * real_adj - imag_fwd * imag_adj, axis=(0, 1))
    layers_onehot = (layer_map[None, :] == jnp.arange(LAYERS, dtype=jnp.int32)[:, None]).astype(jnp.float32)
    thickness = jnp.sum(layers_onehot, axis=1)
    summed = jnp.einsum("ls,sxy->lxy", layers_onehot, products, precision=lax.Precision.HIGHEST)
    gradient = summed / (3.0 * thickness)[:, None, None]
    return e_fwd_new, h_fwd_new, e_adj_new, h_adj_new, gradient
```

```python
import functools

import jax
import jax.numpy as jnp
from jax import lax
from jax.experimental import pallas as pl
from jax.experimental.pallas import tpu as pltpu
from jax.sharding import PartitionSpec as P

LAYERS = 16
STEP = 40
PERMITTIVITIES = (1.0, 2.1, 4.0, 12.0)
COURANT = 0.5
LANES = 128
VMEM_LIMIT = 48 * 1024 * 1024
ANY = pl.BlockSpec(memory_space=pl.ANY)
VMEM = pl.BlockSpec(memory_space=pltpu.VMEM)


def f32(*shape):
    return jax.ShapeDtypeStruct(shape, jnp.float32)


def ring(x, axis, by):
    peers = lax.axis_size(axis)
    return lax.ppermute(x, axis, [(i, (i + by) % peers) for i in range(peers)])


def line(x, axis, by):
    peers = lax.axis_size(axis)
    return lax.ppermute(x, axis, [(i, i + by) for i in range(peers) if 0 <= i + by < peers])


def call(body, outs, out_specs, in_specs, scratch, flops, nbytes, name):
    return pl.pallas_call(
        body,
        out_shape=outs,
        in_specs=in_specs,
        out_specs=out_specs,
        scratch_shapes=scratch,
        compiler_params=pltpu.CompilerParams(vmem_limit_bytes=VMEM_LIMIT),
        cost_estimate=pl.CostEstimate(flops=flops, bytes_accessed=nbytes, transcendentals=0),
        name=name,
    )


def lane_ids(rows):
    return lax.broadcasted_iota(jnp.int32, (rows, LANES), 1)


def row_ids(rows):
    return lax.broadcasted_iota(jnp.int32, (rows, LANES), 0)


def column(a, lane):
    return jnp.broadcast_to(a[:, lane : lane + 1], a.shape)


def up_y(a, row):
    n = a.shape[0]
    return jnp.where(row_ids(n) == n - 1, jnp.broadcast_to(row, a.shape), pltpu.roll(a, n - 1, 0))


def down_y(a, row):
    return jnp.where(row_ids(a.shape[0]) == 0, jnp.broadcast_to(row, a.shape), pltpu.roll(a, 1, 0))


def up_z(a, col):
    n = a.shape[1]
    return jnp.where(lane_ids(a.shape[0]) == n - 1, col, pltpu.roll(a, n - 1, 1))


def down_z(a, col):
    return jnp.where(lane_ids(a.shape[0]) == 0, col, pltpu.roll(a, 1, 1))


def first_faces_body(nx, chunk, ef, ea, xs, ys, zs, xy, zrow, sems):
    fields = (ef, ea)
    copies = {}
    for r, e in enumerate(fields):
        copies[r, "x"] = pltpu.make_async_copy(e.at[1:3, 0], xs.at[r], sems.at[r, 0])
        copies[r, "z"] = pltpu.make_async_copy(e.at[2, :, 0:8], zrow.at[r], sems.at[r, 1])
        for i in range(nx // chunk):
            part = pl.ds(i * chunk, chunk)
            copies[r, i] = pltpu.make_async_copy(e.at[0:2, part], xy.at[r, :, part], sems.at[r, 2 + i])
    for i in range(nx // chunk):
        for r in range(2):
            copies[r, i].start()
    for r in range(2):
        copies[r, "x"].start()
        copies[r, "z"].start()
    ny = xy.shape[3]
    lane = lane_ids(ny)
    total = jnp.zeros((ny, LANES), jnp.float32)
    for i in range(nx // chunk):
        for r in range(2):
            copies[r, i].wait()
            for x in range(i * chunk, (i + 1) * chunk):
                for c in range(2):
                    a = xy[r, c, x]
                    total = jnp.where(lane == (r * 2 + c) * nx + x, column(a, 0), total)
                ys[r, 0, x : x + 1, :] = xy[r, 0, x, 0:1, :]
    zs[...] = total
    for r in range(2):
        copies[r, "x"].wait()
        copies[r, "z"].wait()
        for x in range(nx):
            ys[r, 1, x : x + 1, :] = zrow[r, x, 0:1, :]


def first_faces(ef, ea):
    _, nx, ny, nz = ef.shape
    chunk = 4
    return call(
        functools.partial(first_faces_body, nx, chunk),
        (f32(2, 2, ny, nz), f32(2, 2, nx, nz), f32(ny, LANES)),
        (VMEM, VMEM, VMEM),
        [ANY, ANY],
        [
            pltpu.VMEM((2, 2, nx, ny, nz), jnp.float32),
            pltpu.VMEM((2, nx, 8, nz), jnp.float32),
            pltpu.SemaphoreType.DMA((2, 2 + nx // chunk)),
        ],
        1000,
        1500000,
        "first_faces",
    )(ef, ea)


def magnetic_body(nx, chunk, ef, hf, ea, ha, xr, yr, zr, hfn, han, xs, ys, zs, ev, hv, insem, outsem):
    runs = ((ef, hf, hfn), (ea, ha, han))
    ny, nz = ev.shape[3], ev.shape[4]
    n = nx // chunk
    copies, outs = {}, {}
    for i in range(n):
        part = pl.ds(i * chunk, chunk)
        for r, (e, h, hn) in enumerate(runs):
            copies[r, i, 0] = pltpu.make_async_copy(e.at[:, part], ev.at[r, :, part], insem.at[r, i, 0])
            copies[r, i, 1] = pltpu.make_async_copy(h.at[:, part], hv.at[r, :, part], insem.at[r, i, 1])
            outs[r, i] = pltpu.make_async_copy(hv.at[r, :, part], hn.at[:, part], outsem.at[r, i])
    for i in range(n):
        for r in range(2):
            copies[r, i, 0].start()
            copies[r, i, 1].start()
    lane = lane_ids(ny)
    total = jnp.zeros((ny, LANES), jnp.float32)
    zcol = zr[...]
    for i in range(n):
        for r in range(2):
            if i == 0:
                copies[r, 0, 0].wait()
            copies[r, i, 1].wait()
            if i + 1 < n:
                copies[r, i + 1, 0].wait()
            for x in range(i * chunk, (i + 1) * chunk):
                ex, ey, ez = ev[r, 0, x], ev[r, 1, x], ev[r, 2, x]
                ey_x, ez_x = (ev[r, 1, x + 1], ev[r, 2, x + 1]) if x + 1 < nx else (xr[r, 0], xr[r, 1])
                ex_y = up_y(ex, yr[r, 0, x : x + 1, :])
                ez_y = up_y(ez, yr[r, 1, x : x + 1, :])
                ex_z = up_z(ex, column(zcol, (r * 2 + 0) * nx + x))
                ey_z = up_z(ey, column(zcol, (r * 2 + 1) * nx + x))
                hx = hv[r, 0, x] - COURANT * ((ez_y - ez) - (ey_z - ey))
                hy = hv[r, 1, x] - COURANT * ((ex_z - ex) - (ez_x - ez))
                hz = hv[r, 2, x] - COURANT * ((ey_x - ey) - (ex_y - ex))
                hv[r, 0, x] = hx
                hv[r, 1, x] = hy
                hv[r, 2, x] = hz
                ys[r, 0, x : x + 1, :] = hx[ny - 1 : ny, :]
                ys[r, 1, x : x + 1, :] = hz[ny - 1 : ny, :]
                total = jnp.where(lane == (r * 2 + 0) * nx + x, column(hx, nz - 1), total)
                total = jnp.where(lane == (r * 2 + 1) * nx + x, column(hy, nz - 1), total)
                if x == nx - 1:
                    xs[r, 0] = hy
                    xs[r, 1] = hz
            outs[r, i].start()
    zs[...] = total
    for i in range(n):
        for r in range(2):
            outs[r, i].wait()


def magnetic(ef, hf, ea, ha, xr, yr, zr):
    _, nx, ny, nz = ef.shape
    chunk = 4
    field = f32(3, nx, ny, nz)
    return call(
        functools.partial(magnetic_body, nx, chunk),
        (field, field, f32(2, 2, ny, nz), f32(2, 2, nx, nz), f32(ny, LANES)),
        (ANY, ANY, VMEM, VMEM, VMEM),
        [ANY, ANY, ANY, ANY, VMEM, VMEM, VMEM],
        [
            pltpu.VMEM((2, 3, nx, ny, nz), jnp.float32),
            pltpu.VMEM((2, 3, nx, ny, nz), jnp.float32),
            pltpu.SemaphoreType.DMA((2, nx // chunk, 2)),
            pltpu.SemaphoreType.DMA((2, nx // chunk)),
        ],
        6000000,
        4800000,
        "magnetic",
    )(ef, hf, ea, ha, xr, yr, zr)


def slab_start(nz, half):
    return (1 - lax.axis_index("gz")) * (nz - half)


def spectra_body(half, nz, df, da, freq, out):
    phase = freq[...] * float(STEP)
    cos, sin = jnp.cos(phase), jnp.sin(phase)
    freqs, xc, ny = df.shape[0], df.shape[3], df.shape[4]
    shift = slab_start(nz, half)
    blank = jnp.zeros((ny, LANES - half), jnp.float32)

    def place(a):
        return pltpu.roll(jnp.concatenate([a, blank], axis=1), shift, 1)

    cs = [jnp.broadcast_to(cos[:, f : f + 1], (ny, half)) for f in range(freqs)]
    sn = [jnp.broadcast_to(sin[:, f : f + 1], (ny, half)) for f in range(freqs)]
    for x in range(xc):
        base = jnp.zeros((ny, half), jnp.float32)
        for c in range(3):
            with_forward = jnp.zeros((ny, half), jnp.float32)
            with_adjoint = jnp.zeros((ny, half), jnp.float32)
            for f in range(freqs):
                rf, jf, ra, ja = df[f, 0, c, x], df[f, 1, c, x], da[f, 0, c, x], da[f, 1, c, x]
                base = base + (rf * ra - jf * ja)
                with_forward = with_forward + (cs[f] * ra + sn[f] * ja)
                with_adjoint = with_adjoint + (cs[f] * rf + sn[f] * jf)
            out[1 + c, x] = place(with_forward)
            out[4 + c, x] = place(with_adjoint)
        out[0, x] = place(base)


def spectra(df, da, freq, nz):
    freqs, _, _, nx, ny, half = df.shape
    chunk = 2
    spec = pl.BlockSpec((freqs, 2, 3, chunk, ny, half), lambda i: (0, 0, 0, i, 0, 0))
    return pl.pallas_call(
        functools.partial(spectra_body, half, nz),
        out_shape=f32(7, nx, ny, LANES),
        grid=(nx // chunk,),
        in_specs=[spec, spec, pl.BlockSpec((1, freqs), lambda i: (0, 0))],
        out_specs=pl.BlockSpec((7, chunk, ny, LANES), lambda i: (0, i, 0, 0)),
        compiler_params=pltpu.CompilerParams(vmem_limit_bytes=VMEM_LIMIT),
        cost_estimate=pl.CostEstimate(flops=10000000, bytes_accessed=11000000, transcendentals=0),
        name="spectra",
    )(df, da, freq)


def electric_body(
    nx, chunk, half, ef, ea, hf, ha, material, xr, yr, zr, spec, freq, layer_map,
    efn, ean, own, other, ev, hv, mv, sv, insem, outsem,
):
    runs = ((ef, hf, efn), (ea, ha, ean))
    ny, nz = ev.shape[3], ev.shape[4]
    n = nx // chunk
    copies, outs = {}, {}
    for i in range(n):
        part = pl.ds(i * chunk, chunk)
        for r, (e, h, en) in enumerate(runs):
            copies[i, r] = pltpu.make_async_copy(h.at[:, part], hv.at[r, :, part], insem.at[i, r])
            copies[i, 2 + r] = pltpu.make_async_copy(e.at[:, part], ev.at[r, :, part], insem.at[i, 2 + r])
            outs[i, r] = pltpu.make_async_copy(ev.at[r, :, part], en.at[:, part], outsem.at[i, r])
        copies[i, 4] = pltpu.make_async_copy(material.at[part], mv.at[part], insem.at[i, 4])
        copies[i, 5] = pltpu.make_async_copy(spec.at[:, part], sv.at[:, part], insem.at[i, 5])
    for i in range(n):
        for k in range(6):
            copies[i, k].start()
    phase = freq[...] * float(STEP)
    cos, sin = jnp.cos(phase), jnp.sin(phase)
    both = jnp.sum(cos * cos - sin * sin, axis=1, keepdims=True)
    gz = lax.axis_index("gz")
    start = slab_start(nz, half)
    slab = layer_map.shape[1]
    cells = jnp.concatenate([layer_map[...], jnp.full((1, LANES - slab), -1, jnp.int32)], axis=1)
    cells = pltpu.roll(jnp.broadcast_to(cells, (8, LANES)), lax.rem(start + LANES - gz * half, LANES), 1)
    owned = own.shape[0]
    lane = lane_ids(owned)
    inside = (lane >= start) & (lane < start + half)
    cells = jnp.broadcast_to(cells[0:1, :], (owned, LANES))
    layer = row_ids(owned)
    own_hot = jnp.where(inside & (cells == layer + gz * owned), 1.0, 0.0)
    other_hot = jnp.where(inside & (cells == layer + (1 - gz) * owned), 1.0, 0.0)
    zcol = zr[...]
    for i in range(n):
        for k in range(6):
            copies[i, k].wait()
        products = []
        for x in range(i * chunk, (i + 1) * chunk):
            m = mv[x]
            coefficient = jnp.where(
                m == 0,
                COURANT / PERMITTIVITIES[0],
                jnp.where(
                    m == 1,
                    COURANT / PERMITTIVITIES[1],
                    jnp.where(m == 2, COURANT / PERMITTIVITIES[2], COURANT / PERMITTIVITIES[3]),
                ),
            )
            news = []
            for r in range(2):
                hx, hy, hz = hv[r, 0, x], hv[r, 1, x], hv[r, 2, x]
                hy_x, hz_x = (hv[r, 1, x - 1], hv[r, 2, x - 1]) if x else (xr[r, 0], xr[r, 1])
                hx_y = down_y(hx, yr[r, 0, x : x + 1, :])
                hz_y = down_y(hz, yr[r, 1, x : x + 1, :])
                hx_z = down_z(hx, column(zcol, (r * 2 + 0) * nx + x))
                hy_z = down_z(hy, column(zcol, (r * 2 + 1) * nx + x))
                ex = ev[r, 0, x] + coefficient * ((hz - hz_y) - (hy - hy_z))
                ey = ev[r, 1, x] + coefficient * ((hx - hx_z) - (hz - hz_x))
                ez = ev[r, 2, x] + coefficient * ((hy - hy_x) - (hx - hx_y))
                ev[r, 0, x] = ex
                ev[r, 1, x] = ey
                ev[r, 2, x] = ez
                news.append((ex, ey, ez))
            total = sv[0, x]
            for c in range(3):
                f, a = news[0][c], news[1][c]
                total = total + (f * (sv[1 + c, x] + both * a) + a * sv[4 + c, x])
            products.append(total)
        for r in range(2):
            outs[i, r].start()
        block = jnp.concatenate(products, axis=0)
        dims = (((1,), (1,)), ((), ()))
        where = pl.ds(i * chunk * ny, chunk * ny)
        for hot, result in ((own_hot, own), (other_hot, other)):
            result[:, where] = lax.dot_general(
                hot, block, dims, precision=lax.Precision.HIGHEST, preferred_element_type=jnp.float32
            )
    for i in range(n):
        for r in range(2):
            outs[i, r].wait()


def electric(ef, ea, hf, ha, material, xr, yr, zr, spec, freq, layer_map, half, owned):
    _, nx, ny, nz = ef.shape
    chunk = 4
    field = f32(3, nx, ny, nz)
    return call(
        functools.partial(electric_body, nx, chunk, half),
        (field, field, f32(owned, nx * ny), f32(owned, nx * ny)),
        (ANY, ANY, VMEM, VMEM),
        [ANY, ANY, ANY, ANY, ANY, VMEM, VMEM, VMEM, ANY, VMEM, VMEM],
        [
            pltpu.VMEM((2, 3, nx, ny, nz), jnp.float32),
            pltpu.VMEM((2, 3, nx, ny, nz), jnp.float32),
            pltpu.VMEM((nx, ny, nz), jnp.int32),
            pltpu.VMEM((7, nx, ny, LANES), jnp.float32),
            pltpu.SemaphoreType.DMA((nx // chunk, 6)),
            pltpu.SemaphoreType.DMA((nx // chunk, 2)),
        ],
        9000000,
        6700000,
        "electric",
    )(ef, ea, hf, ha, material, xr, yr, zr, spec, freq, layer_map)


def gradient_body(own, came, layer_map, out):
    owned, nx, ny = out.shape
    slab = layer_map.shape[1]
    layer = lax.broadcasted_iota(jnp.int32, (owned, slab), 0) + lax.axis_index("gz") * owned
    same = jnp.where(jnp.broadcast_to(layer_map[...], (owned, slab)) == layer, 1.0, 0.0)
    thickness = jnp.sum(same, axis=1, keepdims=True)
    result = (own[...] + came[...]) / (3.0 * thickness)
    for x in range(nx):
        out[:, x, :] = result[:, x * ny : (x + 1) * ny]


def gradient(own, came, layer_map, nx, ny):
    owned = own.shape[0]
    return call(
        gradient_body,
        f32(owned, nx, ny),
        VMEM,
        [VMEM, VMEM, VMEM],
        [],
        10000,
        100000,
        "gradient",
    )(own, came, layer_map)


def shards(ef, hf, ea, ha, material, df, da, angular_freq, layer_map):
    _, nx, ny, nz = ef.shape
    half = df.shape[3]
    owned = LAYERS // lax.axis_size("gz")
    freq = angular_freq.reshape(1, -1)
    layer_map = layer_map.reshape(1, -1)
    df = jnp.transpose(df, (0, 1, 2, 4, 5, 3))
    da = jnp.transpose(da, (0, 1, 2, 4, 5, 3))
    xs, ys, zs = first_faces(ef, ea)
    yr = ring(ys, "gy", -1)
    xr = ring(xs, "gx", -1)
    zr = line(zs, "gz", -1)
    spec = spectra(df, da, freq, nz)
    hfn, han, xs, ys, zs = magnetic(ef, hf, ea, ha, xr, yr, zr)
    yr = ring(ys, "gy", 1)
    xr = ring(xs, "gx", 1)
    zr = line(zs, "gz", 1)
    efn, ean, own, other = electric(ef, ea, hfn, han, material, xr, yr, zr, spec, freq, layer_map, half, owned)
    came = ring(other, "gz", 1)
    return efn, hfn, ean, han, gradient(own, came, layer_map, nx, ny)


def solution(mesh):
    field = P(None, "gx", "gy", "gz")
    dft = P(None, None, None, "gz", "gx", "gy")
    return jax.shard_map(
        shards,
        mesh=mesh,
        in_specs=(field, field, field, field, P("gx", "gy", "gz"), dft, dft, P(), P()),
        out_specs=(field, field, field, field, P("gz", "gx", "gy")),
        check_vma=False,
    )
```

```python
import functools

import jax
import jax.numpy as jnp
from jax import lax
from jax.experimental import pallas as pl
from jax.experimental.pallas import tpu as pltpu
from jax.sharding import PartitionSpec as P

LAYERS = 16
STEP = 40
PERMITTIVITIES = (1.0, 2.1, 4.0, 12.0)
COURANT = 0.5
LANES = 128
MIB = 1024 * 1024
ANY = pl.BlockSpec(memory_space=pl.ANY)
VMEM = pl.BlockSpec(memory_space=pltpu.VMEM)


def f32(*shape):
    return jax.ShapeDtypeStruct(shape, jnp.float32)


def vmem(*shape):
    return pltpu.VMEM(shape, jnp.float32)


def hbm(x):
    return pltpu.with_memory_space_constraint(x, pltpu.HBM)


def ring(x, axis, by):
    peers = lax.axis_size(axis)
    return lax.ppermute(x, axis, [(i, (i + by) % peers) for i in range(peers)])


def line(x, axis, by):
    peers = lax.axis_size(axis)
    return lax.ppermute(x, axis, [(i, i + by) for i in range(peers) if 0 <= i + by < peers])


def call(body, name, outs, out_specs, in_specs, scratch=(), nbytes=100000, limit=32):
    return pl.pallas_call(
        body,
        out_shape=outs,
        in_specs=in_specs,
        out_specs=out_specs,
        scratch_shapes=list(scratch),
        compiler_params=pltpu.CompilerParams(vmem_limit_bytes=limit * MIB),
        cost_estimate=pl.CostEstimate(flops=nbytes, bytes_accessed=nbytes, transcendentals=0),
        name=name,
    )


def lane_ids(rows):
    return lax.broadcasted_iota(jnp.int32, (rows, LANES), 1)


def row_ids(rows):
    return lax.broadcasted_iota(jnp.int32, (rows, LANES), 0)


def move(a, source, target):
    shift = (target - source) % LANES
    return pltpu.roll(a, shift, 1) if shift else a


def up_y(a, row):
    n = a.shape[0]
    return jnp.where(row_ids(n) == n - 1, jnp.broadcast_to(row, a.shape), pltpu.roll(a, n - 1, 0))


def down_y(a, row):
    return jnp.where(row_ids(a.shape[0]) == 0, jnp.broadcast_to(row, a.shape), pltpu.roll(a, 1, 0))


def up_z(a, packed, lane):
    n = a.shape[1]
    return jnp.where(lane_ids(a.shape[0]) == n - 1, move(packed, lane, n - 1), pltpu.roll(a, n - 1, 1))


def down_z(a, packed, lane):
    return jnp.where(lane_ids(a.shape[0]) == 0, move(packed, lane, 0), pltpu.roll(a, 1, 1))


def first_faces_body(ef, ea, xs, ys, zs, evf, eva, sems):
    fields = ((ef, evf), (ea, eva))
    _, nx, ny, _ = ef.shape
    copies = {}
    for c in range(3):
        for r, (e, v) in enumerate(fields):
            copies[c, r] = pltpu.make_async_copy(e.at[c], v.at[c], sems.at[r, c])
            copies[c, r].start()
    lane = lane_ids(ny)
    total = jnp.zeros((ny, LANES), jnp.float32)
    for c in range(3):
        for r, (_, v) in enumerate(fields):
            copies[c, r].wait()
            for x in range(nx):
                if c < 2:
                    to = (r * 2 + c) * nx + x
                    total = jnp.where(lane == to, move(v[c, x], 0, to), total)
                if c != 1:
                    ys[r, c // 2, x : x + 1, :] = v[c, x, 0:1, :]
            if c:
                xs[r, c - 1] = v[c, 0]
    zs[...] = total


def first_faces(ef, ea):
    _, nx, ny, nz = ef.shape
    field = vmem(3, nx, ny, nz)
    return call(
        first_faces_body,
        "first_faces",
        (vmem(2, 2, ny, nz), vmem(2, 2, nx, nz), vmem(ny, LANES), field, field),
        (VMEM,) * 5,
        [ANY, ANY],
        [pltpu.SemaphoreType.DMA((2, 3))],
        nbytes=1500000,
    )(hbm(ef), hbm(ea))


def transfer_body(n, *refs):
    sems = refs[-1]
    copies = []
    for k, (a, b) in enumerate(zip(refs[:n], refs[-1 - n : -1], strict=True)):
        for c in range(a.shape[0]):
            copies.append(pltpu.make_async_copy(a.at[c], b.at[c], sems.at[k, c]))
    for copy in copies:
        copy.start()
    for copy in copies:
        copy.wait()


def load(fields, after):
    n = len(fields)
    return call(
        functools.partial(transfer_body, n),
        "load",
        tuple(vmem(*f.shape) for f in fields),
        (VMEM,) * n,
        [ANY] * (n + 1),
        [pltpu.SemaphoreType.DMA((n, 3))],
        nbytes=1500000,
    )(*[hbm(f) for f in fields], after)


def store(fields, after):
    n = len(fields)
    return call(
        functools.partial(transfer_body, n),
        "store",
        tuple(f32(*f.shape) for f in fields),
        (ANY,) * n,
        [VMEM] * n + [ANY],
        [pltpu.SemaphoreType.DMA((n, 3))],
        nbytes=3000000,
    )(*fields, after)


def magnetic_body(ef, ea, hf, ha, xr, yr, zr, hfn, han, xs, ys, zs):
    runs = ((ef, hf, hfn), (ea, ha, han))
    _, nx, ny, nz = ef.shape
    packed = zr[...]
    for x in range(nx):
        for r, (e, h, hn) in enumerate(runs):
            ex, ey, ez = e[0, x], e[1, x], e[2, x]
            ey_x, ez_x = (e[1, x + 1], e[2, x + 1]) if x + 1 < nx else (xr[r, 0], xr[r, 1])
            ex_y = up_y(ex, yr[r, 0, x : x + 1, :])
            ez_y = up_y(ez, yr[r, 1, x : x + 1, :])
            ex_z = up_z(ex, packed, (r * 2 + 0) * nx + x)
            ey_z = up_z(ey, packed, (r * 2 + 1) * nx + x)
            hn[0, x] = h[0, x] - COURANT * ((ez_y - ez) - (ey_z - ey))
            hn[1, x] = h[1, x] - COURANT * ((ex_z - ex) - (ez_x - ez))
            hn[2, x] = h[2, x] - COURANT * ((ey_x - ey) - (ex_y - ex))
    lane = lane_ids(ny)
    total = jnp.zeros((ny, LANES), jnp.float32)
    for r, (_, _, hn) in enumerate(runs):
        for c in range(2):
            for x in range(nx):
                to = (r * 2 + c) * nx + x
                total = jnp.where(lane == to, move(hn[c, x], nz - 1, to), total)
                ys[r, c, x : x + 1, :] = hn[2 * c, x, ny - 1 : ny, :]
            xs[r, c] = hn[1 + c, nx - 1]
    zs[...] = total


def magnetic(ef, ea, hf, ha, xr, yr, zr):
    _, nx, ny, nz = ef.shape
    field = vmem(3, nx, ny, nz)
    return call(
        magnetic_body,
        "magnetic",
        (field, field, vmem(2, 2, ny, nz), vmem(2, 2, nx, nz), vmem(ny, LANES)),
        (VMEM,) * 5,
        [VMEM] * 7,
        nbytes=4800000,
    )(ef, ea, hf, ha, xr, yr, zr)


def slab_start(nz, half):
    return (1 - lax.axis_index("gz")) * (nz - half)


def spectra_body(half, nz, chunk, df, da, freq, after, out, dfv, dav, sems):
    freqs, nx, ny = df.shape[0], df.shape[3], df.shape[4]
    copies = {}
    for i in range(nx // chunk):
        part = pl.ds(i * chunk, chunk)
        for k, (d, v) in enumerate(((df, dfv), (da, dav))):
            copies[i, k] = pltpu.make_async_copy(d.at[:, :, :, part], v.at[:, :, :, part], sems.at[i, k])
            copies[i, k].start()
    phase = freq[...] * float(STEP)
    cos, sin = jnp.cos(phase), jnp.sin(phase)
    cs = [jnp.broadcast_to(cos[:, f : f + 1], (ny, half)) for f in range(freqs)]
    sn = [jnp.broadcast_to(sin[:, f : f + 1], (ny, half)) for f in range(freqs)]
    shift = slab_start(nz, half)
    blank = jnp.zeros((ny, LANES - half), jnp.float32)

    def place(a):
        return pltpu.roll(jnp.concatenate([a, blank], axis=1), shift, 1)

    for x in range(nx):
        if x % chunk == 0:
            copies[x // chunk, 0].wait()
            copies[x // chunk, 1].wait()
        base = jnp.zeros((ny, half), jnp.float32)
        for c in range(3):
            with_forward = jnp.zeros((ny, half), jnp.float32)
            with_adjoint = jnp.zeros((ny, half), jnp.float32)
            for f in range(freqs):
                rf, jf, ra, ja = dfv[f, 0, c, x], dfv[f, 1, c, x], dav[f, 0, c, x], dav[f, 1, c, x]
                base = base + (rf * ra - jf * ja)
                with_forward = with_forward + (cs[f] * ra + sn[f] * ja)
                with_adjoint = with_adjoint + (cs[f] * rf + sn[f] * jf)
            out[1 + c, x] = place(with_forward)
            out[4 + c, x] = place(with_adjoint)
        out[0, x] = place(base)


def spectra(df, da, freq, after, nz):
    freqs, _, _, nx, ny, half = df.shape
    chunk = 2
    held = vmem(*df.shape)
    return call(
        functools.partial(spectra_body, half, nz, chunk),
        "spectra",
        vmem(7, nx, ny, LANES),
        VMEM,
        [ANY, ANY, VMEM, ANY],
        [held, held, pltpu.SemaphoreType.DMA((nx // chunk, 2))],
        nbytes=11000000,
    )(hbm(df), hbm(da), freq, after)


def electric_body(half, owned, ef, ea, hf, ha, material, xr, yr, zr, spec, freq, layer_map, efn, ean, own, other):
    runs = ((ef, hf, efn), (ea, ha, ean))
    _, nx, ny, nz = ef.shape
    phase = freq[...] * float(STEP)
    cos, sin = jnp.cos(phase), jnp.sin(phase)
    both = jnp.sum(cos * cos - sin * sin, axis=1, keepdims=True)
    gz = lax.axis_index("gz")
    start = slab_start(nz, half)
    slab = layer_map.shape[1]
    cells = jnp.concatenate([layer_map[...], jnp.full((1, LANES - slab), -1, jnp.int32)], axis=1)
    cells = pltpu.roll(jnp.broadcast_to(cells, (8, LANES)), lax.rem(start + LANES - gz * half, LANES), 1)
    lane, layer = lane_ids(2 * owned), row_ids(2 * owned)
    inside = (lane >= start) & (lane < start + half)
    cells = jnp.broadcast_to(cells[0:1, :], (2 * owned, LANES))
    layer = lax.rem(layer + gz * owned, 2 * owned)
    hot = jnp.where(inside & (cells == layer), 1.0, 0.0).astype(jnp.bfloat16)
    packed = zr[...]
    dims = (((1,), (1,)), ((), ()))
    group = LANES // ny
    products = []
    for x in range(nx):
        m = material[x]
        coefficient = jnp.where(
            m == 0,
            COURANT / PERMITTIVITIES[0],
            jnp.where(
                m == 1,
                COURANT / PERMITTIVITIES[1],
                jnp.where(m == 2, COURANT / PERMITTIVITIES[2], COURANT / PERMITTIVITIES[3]),
            ),
        )
        news = []
        for r, (e, h, en) in enumerate(runs):
            hx, hy, hz = h[0, x], h[1, x], h[2, x]
            hy_x, hz_x = (h[1, x - 1], h[2, x - 1]) if x else (xr[r, 0], xr[r, 1])
            hx_y = down_y(hx, yr[r, 0, x : x + 1, :])
            hz_y = down_y(hz, yr[r, 1, x : x + 1, :])
            hx_z = down_z(hx, packed, (r * 2 + 0) * nx + x)
            hy_z = down_z(hy, packed, (r * 2 + 1) * nx + x)
            ex = e[0, x] + coefficient * ((hz - hz_y) - (hy - hy_z))
            ey = e[1, x] + coefficient * ((hx - hx_z) - (hz - hz_x))
            ez = e[2, x] + coefficient * ((hy - hy_x) - (hx - hx_y))
            en[0, x] = ex
            en[1, x] = ey
            en[2, x] = ez
            news.append((ex, ey, ez))
        total = spec[0, x]
        for c in range(3):
            f, a = news[0][c], news[1][c]
            total = total + (f * (spec[1 + c, x] + both * a) + a * spec[4 + c, x])
        products.append(total)
        if len(products) == group:
            block = jnp.concatenate(products, axis=0)
            products = []
            sums = jnp.zeros((2 * owned, group * ny), jnp.float32)
            for _ in range(3):
                part = block.astype(jnp.bfloat16)
                block = block - part.astype(jnp.float32)
                sums = sums + lax.dot_general(hot, part, dims, preferred_element_type=jnp.float32)
            where = pl.ds((x + 1 - group) * ny, group * ny)
            own[:, where] = sums[:owned]
            other[:, where] = sums[owned:]


def electric(ef, ea, hf, ha, material, xr, yr, zr, spec, freq, layer_map, half, owned):
    _, nx, ny, nz = ef.shape
    field = vmem(3, nx, ny, nz)
    return call(
        functools.partial(electric_body, half, owned),
        "electric",
        (field, field, vmem(owned, nx * ny), vmem(owned, nx * ny)),
        (VMEM,) * 4,
        [VMEM] * 11,
        nbytes=6700000,
    )(ef, ea, hf, ha, material, xr, yr, zr, spec, freq, layer_map)


def gradient_body(own, came, layer_map, out):
    owned, nx, ny = out.shape
    slab = layer_map.shape[1]
    layer = lax.broadcasted_iota(jnp.int32, (owned, slab), 0) + lax.axis_index("gz") * owned
    same = jnp.where(jnp.broadcast_to(layer_map[...], (owned, slab)) == layer, 1.0, 0.0)
    thickness = jnp.sum(same, axis=1, keepdims=True)
    result = (own[...] + came[...]) / (3.0 * thickness)
    for x in range(nx):
        out[:, x, :] = result[:, x * ny : (x + 1) * ny]


def gradient(own, came, layer_map, nx, ny):
    return call(gradient_body, "gradient", f32(own.shape[0], nx, ny), VMEM, [VMEM, VMEM, VMEM])(own, came, layer_map)


def shards(ef, hf, ea, ha, material, df, da, angular_freq, layer_map):
    _, nx, ny, nz = ef.shape
    half = df.shape[3]
    owned = LAYERS // lax.axis_size("gz")
    freq = angular_freq.reshape(1, -1)
    layer_map = layer_map.reshape(1, -1)
    df = jnp.transpose(df, (0, 1, 2, 4, 5, 3))
    da = jnp.transpose(da, (0, 1, 2, 4, 5, 3))
    xs, ys, zs, ef, ea = first_faces(ef, ea)
    yr = ring(ys, "gy", -1)
    xr = ring(xs, "gx", -1)
    zr = line(zs, "gz", -1)
    hf, ha = load((hf, ha), zs)
    hf, ha, xs, ys, zs = magnetic(ef, ea, hf, ha, xr, yr, zr)
    yr = ring(ys, "gy", 1)
    xr = ring(xs, "gx", 1)
    zr = line(zs, "gz", 1)
    spec = spectra(df, da, freq, zs, nz)
    ef, ea, own, other = electric(ef, ea, hf, ha, material, xr, yr, zr, spec, freq, layer_map, half, owned)
    came = ring(other, "gz", 1)
    ef, hf, ea, ha = store((ef, hf, ea, ha), own)
    return ef, hf, ea, ha, gradient(own, came, layer_map, nx, ny)


def solution(mesh):
    field = P(None, "gx", "gy", "gz")
    dft = P(None, None, None, "gz", "gx", "gy")
    return jax.shard_map(
        shards,
        mesh=mesh,
        in_specs=(field, field, field, field, P("gx", "gy", "gz"), dft, dft, P(), P()),
        out_specs=(field, field, field, field, P("gz", "gx", "gy")),
        check_vma=False,
    )
```

```python
import functools

import jax
import jax.numpy as jnp
from jax import lax
from jax.experimental import pallas as pl
from jax.experimental.pallas import tpu as pltpu
from jax.sharding import PartitionSpec as P

LAYERS = 16
STEP = 40
PERMITTIVITIES = (1.0, 2.1, 4.0, 12.0)
COURANT = 0.5
LANES = 128
MIB = 1024 * 1024
ANY = pl.BlockSpec(memory_space=pl.ANY)
VMEM = pl.BlockSpec(memory_space=pltpu.VMEM)


def f32(*shape):
    return jax.ShapeDtypeStruct(shape, jnp.float32)


def vmem(*shape):
    return pltpu.VMEM(shape, jnp.float32)


def hbm(x):
    return pltpu.with_memory_space_constraint(x, pltpu.HBM)


def ring(x, axis, by):
    peers = lax.axis_size(axis)
    return lax.ppermute(x, axis, [(i, (i + by) % peers) for i in range(peers)])


def call(body, name, outs, out_specs, in_specs, scratch=(), nbytes=100000, limit=32):
    return pl.pallas_call(
        body,
        out_shape=outs,
        in_specs=in_specs,
        out_specs=out_specs,
        scratch_shapes=list(scratch),
        compiler_params=pltpu.CompilerParams(vmem_limit_bytes=limit * MIB),
        cost_estimate=pl.CostEstimate(flops=nbytes, bytes_accessed=nbytes, transcendentals=0),
        name=name,
    )


def lane_ids(rows):
    return lax.broadcasted_iota(jnp.int32, (rows, LANES), 1)


def row_ids(rows):
    return lax.broadcasted_iota(jnp.int32, (rows, LANES), 0)


def move(a, source, target):
    shift = (target - source) % LANES
    return pltpu.roll(a, shift, 1) if shift else a


def up_y(a, row):
    n = a.shape[0]
    return jnp.where(row_ids(n) == n - 1, jnp.broadcast_to(row, a.shape), pltpu.roll(a, n - 1, 0))


def down_y(a, row):
    return jnp.where(row_ids(a.shape[0]) == 0, jnp.broadcast_to(row, a.shape), pltpu.roll(a, 1, 0))


def up_z(a, packed, lane):
    n = a.shape[1]
    return jnp.where(lane_ids(a.shape[0]) == n - 1, move(packed, lane, n - 1), pltpu.roll(a, n - 1, 1))


def down_z(a, packed, lane):
    return jnp.where(lane_ids(a.shape[0]) == 0, move(packed, lane, 0), pltpu.roll(a, 1, 1))


def first_faces_body(ef, ea, xs, ys, zs, evf, eva, sems):
    fields = ((ef, evf), (ea, eva))
    _, nx, ny, _ = ef.shape
    copies = {}
    for c in range(3):
        for r, (e, v) in enumerate(fields):
            copies[c, r] = pltpu.make_async_copy(e.at[c], v.at[c], sems.at[r, c])
            copies[c, r].start()
    lane = lane_ids(ny)
    total = jnp.zeros((ny, LANES), jnp.float32)
    for c in range(3):
        for r, (_, v) in enumerate(fields):
            copies[c, r].wait()
            for x in range(nx):
                if c < 2:
                    to = (r * 2 + c) * nx + x
                    total = jnp.where(lane == to, move(v[c, x], 0, to), total)
                if c != 1:
                    ys[r, c // 2, x : x + 1, :] = v[c, x, 0:1, :]
            if c:
                xs[r, c - 1] = v[c, 0]
    zs[...] = total


def first_faces(ef, ea):
    _, nx, ny, nz = ef.shape
    field = vmem(3, nx, ny, nz)
    return call(
        first_faces_body,
        "first_faces",
        (vmem(2, 2, ny, nz), vmem(2, 2, nx, nz), vmem(ny, LANES), field, field),
        (VMEM,) * 5,
        [ANY, ANY],
        [pltpu.SemaphoreType.DMA((2, 3))],
        nbytes=1500000,
    )(hbm(ef), hbm(ea))


def transfer_body(n, *refs):
    sems = refs[-1]
    copies = []
    for k, (a, b) in enumerate(zip(refs[:n], refs[-1 - n : -1], strict=True)):
        for c in range(a.shape[0]):
            copies.append(pltpu.make_async_copy(a.at[c], b.at[c], sems.at[k, c]))
    for copy in copies:
        copy.start()
    for copy in copies:
        copy.wait()


def load(fields, after):
    n = len(fields)
    return call(
        functools.partial(transfer_body, n),
        "load",
        tuple(vmem(*f.shape) for f in fields),
        (VMEM,) * n,
        [ANY] * (n + 1),
        [pltpu.SemaphoreType.DMA((n, 3))],
        nbytes=1500000,
    )(*[hbm(f) for f in fields], after)


def store(fields, after):
    n = len(fields)
    return call(
        functools.partial(transfer_body, n),
        "store",
        tuple(f32(*f.shape) for f in fields),
        (ANY,) * n,
        [VMEM] * n + [ANY],
        [pltpu.SemaphoreType.DMA((n, 3))],
        nbytes=3000000,
    )(*fields, after)


def magnetic_update(e, h, x, rows, next_x, next_y, packed, r):
    nx = e.shape[1]
    ex, ey, ez = e[0, x, rows], e[1, x, rows], e[2, x, rows]
    ey_x, ez_x = (e[1, x + 1, rows], e[2, x + 1, rows]) if x + 1 < nx else (next_x[r, 0, rows], next_x[r, 1, rows])
    ex_y = up_y(ex, next_y[r, 0, x : x + 1, :])
    ez_y = up_y(ez, next_y[r, 1, x : x + 1, :])
    ex_z = up_z(ex, packed, (r * 2 + 0) * nx + x)
    ey_z = up_z(ey, packed, (r * 2 + 1) * nx + x)
    hx = h[0, x, rows] - COURANT * ((ez_y - ez) - (ey_z - ey))
    hy = h[1, x, rows] - COURANT * ((ex_z - ex) - (ez_x - ez))
    hz = h[2, x, rows] - COURANT * ((ey_x - ey) - (ex_y - ex))
    return hx, hy, hz


def within_upper_wall(zr):
    return jnp.where(lax.axis_index("gz") == lax.axis_size("gz") - 1, 0.0, zr)


def last_faces_body(ef, ea, hf, ha, xr, yr, zr, xs, ys):
    _, nx, ny, _ = ef.shape
    packed = within_upper_wall(zr[...])
    last = slice(ny - 8, ny)
    for r, (e, h) in enumerate(((ef, hf), (ea, ha))):
        for x in range(nx):
            hx, _, hz = magnetic_update(e, h, x, last, xr, yr, packed[last], r)
            ys[r, 0, x : x + 1, :] = hx[7:8, :]
            ys[r, 1, x : x + 1, :] = hz[7:8, :]
        _, xs[r, 0], xs[r, 1] = magnetic_update(e, h, nx - 1, slice(0, ny), xr, yr, packed, r)


def last_faces(ef, ea, hf, ha, xr, yr, zr):
    _, nx, ny, nz = ef.shape
    return call(
        last_faces_body,
        "last_faces",
        (vmem(2, 2, ny, nz), vmem(2, 2, nx, nz)),
        (VMEM,) * 2,
        [VMEM] * 7,
        nbytes=500000,
    )(ef, ea, hf, ha, xr, yr, zr)


def magnetic_body(ef, ea, hf, ha, xr, yr, zr, after, hfn, han, zs):
    runs = ((ef, hf, hfn), (ea, ha, han))
    _, nx, ny, nz = ef.shape
    packed = within_upper_wall(zr[...])
    for x in range(nx):
        for r, (e, h, hn) in enumerate(runs):
            hn[0, x], hn[1, x], hn[2, x] = magnetic_update(e, h, x, slice(0, ny), xr, yr, packed, r)
    lane = lane_ids(ny)
    total = jnp.zeros((ny, LANES), jnp.float32)
    for r, (_, _, hn) in enumerate(runs):
        for c in range(2):
            for x in range(nx):
                to = (r * 2 + c) * nx + x
                total = jnp.where(lane == to, move(hn[c, x], nz - 1, to), total)
    zs[...] = total


def magnetic(ef, ea, hf, ha, xr, yr, zr, after):
    _, nx, ny, nz = ef.shape
    field = vmem(3, nx, ny, nz)
    return call(
        magnetic_body,
        "magnetic",
        (field, field, vmem(ny, LANES)),
        (VMEM,) * 3,
        [VMEM] * 7 + [ANY],
        nbytes=4800000,
    )(ef, ea, hf, ha, xr, yr, zr, after)


def slab_start(nz, half):
    return (1 - lax.axis_index("gz")) * (nz - half)


def spectra_body(half, nz, chunk, df, dav, freq, after, out, dfv, sems):
    freqs, nx, ny = df.shape[0], df.shape[3], df.shape[4]
    copies = {}
    for i in range(nx // chunk):
        part = pl.ds(i * chunk, chunk)
        copies[i] = pltpu.make_async_copy(df.at[:, :, :, part], dfv.at[:, :, :, part], sems.at[i])
        copies[i].start()
    phase = freq[...] * float(STEP)
    cos, sin = jnp.cos(phase), jnp.sin(phase)
    cs = [jnp.broadcast_to(cos[:, f : f + 1], (ny, half)) for f in range(freqs)]
    sn = [jnp.broadcast_to(sin[:, f : f + 1], (ny, half)) for f in range(freqs)]
    shift = slab_start(nz, half)
    blank = jnp.zeros((ny, LANES - half), jnp.float32)

    def place(a):
        return pltpu.roll(jnp.concatenate([a, blank], axis=1), shift, 1)

    for x in range(nx):
        if x % chunk == 0:
            copies[x // chunk].wait()
        base = jnp.zeros((ny, half), jnp.float32)
        for c in range(3):
            with_forward = jnp.zeros((ny, half), jnp.float32)
            with_adjoint = jnp.zeros((ny, half), jnp.float32)
            for f in range(freqs):
                rf, jf, ra, ja = dfv[f, 0, c, x], dfv[f, 1, c, x], dav[f, 0, c, x], dav[f, 1, c, x]
                base = base + (rf * ra - jf * ja)
                with_forward = with_forward + (cs[f] * ra + sn[f] * ja)
                with_adjoint = with_adjoint + (cs[f] * rf + sn[f] * jf)
            out[1 + c, x] = place(with_forward)
            out[4 + c, x] = place(with_adjoint)
        out[0, x] = place(base)


def spectra(df, da, freq, after, nz):
    freqs, _, _, nx, ny, half = df.shape
    chunk = 2
    held = vmem(*df.shape)
    return call(
        functools.partial(spectra_body, half, nz, chunk),
        "spectra",
        vmem(7, nx, ny, LANES),
        VMEM,
        [ANY, VMEM, VMEM, ANY],
        [held, pltpu.SemaphoreType.DMA((nx // chunk,))],
        nbytes=11000000,
    )(hbm(df), da, freq, after)


def electric_body(half, owned, ef, ea, hf, ha, material, xr, yr, zr, spec, freq, layer_map, efn, ean, own, other):
    runs = ((ef, hf, efn), (ea, ha, ean))
    _, nx, ny, nz = ef.shape
    phase = freq[...] * float(STEP)
    cos, sin = jnp.cos(phase), jnp.sin(phase)
    both = jnp.sum(cos * cos - sin * sin, axis=1, keepdims=True)
    gz = lax.axis_index("gz")
    start = slab_start(nz, half)
    slab = layer_map.shape[1]
    cells = jnp.concatenate([layer_map[...], jnp.full((1, LANES - slab), -1, jnp.int32)], axis=1)
    cells = pltpu.roll(jnp.broadcast_to(cells, (8, LANES)), lax.rem(start + LANES - gz * half, LANES), 1)
    lane, layer = lane_ids(2 * owned), row_ids(2 * owned)
    inside = (lane >= start) & (lane < start + half)
    cells = jnp.broadcast_to(cells[0:1, :], (2 * owned, LANES))
    layer = lax.rem(layer + gz * owned, 2 * owned)
    hot = jnp.where(inside & (cells == layer), 1.0, 0.0).astype(jnp.bfloat16)
    owner = jnp.broadcast_to(layer_map[...], (2 * owned, slab)) == layer[:, :slab]
    share = 1.0 / (3.0 * jnp.sum(jnp.where(owner, 1.0, 0.0), axis=1, keepdims=True))
    packed = jnp.where(gz == 0, 0.0, zr[...])
    dims = (((1,), (1,)), ((), ()))
    group = LANES // ny
    products = []
    for x in range(nx):
        m = material[x]
        coefficient = jnp.where(
            m == 0,
            COURANT / PERMITTIVITIES[0],
            jnp.where(
                m == 1,
                COURANT / PERMITTIVITIES[1],
                jnp.where(m == 2, COURANT / PERMITTIVITIES[2], COURANT / PERMITTIVITIES[3]),
            ),
        )
        news = []
        for r, (e, h, en) in enumerate(runs):
            hx, hy, hz = h[0, x], h[1, x], h[2, x]
            hy_x, hz_x = (h[1, x - 1], h[2, x - 1]) if x else (xr[r, 0], xr[r, 1])
            hx_y = down_y(hx, yr[r, 0, x : x + 1, :])
            hz_y = down_y(hz, yr[r, 1, x : x + 1, :])
            hx_z = down_z(hx, packed, (r * 2 + 0) * nx + x)
            hy_z = down_z(hy, packed, (r * 2 + 1) * nx + x)
            ex = e[0, x] + coefficient * ((hz - hz_y) - (hy - hy_z))
            ey = e[1, x] + coefficient * ((hx - hx_z) - (hz - hz_x))
            ez = e[2, x] + coefficient * ((hy - hy_x) - (hx - hx_y))
            en[0, x] = ex
            en[1, x] = ey
            en[2, x] = ez
            news.append((ex, ey, ez))
        total = spec[0, x]
        for c in range(3):
            f, a = news[0][c], news[1][c]
            total = total + (f * (spec[1 + c, x] + both * a) + a * spec[4 + c, x])
        products.append(total)
        if len(products) == group:
            block = jnp.concatenate(products, axis=0)
            products = []
            sums = jnp.zeros((2 * owned, group * ny), jnp.float32)
            for _ in range(3):
                part = block.astype(jnp.bfloat16)
                block = block - part.astype(jnp.float32)
                sums = sums + lax.dot_general(hot, part, dims, preferred_element_type=jnp.float32)
            where = pl.ds((x + 1 - group) * ny, group * ny)
            sums = sums * share
            own[:, where] = sums[:owned]
            other[:, where] = sums[owned:]


def electric(ef, ea, hf, ha, material, xr, yr, zr, spec, freq, layer_map, half, owned):
    _, nx, ny, nz = ef.shape
    field = vmem(3, nx, ny, nz)
    return call(
        functools.partial(electric_body, half, owned),
        "electric",
        (field, field, vmem(owned, nx * ny), vmem(owned, nx * ny)),
        (VMEM,) * 4,
        [VMEM] * 11,
        nbytes=6700000,
    )(ef, ea, hf, ha, material, xr, yr, zr, spec, freq, layer_map)


def gradient_body(own, came, out):
    _, nx, ny = out.shape
    result = own[...] + came[...]
    for x in range(nx):
        out[:, x, :] = result[:, x * ny : (x + 1) * ny]


def gradient(own, came, nx, ny):
    return call(gradient_body, "gradient", f32(own.shape[0], nx, ny), VMEM, [VMEM, VMEM])(own, came)


def shards(ef, hf, ea, ha, material, df, da, angular_freq, layer_map):
    _, nx, ny, nz = ef.shape
    half = df.shape[3]
    owned = LAYERS // lax.axis_size("gz")
    freq = angular_freq.reshape(1, -1)
    layer_map = layer_map.reshape(1, -1)
    df = jnp.transpose(df, (0, 1, 2, 4, 5, 3))
    da = jnp.transpose(da, (0, 1, 2, 4, 5, 3))
    xs, ys, zs, ef, ea = first_faces(ef, ea)
    yr = ring(ys, "gy", -1)
    xr = ring(xs, "gx", -1)
    zr = ring(zs, "gz", -1)
    hf, ha = load((hf, ha), zs)
    xs, ys = last_faces(ef, ea, hf, ha, xr, yr, zr)
    hf, ha, zs = magnetic(ef, ea, hf, ha, xr, yr, zr, ys)
    yr = ring(ys, "gy", 1)
    xr = ring(xs, "gx", 1)
    zr = ring(zs, "gz", 1)
    spec = spectra(df, da, freq, zs, nz)
    ef, ea, own, other = electric(ef, ea, hf, ha, material, xr, yr, zr, spec, freq, layer_map, half, owned)
    came = ring(other, "gz", 1)
    ef, hf, ea, ha = store((ef, hf, ea, ha), own)
    return ef, hf, ea, ha, gradient(own, came, nx, ny)


def solution(mesh):
    field = P(None, "gx", "gy", "gz")
    dft = P(None, None, None, "gz", "gx", "gy")
    return jax.shard_map(
        shards,
        mesh=mesh,
        in_specs=(field, field, field, field, P("gx", "gy", "gz"), dft, dft, P(), P()),
        out_specs=(field, field, field, field, P("gz", "gx", "gy")),
        check_vma=False,
    )
```

```python
import functools

import jax
import jax.numpy as jnp
from jax import lax
from jax.experimental import pallas as pl
from jax.experimental.pallas import tpu as pltpu
from jax.sharding import PartitionSpec as P

LAYERS = 16
STEP = 40
PERMITTIVITIES = (1.0, 2.1, 4.0, 12.0)
COURANT = 0.5
LANES = 128
MIB = 1024 * 1024
ANY = pl.BlockSpec(memory_space=pl.ANY)
VMEM = pl.BlockSpec(memory_space=pltpu.VMEM)


def f32(*shape):
    return jax.ShapeDtypeStruct(shape, jnp.float32)


def vmem(*shape):
    return pltpu.VMEM(shape, jnp.float32)


def hbm(x):
    return pltpu.with_memory_space_constraint(x, pltpu.HBM)


def ring(x, axis, by):
    peers = lax.axis_size(axis)
    return lax.ppermute(x, axis, [(i, (i + by) % peers) for i in range(peers)])


def call(body, name, outs, out_specs, in_specs, scratch=(), nbytes=100000, limit=32):
    return pl.pallas_call(
        body,
        out_shape=outs,
        in_specs=in_specs,
        out_specs=out_specs,
        scratch_shapes=list(scratch),
        compiler_params=pltpu.CompilerParams(vmem_limit_bytes=limit * MIB),
        cost_estimate=pl.CostEstimate(flops=nbytes, bytes_accessed=nbytes, transcendentals=0),
        name=name,
    )


def lane_ids(rows):
    return lax.broadcasted_iota(jnp.int32, (rows, LANES), 1)


def row_ids(rows):
    return lax.broadcasted_iota(jnp.int32, (rows, LANES), 0)


def move(a, source, target):
    shift = (target - source) % LANES
    return pltpu.roll(a, shift, 1) if shift else a


def up_y(a, row):
    n = a.shape[0]
    return jnp.where(row_ids(n) == n - 1, jnp.broadcast_to(row, a.shape), pltpu.roll(a, n - 1, 0))


def down_y(a, row):
    return jnp.where(row_ids(a.shape[0]) == 0, jnp.broadcast_to(row, a.shape), pltpu.roll(a, 1, 0))


def up_z(a):
    n = a.shape[1]
    return jnp.where(lane_ids(a.shape[0]) == n - 1, 0.0, pltpu.roll(a, n - 1, 1))


def down_z(a, packed, lane):
    return jnp.where(lane_ids(a.shape[0]) == 0, move(packed, lane, 0), pltpu.roll(a, 1, 1))


def first_faces_body(ef, ea, xs, ys, evf, eva, sems):
    fields = ((ef, evf), (ea, eva))
    nx = ef.shape[1]
    copies = {}
    for c in range(3):
        for r, (e, v) in enumerate(fields):
            copies[c, r] = pltpu.make_async_copy(e.at[c], v.at[c], sems.at[r, c])
            copies[c, r].start()
    for c in range(3):
        for r, (_, v) in enumerate(fields):
            copies[c, r].wait()
            if c != 1:
                for x in range(nx):
                    ys[r, c // 2, x : x + 1, :] = v[c, x, 0:1, :]
            if c:
                xs[r, c - 1] = v[c, 0]


def first_faces(ef, ea):
    _, nx, ny, nz = ef.shape
    field = vmem(3, nx, ny, nz)
    return call(
        first_faces_body,
        "first_faces",
        (vmem(2, 2, ny, nz), vmem(2, 2, nx, nz), field, field),
        (VMEM,) * 4,
        [ANY, ANY],
        [pltpu.SemaphoreType.DMA((2, 3))],
        nbytes=1500000,
    )(hbm(ef), hbm(ea))


def load_body(hf, ha, ef, ea, after, hvf, hva, along_x, along_y, sems):
    _, nx, ny, _ = ef.shape
    copies = []
    for r, (h, v) in enumerate(((hf, hvf), (ha, hva))):
        for c in range(3):
            copies.append(pltpu.make_async_copy(h.at[c], v.at[c], sems.at[r, c]))
    for copy in copies:
        copy.start()
    lane, lane_8 = lane_ids(ny), lane_ids(8)
    by_x = jnp.zeros((ny, LANES), jnp.float32)
    by_y = jnp.zeros((8, LANES), jnp.float32)
    for r, e in enumerate((ef, ea)):
        by_x = jnp.where(lane == r * nx, move(e[0, nx - 1], 0, r * nx), by_x)
        for x in range(nx):
            by_y = jnp.where(lane_8 == r * nx + x, move(e[1, x, ny - 8 : ny, :], 0, r * nx + x), by_y)
    along_x[...] = by_x
    along_y[...] = jnp.where(row_ids(8) == 0, pltpu.roll(by_y, 1, 0), 0.0)
    for copy in copies:
        copy.wait()


def load(hf, ha, ef, ea, after):
    _, nx, ny, nz = ef.shape
    field = vmem(3, nx, ny, nz)
    return call(
        load_body,
        "load",
        (field, field, vmem(ny, LANES), vmem(8, LANES)),
        (VMEM,) * 4,
        [ANY, ANY, VMEM, VMEM, ANY],
        [pltpu.SemaphoreType.DMA((2, 3))],
        nbytes=1500000,
    )(hbm(hf), hbm(ha), ef, ea, after)


def magnetic_update(e, h, x, rows, next_x, next_y, r):
    nx = e.shape[1]
    ex, ey, ez = e[0, x, rows], e[1, x, rows], e[2, x, rows]
    ey_x, ez_x = (e[1, x + 1, rows], e[2, x + 1, rows]) if x + 1 < nx else (next_x[r, 0, rows], next_x[r, 1, rows])
    ex_y = up_y(ex, next_y[r, 0, x : x + 1, :])
    ez_y = up_y(ez, next_y[r, 1, x : x + 1, :])
    ex_z = up_z(ex)
    ey_z = up_z(ey)
    hx = h[0, x, rows] - COURANT * ((ez_y - ez) - (ey_z - ey))
    hy = h[1, x, rows] - COURANT * ((ex_z - ex) - (ez_x - ez))
    hz = h[2, x, rows] - COURANT * ((ey_x - ey) - (ex_y - ex))
    return hx, hy, hz


def last_faces_body(ef, ea, hf, ha, xr, yr, along_x, along_y, xs, ys):
    _, nx, ny, _ = ef.shape
    last = slice(ny - 8, ny)
    for r, (e, h) in enumerate(((ef, hf), (ea, ha))):
        for x in range(nx):
            hx, _, hz = magnetic_update(e, h, x, last, xr, yr, r)
            for c, a in enumerate((hx, hz)):
                at = packed_lane(r, c, x, nx)
                ys[at : at + 1, :] = a[7:8, :]
        _, xs[r * 2], xs[r * 2 + 1] = magnetic_update(e, h, nx - 1, slice(0, ny), xr, yr, r)
    xs[4] = along_x[...]
    ys[4 * nx : 4 * nx + 8, :] = along_y[...]


def last_faces(ef, ea, hf, ha, xr, yr, along_x, along_y):
    _, nx, ny, nz = ef.shape
    return call(
        last_faces_body,
        "last_faces",
        (vmem(5, ny, nz), vmem(4 * nx + 8, nz)),
        (VMEM,) * 2,
        [VMEM] * 8,
        nbytes=500000,
    )(ef, ea, hf, ha, xr, yr, along_x, along_y)


def magnetic_body(ef, ea, hf, ha, xr, yr, after, hfn, han, layer, zs):
    _, nx, ny, nz = ef.shape
    for x in range(nx):
        for r, (e, h, hn) in enumerate(((ef, hf, hfn), (ea, ha, han))):
            hn[0, x], hn[1, x], hn[2, x] = magnetic_update(e, h, x, slice(0, ny), xr, yr, r)
    first = pack_layer((ef, ea), nx, ny, 0)
    layer[...] = first
    zs[...] = jnp.where(lax.axis_index("gz") == 0, pack_layer((hfn, han), nx, ny, nz - 1), first)


def magnetic(ef, ea, hf, ha, xr, yr, after):
    _, nx, ny, nz = ef.shape
    field = vmem(3, nx, ny, nz)
    return call(
        magnetic_body,
        "magnetic",
        (field, field, vmem(ny, LANES), vmem(ny, LANES)),
        (VMEM,) * 4,
        [VMEM] * 6 + [ANY],
        nbytes=4800000,
    )(ef, ea, hf, ha, xr, yr, after)


def packed_lane(r, c, x, nx):
    return (r * 2 + c) * nx + x


def pack_layer(fields, nx, ny, z):
    lane = lane_ids(ny)
    total = jnp.zeros((ny, LANES), jnp.float32)
    for r, f in enumerate(fields):
        for c in range(2):
            for x in range(nx):
                to = packed_lane(r, c, x, nx)
                total = jnp.where(lane == to, move(f[c, x], z, to), total)
    return total


def from_layer_above(tile, nx):
    first = lax.rem(lane_ids(tile.shape[0]) // nx, 2) == 0
    return COURANT * jnp.where(first, pltpu.roll(tile, LANES - nx, 1), -pltpu.roll(tile, nx, 1))


def pack_open(planes, z):
    ny = planes[0].shape[0]
    lane_8 = lane_ids(8)
    first = jnp.where(lane_ids(ny) == 0, move(planes[0], z, 0), 0.0)
    top = first[0:8, :]
    for x in range(1, len(planes)):
        top = jnp.where(lane_8 == x, move(planes[x], z, x), top)
    return jnp.concatenate([top, first[8:, :]], axis=0)


def update_coefficient(m):
    return jnp.where(
        m == 0,
        COURANT / PERMITTIVITIES[0],
        jnp.where(
            m == 1,
            COURANT / PERMITTIVITIES[1],
            jnp.where(m == 2, COURANT / PERMITTIVITIES[2], COURANT / PERMITTIVITIES[3]),
        ),
    )


def slab_start(nz, half):
    return (1 - lax.axis_index("gz")) * (nz - half)


def spectra_body(half, nz, chunk, df, dav, freq, material, after, out, still, dfv, sems):
    freqs, nx, ny = df.shape[0], df.shape[3], df.shape[4]
    copies = {}
    for i in range(nx // chunk):
        part = pl.ds(i * chunk, chunk)
        copies[i] = pltpu.make_async_copy(df.at[:, :, :, part], dfv.at[:, :, :, part], sems.at[i])
        copies[i].start()
    phase = freq[...] * float(STEP)
    cos, sin = jnp.cos(phase), jnp.sin(phase)
    cs = [jnp.broadcast_to(cos[:, f : f + 1], (ny, half)) for f in range(freqs)]
    sn = [jnp.broadcast_to(sin[:, f : f + 1], (ny, half)) for f in range(freqs)]
    shift = slab_start(nz, half)
    blank = jnp.zeros((ny, LANES - half), jnp.float32)

    def place(a):
        return pltpu.roll(jnp.concatenate([a, blank], axis=1), shift, 1)

    for x in range(nx):
        if x % chunk == 0:
            copies[x // chunk].wait()
        base = jnp.zeros((ny, half), jnp.float32)
        for c in range(3):
            with_forward = jnp.zeros((ny, half), jnp.float32)
            with_adjoint = jnp.zeros((ny, half), jnp.float32)
            for f in range(freqs):
                rf, jf, ra, ja = dfv[f, 0, c, x], dfv[f, 1, c, x], dav[f, 0, c, x], dav[f, 1, c, x]
                base = base + (rf * ra - jf * ja)
                with_forward = with_forward + (cs[f] * ra + sn[f] * ja)
                with_adjoint = with_adjoint + (cs[f] * rf + sn[f] * jf)
            out[1 + c, x] = place(with_forward)
            out[4 + c, x] = place(with_adjoint)
        out[0, x] = place(base)

    def cells(planes):
        return pack_open([planes(x, slice(0, 8 if x else ny)) for x in range(nx)], nz - 1)

    still[0] = cells(lambda x, rows: out[3, x, rows])
    still[1] = cells(lambda x, rows: out[6, x, rows])
    still[2] = cells(lambda x, rows: update_coefficient(material[x, rows]))


def spectra(df, da, freq, material, after, nz):
    freqs, _, _, nx, ny, half = df.shape
    chunk = 2
    held = vmem(*df.shape)
    return call(
        functools.partial(spectra_body, half, nz, chunk),
        "spectra",
        (vmem(7, nx, ny, LANES), vmem(3, ny, LANES)),
        (VMEM,) * 2,
        [ANY, VMEM, VMEM, VMEM, ANY],
        [held, pltpu.SemaphoreType.DMA((nx // chunk,))],
        nbytes=11000000,
    )(hbm(df), da, freq, material, after)


def complete_body(hf, ha, zr, layer, hfn, han, below):
    _, nx, ny, nz = hf.shape
    lower = lax.axis_index("gz") == 0
    came = zr[...]
    above = jnp.where(lower, from_layer_above(came, nx), 0.0)
    below[...] = jnp.where(lower, 0.0, came + from_layer_above(layer[...], nx))
    top = lane_ids(ny) == nz - 1
    for r, (h, hn) in enumerate(((hf, hfn), (ha, han))):
        for c in range(2):
            for x in range(nx):
                hn[c, x] = h[c, x] + jnp.where(top, move(above, packed_lane(r, c, x, nx), nz - 1), 0.0)


def complete(hf, ha, zr, layer):
    _, nx, ny, nz = hf.shape
    part = vmem(2, nx, ny, nz)
    return call(
        complete_body,
        "complete",
        (part, part, vmem(ny, LANES)),
        (VMEM,) * 3,
        [VMEM] * 4,
        nbytes=2000000,
    )(hf, ha, zr, layer)


def electric_body(
    half, owned, ef, ea, hf, ha, hzf, hza, material, xr, yr, zr, spec, still, freq, layer_map, efn, ean, own, other, tile
):
    runs = ((ef, hf, hzf, efn), (ea, ha, hza, ean))
    _, nx, ny, nz = ef.shape
    phase = freq[...] * float(STEP)
    cos, sin = jnp.cos(phase), jnp.sin(phase)
    both = jnp.sum(cos * cos - sin * sin, axis=1, keepdims=True)
    gz = lax.axis_index("gz")
    lower = gz == 0
    start = slab_start(nz, half)
    slab = layer_map.shape[1]
    cells = jnp.concatenate([layer_map[...], jnp.full((1, LANES - slab), -1, jnp.int32)], axis=1)
    cells = pltpu.roll(jnp.broadcast_to(cells, (8, LANES)), lax.rem(start + LANES - gz * half, LANES), 1)
    lane, row = lane_ids(2 * owned), row_ids(2 * owned)
    inside = (lane >= start) & (lane < start + half)
    cells = jnp.broadcast_to(cells[0:1, :], (2 * owned, LANES))
    ids = lax.rem(row + gz * owned, 2 * owned)
    hot = jnp.where(inside & (cells == ids), 1.0, 0.0).astype(jnp.bfloat16)
    owner = jnp.broadcast_to(layer_map[...], (2 * owned, slab)) == ids[:, :slab]
    share = 1.0 / (3.0 * jnp.sum(jnp.where(owner, 1.0, 0.0), axis=1, keepdims=True))
    middle = jnp.broadcast_to(layer_map[0:1, half - 1 : half], (2 * owned, 1)) == ids[:, 0:1]
    middle_share = jnp.sum(jnp.where(middle, share, 0.0), axis=0, keepdims=True)
    below = zr[...]
    dims = (((1,), (1,)), ((), ()))
    group = LANES // ny
    products = []
    for x in range(nx):
        coefficient = update_coefficient(material[x])
        news = []
        for r, (e, h, hz, en) in enumerate(runs):
            at_x, at_y = packed_lane(r, 0, x, nx), packed_lane(r, 1, x, nx)
            hx, hy, hz_here = h[0, x], h[1, x], hz[2, x]
            hy_x, hz_x = (h[1, x - 1], hz[2, x - 1]) if x else (xr[2 * r], xr[2 * r + 1])
            hx_y = down_y(hx, yr[at_x : at_x + 1, :])
            hz_y = down_y(hz_here, yr[at_y : at_y + 1, :])
            hx_z = down_z(hx, below, at_x)
            hy_z = down_z(hy, below, at_y)
            ex = e[0, x] + coefficient * ((hz_here - hz_y) - (hy - hy_z))
            ey = e[1, x] + coefficient * ((hx - hx_z) - (hz_here - hz_x))
            ez = e[2, x] + coefficient * ((hy - hy_x) - (hx - hx_y))
            en[0, x] = ex
            en[1, x] = ey
            en[2, x] = ez
            news.append((ex, ey, ez))
        total = spec[0, x]
        for c in range(3):
            f, a = news[0][c], news[1][c]
            total = total + (f * (spec[1 + c, x] + both * a) + a * spec[4 + c, x])
        products.append(total)
        if len(products) == group:
            block = jnp.concatenate(products, axis=0)
            products = []
            sums = jnp.zeros((2 * owned, group * ny), jnp.float32)
            for _ in range(3):
                part = block.astype(jnp.bfloat16)
                block = block - part.astype(jnp.float32)
                sums = sums + lax.dot_general(hot, part, dims, preferred_element_type=jnp.float32)
            sums = sums * share
            where = pl.ds(x // group * owned, owned)
            own[where, :] = sums[:owned]
            other[where, :] = sums[owned:]
    f, a = (pack_open([e[2, x, 0 : 8 if x else ny, :] for x in range(nx)], nz - 1) for e in (efn, ean))
    ratio = COURANT * still[2]
    scaled = ratio * middle_share
    rest = scaled * (still[0] + both * a)
    rest = rest + pltpu.roll(scaled * (still[1] + both * f), nx, 1)
    rest = rest + pltpu.roll(scaled * ratio * both, 2 * nx, 1)
    rest = rest + pltpu.roll(ratio, 3 * nx, 1)
    along = xr[4]
    along = along + jnp.concatenate([yr[4 * nx : 4 * nx + 8, :], jnp.zeros((ny - 8, LANES), jnp.float32)], axis=0)
    rest = jnp.where(lower, rest, along)
    tile[...] = rest
    other[nx // group * owned :, :] = rest


def electric(ef, ea, hf, ha, hzf, hza, material, xr, yr, zr, spec, still, freq, layer_map, half, owned):
    _, nx, ny, nz = ef.shape
    field = vmem(3, nx, ny, nz)
    rows = nx * ny // LANES * owned
    return call(
        functools.partial(electric_body, half, owned),
        "electric",
        (field, field, vmem(rows, LANES), vmem(rows + ny, LANES), vmem(ny, LANES)),
        (VMEM,) * 5,
        [VMEM] * 14,
        nbytes=6700000,
    )(ef, ea, hf, ha, hzf, hza, material, xr, yr, zr, spec, still, freq, layer_map)


def store_body(ef, ea, hf, ha, hzf, hza, after, efn, ean, hfn, han, sems):
    copies = []
    for r, (e, h, hz, en, hn) in enumerate(((ef, hf, hzf, efn, hfn), (ea, ha, hza, ean, han))):
        for c in range(3):
            copies.append(pltpu.make_async_copy(e.at[c], en.at[c], sems.at[r, c]))
            copies.append(pltpu.make_async_copy((h if c < 2 else hz).at[c], hn.at[c], sems.at[r, 3 + c]))
    for copy in copies:
        copy.start()
    for copy in copies:
        copy.wait()


def store(ef, ea, hf, ha, hzf, hza, after):
    field = f32(*ef.shape)
    return call(
        store_body,
        "store",
        (field,) * 4,
        (ANY,) * 4,
        [VMEM] * 6 + [ANY],
        [pltpu.SemaphoreType.DMA((2, 6))],
        nbytes=3000000,
    )(ef, ea, hf, ha, hzf, hza, after)


def gradient_body(ef, ea, own, tile, came, layer_map, _f, _a, out, efn, ean, plane, rows, result, sems):
    owned, nx, ny = out.shape
    nz = ef.shape[3]
    half = layer_map.shape[1] // 2
    gz = lax.axis_index("gz")
    lower = gz == 0
    sums = own.shape[0]
    mine, theirs = tile[...], came[sums:, :]
    change, cells = jnp.where(lower, mine, theirs), jnp.where(lower, theirs, mine)
    cell = [cells, pltpu.roll(cells, LANES - nx, 1)]
    ratio = jnp.where(lower, pltpu.roll(change, LANES - 3 * nx, 1), 0.0)
    copies = []
    for r, (e, en) in enumerate(((ef, efn), (ea, ean))):
        add = ratio * cell[r]
        plane[r] = e[2, 0] + jnp.where(lane_ids(ny) == nz - 1, move(add, 0, nz - 1), 0.0)
        corner = (lane_ids(8) == nz - 1) & (row_ids(8) == 0)
        for x in range(1, nx):
            rows[r, x - 1] = e[2, x, 0:8, :] + jnp.where(corner, move(add[0:8, :], x, nz - 1), 0.0)
        copies.append(pltpu.make_async_copy(plane.at[r], en.at[2, 0], sems.at[r, 0]))
        copies.append(pltpu.make_async_copy(rows.at[r], en.at[2, 1:nx, 0:8], sems.at[r, 1]))
    for copy in copies:
        copy.start()
    by_a, by_both = pltpu.roll(change, LANES - nx, 1), pltpu.roll(change, LANES - 2 * nx, 1)
    missing = change * cell[0] + by_a * cell[1] + by_both * (cell[0] * cell[1])
    missing = jnp.transpose(missing)[0:nx, 0:ny]
    share = own[...] + came[0:sums, :]
    group = nx * owned // sums
    for x in range(nx):
        block = share[x // group * owned : (x // group + 1) * owned]
        at = x % group * ny
        result[:, x, :] = block[:, at : at + ny]
    middle = layer_map[0:1, half - 1 : half]
    for k in range(owned):
        mine = jnp.broadcast_to(middle == gz * owned + k, (nx, ny))
        result[k] = result[k] + jnp.where(mine, missing, 0.0)
    last = pltpu.make_async_copy(result, out, sems.at[0, 2])
    last.start()
    for copy in copies:
        copy.wait()
    last.wait()


def gradient(ef, ea, own, tile, came, layer_map, efn, ean, owned):
    _, nx, ny, nz = ef.shape
    return pl.pallas_call(
        gradient_body,
        out_shape=(f32(owned, nx, ny), f32(*efn.shape), f32(*ean.shape)),
        in_specs=[VMEM] * 6 + [ANY] * 2,
        out_specs=(ANY,) * 3,
        scratch_shapes=[
            pltpu.VMEM((2, ny, nz), jnp.float32),
            pltpu.VMEM((2, nx - 1, 8, nz), jnp.float32),
            pltpu.VMEM((owned, nx, ny), jnp.float32),
            pltpu.SemaphoreType.DMA((2, 3)),
        ],
        input_output_aliases={6: 1, 7: 2},
        compiler_params=pltpu.CompilerParams(vmem_limit_bytes=32 * MIB),
        cost_estimate=pl.CostEstimate(flops=100000, bytes_accessed=400000, transcendentals=0),
        name="gradient",
    )(ef, ea, own, tile, came, layer_map, efn, ean)


def shards(ef, hf, ea, ha, material, df, da, angular_freq, layer_map):
    _, nx, ny, nz = ef.shape
    half = df.shape[3]
    owned = LAYERS // lax.axis_size("gz")
    freq = angular_freq.reshape(1, -1)
    layer_map = layer_map.reshape(1, -1)
    df = jnp.transpose(df, (0, 1, 2, 4, 5, 3))
    da = jnp.transpose(da, (0, 1, 2, 4, 5, 3))
    xs, ys, ef, ea = first_faces(ef, ea)
    yr = ring(ys, "gy", -1)
    xr = ring(xs, "gx", -1)
    hf, ha, along_x, along_y = load(hf, ha, ef, ea, ys)
    xs, ys = last_faces(ef, ea, hf, ha, xr, yr, along_x, along_y)
    hf, ha, layer, zs = magnetic(ef, ea, hf, ha, xr, yr, ys)
    yr = ring(ys, "gy", 1)
    xr = ring(xs, "gx", 1)
    zr = ring(zs, "gz", 1)
    spec, still = spectra(df, da, freq, material, zs, nz)
    hxyf, hxya, below = complete(hf, ha, zr, layer)
    ef, ea, own, other, tile = electric(
        ef, ea, hxyf, hxya, hf, ha, material, xr, yr, below, spec, still, freq, layer_map, half, owned
    )
    came = ring(other, "gz", 1)
    efn, ean, hfn, han = store(ef, ea, hxyf, hxya, hf, ha, own)
    out, efn, ean = gradient(ef, ea, own, tile, came, layer_map, efn, ean, owned)
    return efn, hfn, ean, han, out


def solution(mesh):
    field = P(None, "gx", "gy", "gz")
    dft = P(None, None, None, "gz", "gx", "gy")
    return jax.shard_map(
        shards,
        mesh=mesh,
        in_specs=(field, field, field, field, P("gx", "gy", "gz"), dft, dft, P(), P()),
        out_specs=(field, field, field, field, P("gz", "gx", "gy")),
        check_vma=False,
    )
```

```python
import functools

import jax
import jax.numpy as jnp
from jax import lax
from jax.experimental import pallas as pl
from jax.experimental.pallas import tpu as pltpu
from jax.sharding import PartitionSpec as P

LAYERS = 16
STEP = 40
PERMITTIVITIES = (1.0, 2.1, 4.0, 12.0)
COURANT = 0.5
LANES = 128
MIB = 1024 * 1024
ANY = pl.BlockSpec(memory_space=pl.ANY)
VMEM = pl.BlockSpec(memory_space=pltpu.VMEM)


def f32(*shape):
    return jax.ShapeDtypeStruct(shape, jnp.float32)


def vmem(*shape):
    return pltpu.VMEM(shape, jnp.float32)


def hbm(x):
    return pltpu.with_memory_space_constraint(x, pltpu.HBM)


def ring(x, axis, by):
    peers = lax.axis_size(axis)
    return lax.ppermute(x, axis, [(i, (i + by) % peers) for i in range(peers)])


def call(body, name, outs, out_specs, in_specs, scratch=(), nbytes=100000, limit=32):
    return pl.pallas_call(
        body,
        out_shape=outs,
        in_specs=in_specs,
        out_specs=out_specs,
        scratch_shapes=list(scratch),
        compiler_params=pltpu.CompilerParams(vmem_limit_bytes=limit * MIB),
        cost_estimate=pl.CostEstimate(flops=nbytes, bytes_accessed=nbytes, transcendentals=0),
        name=name,
    )


def lane_ids(rows):
    return lax.broadcasted_iota(jnp.int32, (rows, LANES), 1)


def row_ids(rows):
    return lax.broadcasted_iota(jnp.int32, (rows, LANES), 0)


def move(a, source, target):
    shift = (target - source) % LANES
    return pltpu.roll(a, shift, 1) if shift else a


def up_y(a, row):
    n = a.shape[0]
    return jnp.where(row_ids(n) == n - 1, jnp.broadcast_to(row, a.shape), pltpu.roll(a, n - 1, 0))


def down_y(a, row):
    return jnp.where(row_ids(a.shape[0]) == 0, jnp.broadcast_to(row, a.shape), pltpu.roll(a, 1, 0))


def up_z(a):
    n = a.shape[1]
    return jnp.where(lane_ids(a.shape[0]) == n - 1, 0.0, pltpu.roll(a, n - 1, 1))


def down_z(a, packed, lane):
    return jnp.where(lane_ids(a.shape[0]) == 0, move(packed, lane, 0), pltpu.roll(a, 1, 1))


def first_faces_body(ef, ea, hf, ha, xs, ys, evf, eva, hvf, hva, along_x, along_y, sems):
    fields = (evf, eva)
    _, nx, ny, _ = ef.shape
    copies = {}
    for k, (pair, held) in enumerate((((ef, ea), (evf, eva)), ((hf, ha), (hvf, hva)))):
        for c in range(3):
            for r in range(2):
                copies[k, c, r] = pltpu.make_async_copy(pair[r].at[c], held[r].at[c], sems.at[k, r, c])
                copies[k, c, r].start()
    for c in range(3):
        for r, v in enumerate(fields):
            copies[0, c, r].wait()
            if c != 1:
                for x in range(nx):
                    ys[r, c // 2, x : x + 1, :] = v[c, x, 0:1, :]
            if c:
                xs[r, c - 1] = v[c, 0]
    lane, lane_8 = lane_ids(ny), lane_ids(8)
    by_x = jnp.zeros((ny, LANES), jnp.float32)
    by_y = jnp.zeros((8, LANES), jnp.float32)
    for r, e in enumerate(fields):
        by_x = jnp.where(lane == r * nx, move(e[0, nx - 1], 0, r * nx), by_x)
        for x in range(nx):
            by_y = jnp.where(lane_8 == r * nx + x, move(e[1, x, ny - 8 : ny, :], 0, r * nx + x), by_y)
    along_x[...] = by_x
    along_y[...] = jnp.where(row_ids(8) == 0, pltpu.roll(by_y, 1, 0), 0.0)
    for c in range(3):
        for r in range(2):
            copies[1, c, r].wait()


def first_faces(ef, ea, hf, ha):
    _, nx, ny, nz = ef.shape
    field = vmem(3, nx, ny, nz)
    return call(
        first_faces_body,
        "first_faces",
        (vmem(2, 2, ny, nz), vmem(2, 2, nx, nz)) + (field,) * 4 + (vmem(ny, LANES), vmem(8, LANES)),
        (VMEM,) * 8,
        [ANY] * 4,
        [pltpu.SemaphoreType.DMA((2, 2, 3))],
        nbytes=3000000,
    )(hbm(ef), hbm(ea), hbm(hf), hbm(ha))


def magnetic_update(e, h, x, rows, next_x, next_y, r):
    nx = e.shape[1]
    ex, ey, ez = e[0, x, rows], e[1, x, rows], e[2, x, rows]
    ey_x, ez_x = (e[1, x + 1, rows], e[2, x + 1, rows]) if x + 1 < nx else (next_x[r, 0, rows], next_x[r, 1, rows])
    ex_y = up_y(ex, 0.0 if next_y is None else next_y[r, 0, x : x + 1, :])
    ez_y = up_y(ez, 0.0 if next_y is None else next_y[r, 1, x : x + 1, :])
    ex_z = up_z(ex)
    ey_z = up_z(ey)
    hx = h[0, x, rows] - COURANT * ((ez_y - ez) - (ey_z - ey))
    hy = h[1, x, rows] - COURANT * ((ex_z - ex) - (ez_x - ez))
    hz = h[2, x, rows] - COURANT * ((ey_x - ey) - (ex_y - ex))
    return hx, hy, hz


def last_y_body(ef, ea, hf, ha, xr, along_y, ys):
    _, nx, ny, _ = ef.shape
    last = slice(ny - 8, ny)
    for r, (e, h) in enumerate(((ef, hf), (ea, ha))):
        for x in range(nx):
            hx, _, hz = magnetic_update(e, h, x, last, xr, None, r)
            for c, a in enumerate((hx, hz)):
                at = packed_lane(r, c, x, nx)
                ys[at : at + 1, :] = a[7:8, :]
    ys[4 * nx : 4 * nx + 8, :] = along_y[...]


def last_y(ef, ea, hf, ha, xr, along_y):
    _, nx, ny, nz = ef.shape
    return call(
        last_y_body,
        "last_y",
        vmem(4 * nx + 112, nz),
        VMEM,
        [VMEM] * 6,
        nbytes=500000,
    )(ef, ea, hf, ha, xr, along_y)


def last_x_body(ef, ea, hf, ha, xr, yr, along_x, after, xs):
    _, nx, ny, _ = ef.shape
    for r, (e, h) in enumerate(((ef, hf), (ea, ha))):
        _, xs[r * 2], xs[r * 2 + 1] = magnetic_update(e, h, nx - 1, slice(0, ny), xr, yr, r)
    xs[4] = along_x[...]


def last_x(ef, ea, hf, ha, xr, yr, along_x, after):
    _, nx, ny, nz = ef.shape
    return call(
        last_x_body,
        "last_x",
        vmem(5, ny, nz),
        VMEM,
        [VMEM] * 7 + [ANY],
        nbytes=500000,
    )(ef, ea, hf, ha, xr, yr, along_x, after)


def magnetic_body(ef, ea, hf, ha, xr, yr, after, hfn, han, layer, zs):
    _, nx, ny, nz = ef.shape
    for x in range(nx):
        for r, (e, h, hn) in enumerate(((ef, hf, hfn), (ea, ha, han))):
            hn[0, x], hn[1, x], hn[2, x] = magnetic_update(e, h, x, slice(0, ny), xr, yr, r)
    first = pack_layer((ef, ea), nx, ny, 0)
    layer[...] = first
    zs[...] = jnp.where(lax.axis_index("gz") == 0, pack_layer((hfn, han), nx, ny, nz - 1), first)


def magnetic(ef, ea, hf, ha, xr, yr, after):
    _, nx, ny, nz = ef.shape
    field = vmem(3, nx, ny, nz)
    return call(
        magnetic_body,
        "magnetic",
        (field, field, vmem(ny, LANES), vmem(ny, LANES)),
        (VMEM,) * 4,
        [VMEM] * 6 + [ANY],
        nbytes=4800000,
    )(ef, ea, hf, ha, xr, yr, after)


def packed_lane(r, c, x, nx):
    return (r * 2 + c) * nx + x


def pack_layer(fields, nx, ny, z):
    lane = lane_ids(ny)
    total = jnp.zeros((ny, LANES), jnp.float32)
    for r, f in enumerate(fields):
        for c in range(2):
            for x in range(nx):
                to = packed_lane(r, c, x, nx)
                total = jnp.where(lane == to, move(f[c, x], z, to), total)
    return total


def from_layer_above(tile, nx):
    first = lax.rem(lane_ids(tile.shape[0]) // nx, 2) == 0
    return COURANT * jnp.where(first, pltpu.roll(tile, LANES - nx, 1), -pltpu.roll(tile, nx, 1))


def pack_open(planes, z):
    ny = planes[0].shape[0]
    lane_8 = lane_ids(8)
    first = jnp.where(lane_ids(ny) == 0, move(planes[0], z, 0), 0.0)
    top = first[0:8, :]
    for x in range(1, len(planes)):
        top = jnp.where(lane_8 == x, move(planes[x], z, x), top)
    return jnp.concatenate([top, first[8:, :]], axis=0)


def update_coefficient(m):
    return jnp.where(
        m == 0,
        COURANT / PERMITTIVITIES[0],
        jnp.where(
            m == 1,
            COURANT / PERMITTIVITIES[1],
            jnp.where(m == 2, COURANT / PERMITTIVITIES[2], COURANT / PERMITTIVITIES[3]),
        ),
    )


def slab_start(nz, half):
    return (1 - lax.axis_index("gz")) * (nz - half)


def spectra_body(half, nz, dfv, dav, freq, material, after, out, still):
    freqs, nx, ny = dfv.shape[0], dfv.shape[3], dfv.shape[4]
    phase = freq[...] * float(STEP)
    cos, sin = jnp.cos(phase), jnp.sin(phase)
    cs = [jnp.broadcast_to(cos[:, f : f + 1], (ny, half)) for f in range(freqs)]
    sn = [jnp.broadcast_to(sin[:, f : f + 1], (ny, half)) for f in range(freqs)]
    shift = slab_start(nz, half)
    blank = jnp.zeros((ny, LANES - half), jnp.float32)

    def place(a):
        return pltpu.roll(jnp.concatenate([a, blank], axis=1), shift, 1)

    for x in range(nx):
        base = jnp.zeros((ny, half), jnp.float32)
        for c in range(3):
            with_forward = jnp.zeros((ny, half), jnp.float32)
            with_adjoint = jnp.zeros((ny, half), jnp.float32)
            for f in range(freqs):
                rf, jf, ra, ja = dfv[f, 0, c, x], dfv[f, 1, c, x], dav[f, 0, c, x], dav[f, 1, c, x]
                base = base + (rf * ra - jf * ja)
                with_forward = with_forward + (cs[f] * ra + sn[f] * ja)
                with_adjoint = with_adjoint + (cs[f] * rf + sn[f] * jf)
            out[1 + c, x] = place(with_forward)
            out[4 + c, x] = place(with_adjoint)
        out[0, x] = place(base)

    def cells(planes):
        return pack_open([planes(x, slice(0, 8 if x else ny)) for x in range(nx)], nz - 1)

    still[0] = cells(lambda x, rows: out[3, x, rows])
    still[1] = cells(lambda x, rows: out[6, x, rows])
    still[2] = cells(lambda x, rows: update_coefficient(material[x, rows]))


def spectra(df, da, freq, material, after, nz):
    _, _, _, nx, ny, half = df.shape
    return call(
        functools.partial(spectra_body, half, nz),
        "spectra",
        (vmem(7, nx, ny, LANES), vmem(3, ny, LANES)),
        (VMEM,) * 2,
        [VMEM] * 4 + [ANY],
        nbytes=11000000,
    )(df, da, freq, material, after)


def complete_body(hf, ha, zr, layer, hfn, han, below):
    _, nx, ny, nz = hf.shape
    lower = lax.axis_index("gz") == 0
    came = zr[...]
    above = jnp.where(lower, from_layer_above(came, nx), 0.0)
    below[...] = jnp.where(lower, 0.0, came + from_layer_above(layer[...], nx))
    top = lane_ids(ny) == nz - 1
    for r, (h, hn) in enumerate(((hf, hfn), (ha, han))):
        for c in range(2):
            for x in range(nx):
                hn[c, x] = h[c, x] + jnp.where(top, move(above, packed_lane(r, c, x, nx), nz - 1), 0.0)


def complete(hf, ha, zr, layer):
    _, nx, ny, nz = hf.shape
    part = vmem(2, nx, ny, nz)
    return call(
        complete_body,
        "complete",
        (part, part, vmem(ny, LANES)),
        (VMEM,) * 3,
        [VMEM] * 4,
        nbytes=2000000,
    )(hf, ha, zr, layer)


def electric_body(
    half, owned, ef, ea, hf, ha, hzf, hza, material, xr, yr, zr, first_y, spec, still, freq, layer_map, efn, ean, own, other, tile
):
    runs = ((ef, hf, hzf, efn), (ea, ha, hza, ean))
    _, nx, ny, nz = ef.shape
    phase = freq[...] * float(STEP)
    cos, sin = jnp.cos(phase), jnp.sin(phase)
    both = jnp.sum(cos * cos - sin * sin, axis=1, keepdims=True)
    gz = lax.axis_index("gz")
    lower = gz == 0
    start = slab_start(nz, half)
    slab = layer_map.shape[1]
    cells = jnp.concatenate([layer_map[...], jnp.full((1, LANES - slab), -1, jnp.int32)], axis=1)
    cells = pltpu.roll(jnp.broadcast_to(cells, (8, LANES)), lax.rem(start + LANES - gz * half, LANES), 1)
    lane, row = lane_ids(2 * owned), row_ids(2 * owned)
    inside = (lane >= start) & (lane < start + half)
    cells = jnp.broadcast_to(cells[0:1, :], (2 * owned, LANES))
    ids = lax.rem(row + gz * owned, 2 * owned)
    hot = jnp.where(inside & (cells == ids), 1.0, 0.0).astype(jnp.bfloat16)
    owner = jnp.broadcast_to(layer_map[...], (2 * owned, slab)) == ids[:, :slab]
    share = 1.0 / (3.0 * jnp.sum(jnp.where(owner, 1.0, 0.0), axis=1, keepdims=True))
    middle = jnp.broadcast_to(layer_map[0:1, half - 1 : half], (2 * owned, 1)) == ids[:, 0:1]
    middle_share = jnp.sum(jnp.where(middle, share, 0.0), axis=0, keepdims=True)
    below = zr[...]
    hx_below = [yr[2 * r * nx : (2 * r + 1) * nx, :] - COURANT * first_y[r, 1] for r in range(2)]
    hz_below = [yr[(2 * r + 1) * nx : (2 * r + 2) * nx, :] + COURANT * first_y[r, 0] for r in range(2)]
    dims = (((1,), (1,)), ((), ()))
    group = LANES // ny
    products = []
    for x in range(nx):
        coefficient = update_coefficient(material[x])
        news = []
        for r, (e, h, hz, en) in enumerate(runs):
            at_x, at_y = packed_lane(r, 0, x, nx), packed_lane(r, 1, x, nx)
            hx, hy, hz_here = h[0, x], h[1, x], hz[2, x]
            hy_x, hz_x = (h[1, x - 1], hz[2, x - 1]) if x else (xr[2 * r], xr[2 * r + 1])
            hx_y = down_y(hx, hx_below[r][x : x + 1, :])
            hz_y = down_y(hz_here, hz_below[r][x : x + 1, :])
            hx_z = down_z(hx, below, at_x)
            hy_z = down_z(hy, below, at_y)
            ex = e[0, x] + coefficient * ((hz_here - hz_y) - (hy - hy_z))
            ey = e[1, x] + coefficient * ((hx - hx_z) - (hz_here - hz_x))
            ez = e[2, x] + coefficient * ((hy - hy_x) - (hx - hx_y))
            en[0, x] = ex
            en[1, x] = ey
            en[2, x] = ez
            news.append((ex, ey, ez))
        total = spec[0, x]
        for c in range(3):
            f, a = news[0][c], news[1][c]
            total = total + (f * (spec[1 + c, x] + both * a) + a * spec[4 + c, x])
        products.append(total)
        if len(products) == group:
            block = jnp.concatenate(products, axis=0)
            products = []
            sums = jnp.zeros((2 * owned, group * ny), jnp.float32)
            for _ in range(3):
                part = block.astype(jnp.bfloat16)
                block = block - part.astype(jnp.float32)
                sums = sums + lax.dot_general(hot, part, dims, preferred_element_type=jnp.float32)
            sums = sums * share
            where = pl.ds(x // group * owned, owned)
            own[where, :] = sums[:owned]
            other[where, :] = sums[owned:]
    f, a = (pack_open([e[2, x, 0 : 8 if x else ny, :] for x in range(nx)], nz - 1) for e in (efn, ean))
    ratio = COURANT * still[2]
    scaled = ratio * middle_share
    rest = scaled * (still[0] + both * a)
    rest = rest + pltpu.roll(scaled * (still[1] + both * f), nx, 1)
    rest = rest + pltpu.roll(scaled * ratio * both, 2 * nx, 1)
    rest = rest + pltpu.roll(ratio, 3 * nx, 1)
    along = xr[4]
    along = along + jnp.concatenate([yr[4 * nx : 4 * nx + 8, :], jnp.zeros((ny - 8, LANES), jnp.float32)], axis=0)
    rest = jnp.where(lower, rest, along)
    tile[...] = rest
    other[nx // group * owned :, :] = rest


def electric(ef, ea, hf, ha, hzf, hza, material, xr, yr, zr, first_y, spec, still, freq, layer_map, half, owned):
    _, nx, ny, nz = ef.shape
    field = vmem(3, nx, ny, nz)
    rows = nx * ny // LANES * owned
    return call(
        functools.partial(electric_body, half, owned),
        "electric",
        (field, field, vmem(rows, LANES), vmem(rows + ny, LANES), vmem(ny, LANES)),
        (VMEM,) * 5,
        [VMEM] * 15,
        nbytes=6700000,
    )(ef, ea, hf, ha, hzf, hza, material, xr, yr, zr, first_y, spec, still, freq, layer_map)


def store_body(ef, ea, hf, ha, hzf, hza, after, efn, ean, hfn, han, sems):
    copies = []
    for r, (e, h, hz, en, hn) in enumerate(((ef, hf, hzf, efn, hfn), (ea, ha, hza, ean, han))):
        for c in range(3):
            copies.append(pltpu.make_async_copy(e.at[c], en.at[c], sems.at[r, c]))
            copies.append(pltpu.make_async_copy((h if c < 2 else hz).at[c], hn.at[c], sems.at[r, 3 + c]))
    for copy in copies:
        copy.start()
    for copy in copies:
        copy.wait()


def store(ef, ea, hf, ha, hzf, hza, after):
    field = f32(*ef.shape)
    return call(
        store_body,
        "store",
        (field,) * 4,
        (ANY,) * 4,
        [VMEM] * 6 + [ANY],
        [pltpu.SemaphoreType.DMA((2, 6))],
        nbytes=3000000,
    )(ef, ea, hf, ha, hzf, hza, after)


def gradient_body(ef, ea, own, tile, came, layer_map, _f, _a, out, efn, ean, plane, rows, result, sems):
    owned, nx, ny = out.shape
    nz = ef.shape[3]
    half = layer_map.shape[1] // 2
    gz = lax.axis_index("gz")
    lower = gz == 0
    sums = own.shape[0]
    mine, theirs = tile[...], came[sums:, :]
    change, cells = jnp.where(lower, mine, theirs), jnp.where(lower, theirs, mine)
    cell = [cells, pltpu.roll(cells, LANES - nx, 1)]
    ratio = jnp.where(lower, pltpu.roll(change, LANES - 3 * nx, 1), 0.0)
    copies = []
    for r, (e, en) in enumerate(((ef, efn), (ea, ean))):
        add = ratio * cell[r]
        plane[r] = e[2, 0] + jnp.where(lane_ids(ny) == nz - 1, move(add, 0, nz - 1), 0.0)
        corner = (lane_ids(8) == nz - 1) & (row_ids(8) == 0)
        for x in range(1, nx):
            rows[r, x - 1] = e[2, x, 0:8, :] + jnp.where(corner, move(add[0:8, :], x, nz - 1), 0.0)
        copies.append(pltpu.make_async_copy(plane.at[r], en.at[2, 0], sems.at[r, 0]))
        copies.append(pltpu.make_async_copy(rows.at[r], en.at[2, 1:nx, 0:8], sems.at[r, 1]))
    for copy in copies:
        copy.start()
    by_a, by_both = pltpu.roll(change, LANES - nx, 1), pltpu.roll(change, LANES - 2 * nx, 1)
    missing = change * cell[0] + by_a * cell[1] + by_both * (cell[0] * cell[1])
    missing = jnp.transpose(missing)[0:nx, 0:ny]
    share = own[...] + came[0:sums, :]
    group = nx * owned // sums
    for x in range(nx):
        block = share[x // group * owned : (x // group + 1) * owned]
        at = x % group * ny
        result[:, x, :] = block[:, at : at + ny]
    middle = layer_map[0:1, half - 1 : half]
    for k in range(owned):
        mine = jnp.broadcast_to(middle == gz * owned + k, (nx, ny))
        result[k] = result[k] + jnp.where(mine, missing, 0.0)
    last = pltpu.make_async_copy(result, out, sems.at[0, 2])
    last.start()
    for copy in copies:
        copy.wait()
    last.wait()


def gradient(ef, ea, own, tile, came, layer_map, efn, ean, owned):
    _, nx, ny, nz = ef.shape
    return pl.pallas_call(
        gradient_body,
        out_shape=(f32(owned, nx, ny), f32(*efn.shape), f32(*ean.shape)),
        in_specs=[VMEM] * 6 + [ANY] * 2,
        out_specs=(ANY,) * 3,
        scratch_shapes=[
            pltpu.VMEM((2, ny, nz), jnp.float32),
            pltpu.VMEM((2, nx - 1, 8, nz), jnp.float32),
            pltpu.VMEM((owned, nx, ny), jnp.float32),
            pltpu.SemaphoreType.DMA((2, 3)),
        ],
        input_output_aliases={6: 1, 7: 2},
        compiler_params=pltpu.CompilerParams(vmem_limit_bytes=32 * MIB),
        cost_estimate=pl.CostEstimate(flops=100000, bytes_accessed=400000, transcendentals=0),
        name="gradient",
    )(ef, ea, own, tile, came, layer_map, efn, ean)


def shards(ef, hf, ea, ha, material, df, da, angular_freq, layer_map):
    _, nx, ny, nz = ef.shape
    half = df.shape[3]
    owned = LAYERS // lax.axis_size("gz")
    freq = angular_freq.reshape(1, -1)
    layer_map = layer_map.reshape(1, -1)
    df = jnp.transpose(df, (0, 1, 2, 4, 5, 3))
    da = jnp.transpose(da, (0, 1, 2, 4, 5, 3))
    xs, first_y, ef, ea, hf, ha, along_x, along_y = first_faces(ef, ea, hf, ha)
    yr = ring(first_y, "gy", -1)
    xr = ring(xs, "gx", -1)
    ys = last_y(ef, ea, hf, ha, xr, along_y)
    xs = last_x(ef, ea, hf, ha, xr, yr, along_x, ys)
    hf, ha, layer, zs = magnetic(ef, ea, hf, ha, xr, yr, xs)
    yr = ring(ys, "gy", 1)
    xr = ring(xs, "gx", 1)
    zr = ring(zs, "gz", 1)
    spec, still = spectra(df, da, freq, material, zs, nz)
    hxyf, hxya, below = complete(hf, ha, zr, layer)
    ef, ea, own, other, tile = electric(
        ef, ea, hxyf, hxya, hf, ha, material, xr, yr, below, first_y, spec, still, freq, layer_map, half, owned
    )
    came = ring(other, "gz", 1)
    efn, ean, hfn, han = store(ef, ea, hxyf, hxya, hf, ha, own)
    out, efn, ean = gradient(ef, ea, own, tile, came, layer_map, efn, ean, owned)
    return efn, hfn, ean, han, out


def solution(mesh):
    field = P(None, "gx", "gy", "gz")
    dft = P(None, None, None, "gz", "gx", "gy")
    return jax.shard_map(
        shards,
        mesh=mesh,
        in_specs=(field, field, field, field, P("gx", "gy", "gz"), dft, dft, P(), P()),
        out_specs=(field, field, field, field, P("gz", "gx", "gy")),
        check_vma=False,
    )
```

```python
import functools

import jax
import jax.numpy as jnp
from jax import lax
from jax.experimental import pallas as pl
from jax.experimental.pallas import tpu as pltpu
from jax.sharding import PartitionSpec as P

LAYERS = 16
STEP = 40
PERMITTIVITIES = (1.0, 2.1, 4.0, 12.0)
COURANT = 0.5
LANES = 128
MIB = 1024 * 1024
ANY = pl.BlockSpec(memory_space=pl.ANY)
VMEM = pl.BlockSpec(memory_space=pltpu.VMEM)


def f32(*shape):
    return jax.ShapeDtypeStruct(shape, jnp.float32)


def vmem(*shape):
    return pltpu.VMEM(shape, jnp.float32)


def hbm(x):
    return pltpu.with_memory_space_constraint(x, pltpu.HBM)


def ring(x, axis, by):
    peers = lax.axis_size(axis)
    return lax.ppermute(x, axis, [(i, (i + by) % peers) for i in range(peers)])


def call(body, name, outs, out_specs, in_specs, scratch=(), nbytes=100000, limit=32):
    return pl.pallas_call(
        body,
        out_shape=outs,
        in_specs=in_specs,
        out_specs=out_specs,
        scratch_shapes=list(scratch),
        compiler_params=pltpu.CompilerParams(vmem_limit_bytes=limit * MIB),
        cost_estimate=pl.CostEstimate(flops=nbytes, bytes_accessed=nbytes, transcendentals=0),
        name=name,
    )


def lane_ids(rows):
    return lax.broadcasted_iota(jnp.int32, (rows, LANES), 1)


def row_ids(rows):
    return lax.broadcasted_iota(jnp.int32, (rows, LANES), 0)


def move(a, source, target):
    shift = (target - source) % LANES
    return pltpu.roll(a, shift, 1) if shift else a


def up_y(a):
    n = a.shape[0]
    return jnp.where(row_ids(n) == n - 1, 0.0, pltpu.roll(a, n - 1, 0))


def down_y(a, row):
    return jnp.where(row_ids(a.shape[0]) == 0, jnp.broadcast_to(row, a.shape), pltpu.roll(a, 1, 0))


def up_z(a):
    n = a.shape[1]
    return jnp.where(lane_ids(a.shape[0]) == n - 1, 0.0, pltpu.roll(a, n - 1, 1))


def down_z(a, packed, lane):
    return jnp.where(lane_ids(a.shape[0]) == 0, move(packed, lane, 0), pltpu.roll(a, 1, 1))


def first_faces_body(ef, ea, hf, ha, xs, ys, evf, eva, hvf, hva, along_x, along_y, sems):
    fields = (evf, eva)
    _, nx, ny, _ = ef.shape
    copies = {}
    for k, (pair, held) in enumerate((((ef, ea), (evf, eva)), ((hf, ha), (hvf, hva)))):
        for c in range(3):
            for r in range(2):
                copies[k, c, r] = pltpu.make_async_copy(pair[r].at[c], held[r].at[c], sems.at[k, r, c])
                copies[k, c, r].start()
    for c in range(3):
        for r, v in enumerate(fields):
            copies[0, c, r].wait()
            if c != 1:
                for x in range(nx):
                    ys[r, c // 2, x : x + 1, :] = v[c, x, 0:1, :]
            if c:
                xs[r, c - 1] = v[c, 0]
    lane, lane_8 = lane_ids(ny), lane_ids(8)
    by_x = jnp.zeros((ny, LANES), jnp.float32)
    by_y = jnp.zeros((8, LANES), jnp.float32)
    for r, e in enumerate(fields):
        by_x = jnp.where(lane == r, move(e[0, nx - 1], 0, r), by_x)
        for x in range(nx):
            by_y = jnp.where(lane_8 == r * nx + x, move(e[1, x, ny - 8 : ny, :], 0, r * nx + x), by_y)
    turned = jnp.transpose(by_x)[0:8, :]
    along_x[...] = jnp.concatenate([turned, jnp.zeros((8, LANES - ny), jnp.float32)], axis=1)
    along_y[...] = jnp.where(row_ids(8) == 0, pltpu.roll(by_y, 1, 0), 0.0)
    for c in range(3):
        for r in range(2):
            copies[1, c, r].wait()


def first_faces(ef, ea, hf, ha):
    _, nx, ny, nz = ef.shape
    field = vmem(3, nx, ny, nz)
    return call(
        first_faces_body,
        "first_faces",
        (vmem(2, 2, ny, nz), vmem(2, 2, nx, nz)) + (field,) * 4 + (vmem(8, LANES), vmem(8, LANES)),
        (VMEM,) * 8,
        [ANY] * 4,
        [pltpu.SemaphoreType.DMA((2, 2, 3))],
        nbytes=3000000,
    )(hbm(ef), hbm(ea), hbm(hf), hbm(ha))


def magnetic_update(e, h, x, rows, next_x, r):
    nx = e.shape[1]
    ex, ey, ez = e[0, x, rows], e[1, x, rows], e[2, x, rows]
    ey_x, ez_x = (e[1, x + 1, rows], e[2, x + 1, rows]) if x + 1 < nx else (next_x[r, 0, rows], next_x[r, 1, rows])
    ex_y = up_y(ex)
    ez_y = up_y(ez)
    ex_z = up_z(ex)
    ey_z = up_z(ey)
    hx = h[0, x, rows] - COURANT * ((ez_y - ez) - (ey_z - ey))
    hy = h[1, x, rows] - COURANT * ((ex_z - ex) - (ez_x - ez))
    hz = h[2, x, rows] - COURANT * ((ey_x - ey) - (ex_y - ex))
    return hx, hy, hz


def last_y_body(ef, ea, hf, ha, xr, along_y, ys):
    _, nx, ny, _ = ef.shape
    last = slice(ny - 8, ny)
    for r, (e, h) in enumerate(((ef, hf), (ea, ha))):
        for x in range(nx):
            hx, _, hz = magnetic_update(e, h, x, last, xr, r)
            for c, a in enumerate((hx, hz)):
                at = packed_lane(r, c, x, nx)
                ys[at : at + 1, :] = a[7:8, :]
    ys[4 * nx : 4 * nx + 8, :] = along_y[...]


def last_y(ef, ea, hf, ha, xr, along_y):
    _, nx, ny, nz = ef.shape
    return call(
        last_y_body,
        "last_y",
        vmem(4 * nx + 80, nz),
        VMEM,
        [VMEM] * 6,
        nbytes=500000,
    )(ef, ea, hf, ha, xr, along_y)


def magnetic_body(ef, ea, hf, ha, xr, after, hfn, han, layer, top):
    _, nx, ny, nz = ef.shape
    for x in range(nx):
        for r, (e, h, hn) in enumerate(((ef, hf, hfn), (ea, ha, han))):
            hn[0, x], hn[1, x], hn[2, x] = magnetic_update(e, h, x, slice(0, ny), xr, r)
    layer[...] = pack_layer((ef, ea), nx, ny, 0)
    top[...] = pack_layer((hfn, han), nx, ny, nz - 1)


def magnetic(ef, ea, hf, ha, xr, after):
    _, nx, ny, nz = ef.shape
    field = vmem(3, nx, ny, nz)
    return call(
        magnetic_body,
        "magnetic",
        (field, field, vmem(ny, LANES), vmem(ny, LANES)),
        (VMEM,) * 4,
        [VMEM] * 5 + [ANY],
        nbytes=4800000,
    )(ef, ea, hf, ha, xr, after)


def last_faces_body(hf, ha, yr, along_x, layer, top, hfn, han, xs, zs):
    _, nx, ny, nz = hf.shape
    last = slice(ny - 8, ny)
    edge, lane = row_ids(8) == 7, lane_ids(8)
    rows = top[last, :]
    for r, (h, hn) in enumerate(((hf, hfn), (ha, han))):
        for x in range(nx):
            hx = h[0, x, last, :] - COURANT * jnp.where(edge, jnp.broadcast_to(yr[r, 1, x : x + 1, :], (8, nz)), 0.0)
            hz = h[2, x, last, :] + COURANT * jnp.where(edge, jnp.broadcast_to(yr[r, 0, x : x + 1, :], (8, nz)), 0.0)
            hn[0, x, last, :] = hx
            hn[2, x, last, :] = hz
            to = packed_lane(r, 0, x, nx)
            rows = jnp.where(lane == to, move(hx, nz - 1, to), rows)
        at = r * 2 * ny
        xs[at : at + ny, :] = h[1, nx - 1]
        xs[at + ny : at + 2 * ny - 8, :] = h[2, nx - 1, 0 : ny - 8, :]
        xs[at + 2 * ny - 8 : at + 2 * ny, :] = hz
    xs[4 * ny :, :] = along_x[...]
    lower = lax.axis_index("gz") == 0
    zs[...] = jnp.where(lower, top[...], layer[...])
    zs[last, :] = jnp.where(lower, rows, layer[last, :])


def last_faces(hf, ha, yr, along_x, layer, top):
    _, nx, ny, nz = hf.shape
    field = vmem(3, nx, ny, nz)
    return pl.pallas_call(
        last_faces_body,
        out_shape=(field, field, vmem(4 * ny + 8, nz), vmem(ny, LANES)),
        in_specs=[VMEM] * 6,
        out_specs=(VMEM,) * 4,
        input_output_aliases={0: 0, 1: 1},
        compiler_params=pltpu.CompilerParams(vmem_limit_bytes=32 * MIB),
        cost_estimate=pl.CostEstimate(flops=500000, bytes_accessed=500000, transcendentals=0),
        name="last_faces",
    )(hf, ha, yr, along_x, layer, top)


def packed_lane(r, c, x, nx):
    return (r * 2 + c) * nx + x


def pack_layer(fields, nx, ny, z):
    lane = lane_ids(ny)
    total = jnp.zeros((ny, LANES), jnp.float32)
    for r, f in enumerate(fields):
        for c in range(2):
            for x in range(nx):
                to = packed_lane(r, c, x, nx)
                total = jnp.where(lane == to, move(f[c, x], z, to), total)
    return total


def from_layer_above(tile, nx):
    first = lax.rem(lane_ids(tile.shape[0]) // nx, 2) == 0
    return COURANT * jnp.where(first, pltpu.roll(tile, LANES - nx, 1), -pltpu.roll(tile, nx, 1))


def pack_open(planes, z):
    ny = planes[0].shape[0]
    lane_8 = lane_ids(8)
    first = jnp.where(lane_ids(ny) == 0, move(planes[0], z, 0), 0.0)
    top = first[0:8, :]
    for x in range(1, len(planes)):
        top = jnp.where(lane_8 == x, move(planes[x], z, x), top)
    return jnp.concatenate([top, first[8:, :]], axis=0)


def update_coefficient(m):
    return jnp.where(
        m == 0,
        COURANT / PERMITTIVITIES[0],
        jnp.where(
            m == 1,
            COURANT / PERMITTIVITIES[1],
            jnp.where(m == 2, COURANT / PERMITTIVITIES[2], COURANT / PERMITTIVITIES[3]),
        ),
    )


def slab_start(nz, half):
    return (1 - lax.axis_index("gz")) * (nz - half)


def spectra_body(half, nz, dfv, dav, freq, material, after, out, still):
    freqs, nx, ny = dfv.shape[0], dfv.shape[3], dfv.shape[4]
    phase = freq[...] * float(STEP)
    cos, sin = jnp.cos(phase), jnp.sin(phase)
    cs = [jnp.broadcast_to(cos[:, f : f + 1], (ny, half)) for f in range(freqs)]
    sn = [jnp.broadcast_to(sin[:, f : f + 1], (ny, half)) for f in range(freqs)]
    shift = slab_start(nz, half)
    blank = jnp.zeros((ny, LANES - half), jnp.float32)

    def place(a):
        return pltpu.roll(jnp.concatenate([a, blank], axis=1), shift, 1)

    for x in range(nx):
        base = jnp.zeros((ny, half), jnp.float32)
        for c in range(3):
            with_forward = jnp.zeros((ny, half), jnp.float32)
            with_adjoint = jnp.zeros((ny, half), jnp.float32)
            for f in range(freqs):
                rf, jf, ra, ja = dfv[f, 0, c, x], dfv[f, 1, c, x], dav[f, 0, c, x], dav[f, 1, c, x]
                base = base + (rf * ra - jf * ja)
                with_forward = with_forward + (cs[f] * ra + sn[f] * ja)
                with_adjoint = with_adjoint + (cs[f] * rf + sn[f] * jf)
            out[1 + c, x] = place(with_forward)
            out[4 + c, x] = place(with_adjoint)
        out[0, x] = place(base)

    def cells(planes):
        return pack_open([planes(x, slice(0, 8 if x else ny)) for x in range(nx)], nz - 1)

    still[0] = cells(lambda x, rows: out[3, x, rows])
    still[1] = cells(lambda x, rows: out[6, x, rows])
    still[2] = cells(lambda x, rows: update_coefficient(material[x, rows]))


def spectra(df, da, freq, material, after, nz):
    _, _, _, nx, ny, half = df.shape
    return call(
        functools.partial(spectra_body, half, nz),
        "spectra",
        (vmem(7, nx, ny, LANES), vmem(3, ny, LANES)),
        (VMEM,) * 2,
        [VMEM] * 4 + [ANY],
        nbytes=11000000,
    )(df, da, freq, material, after)


def complete_body(hf, ha, zr, layer, hfn, han, below):
    _, nx, ny, nz = hf.shape
    lower = lax.axis_index("gz") == 0
    came = zr[...]
    above = jnp.where(lower, from_layer_above(came, nx), 0.0)
    below[...] = jnp.where(lower, 0.0, came + from_layer_above(layer[...], nx))
    top = lane_ids(ny) == nz - 1
    for r, (h, hn) in enumerate(((hf, hfn), (ha, han))):
        for c in range(2):
            for x in range(nx):
                hn[c, x] = h[c, x] + jnp.where(top, move(above, packed_lane(r, c, x, nx), nz - 1), 0.0)


def complete(hf, ha, zr, layer):
    _, nx, ny, nz = hf.shape
    part = vmem(2, nx, ny, nz)
    return call(
        complete_body,
        "complete",
        (part, part, vmem(ny, LANES)),
        (VMEM,) * 3,
        [VMEM] * 4,
        nbytes=2000000,
    )(hf, ha, zr, layer)


def electric_body(
    half, owned, ef, ea, hf, ha, hzf, hza, material, xr, yr, zr, first_y, spec, still, freq, layer_map, efn, ean, own, other, tile
):
    runs = ((ef, hf, hzf, efn), (ea, ha, hza, ean))
    _, nx, ny, nz = ef.shape
    phase = freq[...] * float(STEP)
    cos, sin = jnp.cos(phase), jnp.sin(phase)
    both = jnp.sum(cos * cos - sin * sin, axis=1, keepdims=True)
    gz = lax.axis_index("gz")
    lower = gz == 0
    start = slab_start(nz, half)
    slab = layer_map.shape[1]
    cells = jnp.concatenate([layer_map[...], jnp.full((1, LANES - slab), -1, jnp.int32)], axis=1)
    cells = pltpu.roll(jnp.broadcast_to(cells, (8, LANES)), lax.rem(start + LANES - gz * half, LANES), 1)
    lane, row = lane_ids(2 * owned), row_ids(2 * owned)
    inside = (lane >= start) & (lane < start + half)
    cells = jnp.broadcast_to(cells[0:1, :], (2 * owned, LANES))
    ids = lax.rem(row + gz * owned, 2 * owned)
    hot = jnp.where(inside & (cells == ids), 1.0, 0.0).astype(jnp.bfloat16)
    owner = jnp.broadcast_to(layer_map[...], (2 * owned, slab)) == ids[:, :slab]
    share = 1.0 / (3.0 * jnp.sum(jnp.where(owner, 1.0, 0.0), axis=1, keepdims=True))
    middle = jnp.broadcast_to(layer_map[0:1, half - 1 : half], (2 * owned, 1)) == ids[:, 0:1]
    middle_share = jnp.sum(jnp.where(middle, share, 0.0), axis=0, keepdims=True)
    below = zr[...]
    hx_below = [yr[2 * r * nx : (2 * r + 1) * nx, :] - COURANT * first_y[r, 1] for r in range(2)]
    hz_below = [yr[(2 * r + 1) * nx : (2 * r + 2) * nx, :] + COURANT * first_y[r, 0] for r in range(2)]
    dims = (((1,), (1,)), ((), ()))
    group = LANES // ny
    products = []
    for x in range(nx):
        coefficient = update_coefficient(material[x])
        news = []
        for r, (e, h, hz, en) in enumerate(runs):
            at_x, at_y = packed_lane(r, 0, x, nx), packed_lane(r, 1, x, nx)
            hx, hy, hz_here = h[0, x], h[1, x], hz[2, x]
            hy_x, hz_x = (h[1, x - 1], hz[2, x - 1]) if x else (xr[2 * r * ny : (2 * r + 1) * ny, :], xr[(2 * r + 1) * ny : (2 * r + 2) * ny, :])
            hx_y = down_y(hx, hx_below[r][x : x + 1, :])
            hz_y = down_y(hz_here, hz_below[r][x : x + 1, :])
            hx_z = down_z(hx, below, at_x)
            hy_z = down_z(hy, below, at_y)
            ex = e[0, x] + coefficient * ((hz_here - hz_y) - (hy - hy_z))
            ey = e[1, x] + coefficient * ((hx - hx_z) - (hz_here - hz_x))
            ez = e[2, x] + coefficient * ((hy - hy_x) - (hx - hx_y))
            en[0, x] = ex
            en[1, x] = ey
            en[2, x] = ez
            news.append((ex, ey, ez))
        total = spec[0, x]
        for c in range(3):
            f, a = news[0][c], news[1][c]
            total = total + (f * (spec[1 + c, x] + both * a) + a * spec[4 + c, x])
        products.append(total)
        if len(products) == group:
            block = jnp.concatenate(products, axis=0)
            products = []
            sums = jnp.zeros((2 * owned, group * ny), jnp.float32)
            for _ in range(3):
                part = block.astype(jnp.bfloat16)
                block = block - part.astype(jnp.float32)
                sums = sums + lax.dot_general(hot, part, dims, preferred_element_type=jnp.float32)
            sums = sums * share
            where = pl.ds(x // group * owned, owned)
            own[where, :] = sums[:owned]
            other[where, :] = sums[owned:]
    f, a = (pack_open([e[2, x, 0 : 8 if x else ny, :] for x in range(nx)], nz - 1) for e in (efn, ean))
    ratio = COURANT * still[2]
    scaled = ratio * middle_share
    rest = scaled * (still[0] + both * a)
    rest = rest + pltpu.roll(scaled * (still[1] + both * f), nx, 1)
    rest = rest + pltpu.roll(scaled * ratio * both, 2 * nx, 1)
    rest = rest + pltpu.roll(ratio, 3 * nx, 1)
    turned = jnp.concatenate([xr[4 * ny :, :], jnp.zeros((ny - 8, LANES), jnp.float32)], axis=0)
    turned = jnp.transpose(turned)[0:ny, :]
    turned = jnp.concatenate([turned, jnp.zeros((ny, LANES - ny), jnp.float32)], axis=1)
    lane = lane_ids(ny)
    along = jnp.where(lane == 0, turned, jnp.where(lane == nx, move(turned, 1, nx), 0.0))
    along = along + jnp.concatenate([yr[4 * nx : 4 * nx + 8, :], jnp.zeros((ny - 8, LANES), jnp.float32)], axis=0)
    rest = jnp.where(lower, rest, along)
    tile[...] = rest
    other[nx // group * owned :, :] = rest


def electric(ef, ea, hf, ha, hzf, hza, material, xr, yr, zr, first_y, spec, still, freq, layer_map, half, owned):
    _, nx, ny, nz = ef.shape
    field = vmem(3, nx, ny, nz)
    rows = nx * ny // LANES * owned
    return call(
        functools.partial(electric_body, half, owned),
        "electric",
        (field, field, vmem(rows, LANES), vmem(rows + ny, LANES), vmem(ny, LANES)),
        (VMEM,) * 5,
        [VMEM] * 15,
        nbytes=6700000,
    )(ef, ea, hf, ha, hzf, hza, material, xr, yr, zr, first_y, spec, still, freq, layer_map)


def store_body(ef, ea, hf, ha, hzf, hza, after, efn, ean, hfn, han, sems):
    copies = []
    for r, (e, h, hz, en, hn) in enumerate(((ef, hf, hzf, efn, hfn), (ea, ha, hza, ean, han))):
        for c in range(3):
            copies.append(pltpu.make_async_copy(e.at[c], en.at[c], sems.at[r, c]))
            copies.append(pltpu.make_async_copy((h if c < 2 else hz).at[c], hn.at[c], sems.at[r, 3 + c]))
    for copy in copies:
        copy.start()
    for copy in copies:
        copy.wait()


def store(ef, ea, hf, ha, hzf, hza, after):
    field = f32(*ef.shape)
    return call(
        store_body,
        "store",
        (field,) * 4,
        (ANY,) * 4,
        [VMEM] * 6 + [ANY],
        [pltpu.SemaphoreType.DMA((2, 6))],
        nbytes=3000000,
    )(ef, ea, hf, ha, hzf, hza, after)


def gradient_body(ef, ea, own, tile, came, layer_map, _f, _a, out, efn, ean, plane, rows, result, sems):
    owned, nx, ny = out.shape
    nz = ef.shape[3]
    half = layer_map.shape[1] // 2
    gz = lax.axis_index("gz")
    lower = gz == 0
    sums = own.shape[0]
    mine, theirs = tile[...], came[sums:, :]
    change, cells = jnp.where(lower, mine, theirs), jnp.where(lower, theirs, mine)
    cell = [cells, pltpu.roll(cells, LANES - nx, 1)]
    ratio = jnp.where(lower, pltpu.roll(change, LANES - 3 * nx, 1), 0.0)
    copies = []
    for r, (e, en) in enumerate(((ef, efn), (ea, ean))):
        add = ratio * cell[r]
        plane[r] = e[2, 0] + jnp.where(lane_ids(ny) == nz - 1, move(add, 0, nz - 1), 0.0)
        corner = (lane_ids(8) == nz - 1) & (row_ids(8) == 0)
        for x in range(1, nx):
            rows[r, x - 1] = e[2, x, 0:8, :] + jnp.where(corner, move(add[0:8, :], x, nz - 1), 0.0)
        copies.append(pltpu.make_async_copy(plane.at[r], en.at[2, 0], sems.at[r, 0]))
        copies.append(pltpu.make_async_copy(rows.at[r], en.at[2, 1:nx, 0:8], sems.at[r, 1]))
    for copy in copies:
        copy.start()
    by_a, by_both = pltpu.roll(change, LANES - nx, 1), pltpu.roll(change, LANES - 2 * nx, 1)
    missing = change * cell[0] + by_a * cell[1] + by_both * (cell[0] * cell[1])
    missing = jnp.transpose(missing)[0:nx, 0:ny]
    share = own[...] + came[0:sums, :]
    group = nx * owned // sums
    for x in range(nx):
        block = share[x // group * owned : (x // group + 1) * owned]
        at = x % group * ny
        result[:, x, :] = block[:, at : at + ny]
    middle = layer_map[0:1, half - 1 : half]
    for k in range(owned):
        mine = jnp.broadcast_to(middle == gz * owned + k, (nx, ny))
        result[k] = result[k] + jnp.where(mine, missing, 0.0)
    last = pltpu.make_async_copy(result, out, sems.at[0, 2])
    last.start()
    for copy in copies:
        copy.wait()
    last.wait()


def gradient(ef, ea, own, tile, came, layer_map, efn, ean, owned):
    _, nx, ny, nz = ef.shape
    return pl.pallas_call(
        gradient_body,
        out_shape=(f32(owned, nx, ny), f32(*efn.shape), f32(*ean.shape)),
        in_specs=[VMEM] * 6 + [ANY] * 2,
        out_specs=(ANY,) * 3,
        scratch_shapes=[
            pltpu.VMEM((2, ny, nz), jnp.float32),
            pltpu.VMEM((2, nx - 1, 8, nz), jnp.float32),
            pltpu.VMEM((owned, nx, ny), jnp.float32),
            pltpu.SemaphoreType.DMA((2, 3)),
        ],
        input_output_aliases={6: 1, 7: 2},
        compiler_params=pltpu.CompilerParams(vmem_limit_bytes=32 * MIB),
        cost_estimate=pl.CostEstimate(flops=100000, bytes_accessed=400000, transcendentals=0),
        name="gradient",
    )(ef, ea, own, tile, came, layer_map, efn, ean)


def shards(ef, hf, ea, ha, material, df, da, angular_freq, layer_map):
    _, nx, ny, nz = ef.shape
    half = df.shape[3]
    owned = LAYERS // lax.axis_size("gz")
    freq = angular_freq.reshape(1, -1)
    layer_map = layer_map.reshape(1, -1)
    df = jnp.transpose(df, (0, 1, 2, 4, 5, 3))
    da = jnp.transpose(da, (0, 1, 2, 4, 5, 3))
    xs, first_y, ef, ea, hf, ha, along_x, along_y = first_faces(ef, ea, hf, ha)
    yr = ring(first_y, "gy", -1)
    xr = ring(xs, "gx", -1)
    ys = last_y(ef, ea, hf, ha, xr, along_y)
    hf, ha, layer, top = magnetic(ef, ea, hf, ha, xr, ys)
    hf, ha, xs, zs = last_faces(hf, ha, yr, along_x, layer, top)
    yr = ring(ys, "gy", 1)
    xr = ring(xs, "gx", 1)
    zr = ring(zs, "gz", 1)
    spec, still = spectra(df, da, freq, material, zs, nz)
    hxyf, hxya, below = complete(hf, ha, zr, layer)
    ef, ea, own, other, tile = electric(
        ef, ea, hxyf, hxya, hf, ha, material, xr, yr, below, first_y, spec, still, freq, layer_map, half, owned
    )
    came = ring(other, "gz", 1)
    efn, ean, hfn, han = store(ef, ea, hxyf, hxya, hf, ha, own)
    out, efn, ean = gradient(ef, ea, own, tile, came, layer_map, efn, ean, owned)
    return efn, hfn, ean, han, out


def solution(mesh):
    field = P(None, "gx", "gy", "gz")
    dft = P(None, None, None, "gz", "gx", "gy")
    return jax.shard_map(
        shards,
        mesh=mesh,
        in_specs=(field, field, field, field, P("gx", "gy", "gz"), dft, dft, P(), P()),
        out_specs=(field, field, field, field, P("gz", "gx", "gy")),
        check_vma=False,
    )
```

```python
import functools

import jax
import jax.numpy as jnp
from jax import lax
from jax.experimental import pallas as pl
from jax.experimental.pallas import tpu as pltpu
from jax.sharding import PartitionSpec as P

LAYERS = 16
STEP = 40
PERMITTIVITIES = (1.0, 2.1, 4.0, 12.0)
COURANT = 0.5
LANES = 128
MIB = 1024 * 1024
ANY = pl.BlockSpec(memory_space=pl.ANY)
VMEM = pl.BlockSpec(memory_space=pltpu.VMEM)


def f32(*shape):
    return jax.ShapeDtypeStruct(shape, jnp.float32)


def vmem(*shape):
    return pltpu.VMEM(shape, jnp.float32)


def hbm(x):
    return pltpu.with_memory_space_constraint(x, pltpu.HBM)


def ring(x, axis, by):
    peers = lax.axis_size(axis)
    return lax.ppermute(x, axis, [(i, (i + by) % peers) for i in range(peers)])


def call(body, name, outs, out_specs, in_specs, scratch=(), nbytes=100000, limit=32):
    return pl.pallas_call(
        body,
        out_shape=outs,
        in_specs=in_specs,
        out_specs=out_specs,
        scratch_shapes=list(scratch),
        compiler_params=pltpu.CompilerParams(vmem_limit_bytes=limit * MIB),
        cost_estimate=pl.CostEstimate(flops=nbytes, bytes_accessed=nbytes, transcendentals=0),
        name=name,
    )


def lane_ids(rows):
    return lax.broadcasted_iota(jnp.int32, (rows, LANES), 1)


def row_ids(rows):
    return lax.broadcasted_iota(jnp.int32, (rows, LANES), 0)


def move(a, source, target):
    shift = (target - source) % LANES
    return pltpu.roll(a, shift, 1) if shift else a


def up_y(a):
    n = a.shape[0]
    return jnp.where(row_ids(n) == n - 1, 0.0, pltpu.roll(a, n - 1, 0))


def down_y(a, row):
    return jnp.where(row_ids(a.shape[0]) == 0, jnp.broadcast_to(row, a.shape), pltpu.roll(a, 1, 0))


def up_z(a):
    n = a.shape[1]
    return jnp.where(lane_ids(a.shape[0]) == n - 1, 0.0, pltpu.roll(a, n - 1, 1))


def down_z(a, packed, lane):
    return jnp.where(lane_ids(a.shape[0]) == 0, move(packed, lane, 0), pltpu.roll(a, 1, 1))


def first_faces_body(ef, ea, hf, ha, xs, ys, evf, eva, hvf, hva, along_x, along_y, sems):
    fields = (evf, eva)
    _, nx, ny, _ = ef.shape
    copies = {}
    for k, (pair, held) in enumerate((((ef, ea), (evf, eva)), ((hf, ha), (hvf, hva)))):
        for c in range(3):
            for r in range(2):
                copies[k, c, r] = pltpu.make_async_copy(pair[r].at[c], held[r].at[c], sems.at[k, r, c])
                copies[k, c, r].start()
    for c in range(3):
        for r, v in enumerate(fields):
            copies[0, c, r].wait()
            if c != 1:
                for x in range(nx):
                    ys[r, c // 2, x : x + 1, :] = v[c, x, 0:1, :]
            if c:
                xs[r, c - 1] = v[c, 0]
    lane, lane_8 = lane_ids(ny), lane_ids(8)
    by_x = jnp.zeros((ny, LANES), jnp.float32)
    by_y = jnp.zeros((8, LANES), jnp.float32)
    for r, e in enumerate(fields):
        by_x = jnp.where(lane == r, move(e[0, nx - 1], 0, r), by_x)
        for x in range(nx):
            by_y = jnp.where(lane_8 == r * nx + x, move(e[1, x, ny - 8 : ny, :], 0, r * nx + x), by_y)
    turned = jnp.transpose(by_x)[0:8, :]
    along_x[...] = jnp.concatenate([turned, jnp.zeros((8, LANES - ny), jnp.float32)], axis=1)
    along_y[...] = jnp.where(row_ids(8) == 0, pltpu.roll(by_y, 1, 0), 0.0)
    for c in range(3):
        for r in range(2):
            copies[1, c, r].wait()


def first_faces(ef, ea, hf, ha):
    _, nx, ny, nz = ef.shape
    field = vmem(3, nx, ny, nz)
    return call(
        first_faces_body,
        "first_faces",
        (vmem(2, 2, ny, nz), vmem(2, 2, nx, nz)) + (field,) * 4 + (vmem(8, LANES), vmem(8, LANES)),
        (VMEM,) * 8,
        [ANY] * 4,
        [pltpu.SemaphoreType.DMA((2, 2, 3))],
        nbytes=3000000,
    )(hbm(ef), hbm(ea), hbm(hf), hbm(ha))


def magnetic_update(e, h, x, rows, next_x, r):
    nx = e.shape[1]
    ex, ey, ez = e[0, x, rows], e[1, x, rows], e[2, x, rows]
    ey_x, ez_x = (e[1, x + 1, rows], e[2, x + 1, rows]) if x + 1 < nx else (next_x[r, 0, rows], next_x[r, 1, rows])
    ex_y = up_y(ex)
    ez_y = up_y(ez)
    ex_z = up_z(ex)
    ey_z = up_z(ey)
    hx = h[0, x, rows] - COURANT * ((ez_y - ez) - (ey_z - ey))
    hy = h[1, x, rows] - COURANT * ((ex_z - ex) - (ez_x - ez))
    hz = h[2, x, rows] - COURANT * ((ey_x - ey) - (ex_y - ex))
    return hx, hy, hz


def last_y_body(ef, ea, hf, ha, xr, along_y, ys):
    _, nx, ny, _ = ef.shape
    last = slice(ny - 8, ny)
    for r, (e, h) in enumerate(((ef, hf), (ea, ha))):
        for x in range(nx):
            hx, _, hz = magnetic_update(e, h, x, last, xr, r)
            for c, a in enumerate((hx, hz)):
                at = packed_lane(r, c, x, nx)
                ys[at : at + 1, :] = a[7:8, :]
    ys[4 * nx : 4 * nx + 8, :] = along_y[...]
    ys[4 * nx + 8 :, :] = jnp.zeros((ys.shape[0] - 4 * nx - 8, ys.shape[1]), jnp.float32)


def last_y(ef, ea, hf, ha, xr, along_y):
    _, nx, ny, nz = ef.shape
    return call(
        last_y_body,
        "last_y",
        vmem(max(4 * nx, 4 * ny + 8) + 8, nz),
        VMEM,
        [VMEM] * 6,
        nbytes=500000,
    )(ef, ea, hf, ha, xr, along_y)


def magnetic_body(ef, ea, hf, ha, xr, after, hfn, han, layer, top):
    _, nx, ny, nz = ef.shape
    for x in range(nx):
        for r, (e, h, hn) in enumerate(((ef, hf, hfn), (ea, ha, han))):
            hn[0, x], hn[1, x], hn[2, x] = magnetic_update(e, h, x, slice(0, ny), xr, r)
    layer[...] = pack_layer((ef, ea), nx, ny, 0)
    top[...] = pack_layer((hfn, han), nx, ny, nz - 1)


def magnetic(ef, ea, hf, ha, xr, after):
    _, nx, ny, nz = ef.shape
    field = vmem(3, nx, ny, nz)
    return call(
        magnetic_body,
        "magnetic",
        (field, field, vmem(ny, LANES), vmem(ny, LANES)),
        (VMEM,) * 4,
        [VMEM] * 5 + [ANY],
        nbytes=4800000,
    )(ef, ea, hf, ha, xr, after)


def last_faces_body(hf, ha, yr, along_x, layer, top, hfn, han, xs, zs):
    _, nx, ny, nz = hf.shape
    last = slice(ny - 8, ny)
    edge, lane = row_ids(8) == 7, lane_ids(8)
    rows = top[last, :]
    for r, (h, hn) in enumerate(((hf, hfn), (ha, han))):
        for x in range(nx):
            hx = h[0, x, last, :] - COURANT * jnp.where(edge, jnp.broadcast_to(yr[r, 1, x : x + 1, :], (8, nz)), 0.0)
            hz = h[2, x, last, :] + COURANT * jnp.where(edge, jnp.broadcast_to(yr[r, 0, x : x + 1, :], (8, nz)), 0.0)
            hn[0, x, last, :] = hx
            hn[2, x, last, :] = hz
            to = packed_lane(r, 0, x, nx)
            rows = jnp.where(lane == to, move(hx, nz - 1, to), rows)
        at = r * 2 * ny
        xs[at : at + ny, :] = h[1, nx - 1]
        xs[at + ny : at + 2 * ny - 8, :] = h[2, nx - 1, 0 : ny - 8, :]
        xs[at + 2 * ny - 8 : at + 2 * ny, :] = hz
    xs[4 * ny :, :] = along_x[...]
    lower = lax.axis_index("gz") == 0
    zs[...] = jnp.where(lower, top[...], layer[...])
    zs[last, :] = jnp.where(lower, rows, layer[last, :])


def last_faces(hf, ha, yr, along_x, layer, top):
    _, nx, ny, nz = hf.shape
    field = vmem(3, nx, ny, nz)
    return pl.pallas_call(
        last_faces_body,
        out_shape=(field, field, vmem(4 * ny + 8, nz), vmem(ny, LANES)),
        in_specs=[VMEM] * 6,
        out_specs=(VMEM,) * 4,
        input_output_aliases={0: 0, 1: 1},
        compiler_params=pltpu.CompilerParams(vmem_limit_bytes=32 * MIB),
        cost_estimate=pl.CostEstimate(flops=500000, bytes_accessed=500000, transcendentals=0),
        name="last_faces",
    )(hf, ha, yr, along_x, layer, top)


def packed_lane(r, c, x, nx):
    return (r * 2 + c) * nx + x


def pack_layer(fields, nx, ny, z):
    lane = lane_ids(ny)
    total = jnp.zeros((ny, LANES), jnp.float32)
    for r, f in enumerate(fields):
        for c in range(2):
            for x in range(nx):
                to = packed_lane(r, c, x, nx)
                total = jnp.where(lane == to, move(f[c, x], z, to), total)
    return total


def from_layer_above(tile, nx):
    first = lax.rem(lane_ids(tile.shape[0]) // nx, 2) == 0
    return COURANT * jnp.where(first, pltpu.roll(tile, LANES - nx, 1), -pltpu.roll(tile, nx, 1))


def pack_open(planes, z):
    ny = planes[0].shape[0]
    lane_8 = lane_ids(8)
    first = jnp.where(lane_ids(ny) == 0, move(planes[0], z, 0), 0.0)
    top = first[0:8, :]
    for x in range(1, len(planes)):
        top = jnp.where(lane_8 == x, move(planes[x], z, x), top)
    return jnp.concatenate([top, first[8:, :]], axis=0)


def update_coefficient(m):
    return jnp.where(
        m == 0,
        COURANT / PERMITTIVITIES[0],
        jnp.where(
            m == 1,
            COURANT / PERMITTIVITIES[1],
            jnp.where(m == 2, COURANT / PERMITTIVITIES[2], COURANT / PERMITTIVITIES[3]),
        ),
    )


def slab_start(nz, half):
    return (1 - lax.axis_index("gz")) * (nz - half)


def spectra_body(half, nz, dfv, dav, freq, material, after, out, still):
    freqs, nx, ny = dfv.shape[0], dfv.shape[3], dfv.shape[4]
    phase = freq[...] * float(STEP)
    cos, sin = jnp.cos(phase), jnp.sin(phase)
    cs = [jnp.broadcast_to(cos[:, f : f + 1], (ny, half)) for f in range(freqs)]
    sn = [jnp.broadcast_to(sin[:, f : f + 1], (ny, half)) for f in range(freqs)]
    shift = slab_start(nz, half)
    blank = jnp.zeros((ny, LANES - half), jnp.float32)

    def place(a):
        return pltpu.roll(jnp.concatenate([a, blank], axis=1), shift, 1)

    for x in range(nx):
        base = jnp.zeros((ny, half), jnp.float32)
        for c in range(3):
            with_forward = jnp.zeros((ny, half), jnp.float32)
            with_adjoint = jnp.zeros((ny, half), jnp.float32)
            for f in range(freqs):
                rf, jf, ra, ja = dfv[f, 0, c, x], dfv[f, 1, c, x], dav[f, 0, c, x], dav[f, 1, c, x]
                base = base + (rf * ra - jf * ja)
                with_forward = with_forward + (cs[f] * ra + sn[f] * ja)
                with_adjoint = with_adjoint + (cs[f] * rf + sn[f] * jf)
            out[1 + c, x] = place(with_forward)
            out[4 + c, x] = place(with_adjoint)
        out[0, x] = place(base)

    def cells(planes):
        return pack_open([planes(x, slice(0, 8 if x else ny)) for x in range(nx)], nz - 1)

    still[0] = cells(lambda x, rows: out[3, x, rows])
    still[1] = cells(lambda x, rows: out[6, x, rows])
    still[2] = cells(lambda x, rows: update_coefficient(material[x, rows]))


def spectra(df, da, freq, material, after, nz):
    _, _, _, nx, ny, half = df.shape
    return call(
        functools.partial(spectra_body, half, nz),
        "spectra",
        (vmem(7, nx, ny, LANES), vmem(3, ny, LANES)),
        (VMEM,) * 2,
        [VMEM] * 4 + [ANY],
        nbytes=11000000,
    )(df, da, freq, material, after)


def complete_body(hf, ha, zr, layer, hfn, han, below):
    _, nx, ny, nz = hf.shape
    lower = lax.axis_index("gz") == 0
    came = zr[...]
    above = jnp.where(lower, from_layer_above(came, nx), 0.0)
    below[...] = jnp.where(lower, 0.0, came + from_layer_above(layer[...], nx))
    top = lane_ids(ny) == nz - 1
    for r, (h, hn) in enumerate(((hf, hfn), (ha, han))):
        for c in range(2):
            for x in range(nx):
                hn[c, x] = h[c, x] + jnp.where(top, move(above, packed_lane(r, c, x, nx), nz - 1), 0.0)


def complete(hf, ha, zr, layer):
    _, nx, ny, nz = hf.shape
    part = vmem(2, nx, ny, nz)
    return call(
        complete_body,
        "complete",
        (part, part, vmem(ny, LANES)),
        (VMEM,) * 3,
        [VMEM] * 4,
        nbytes=2000000,
    )(hf, ha, zr, layer)


def electric_body(
    half, owned, ef, ea, hf, ha, hzf, hza, material, xr, yr, zr, first_y, spec, still, freq, layer_map, efn, ean, own, other, tile
):
    runs = ((ef, hf, hzf, efn), (ea, ha, hza, ean))
    _, nx, ny, nz = ef.shape
    phase = freq[...] * float(STEP)
    cos, sin = jnp.cos(phase), jnp.sin(phase)
    both = jnp.sum(cos * cos - sin * sin, axis=1, keepdims=True)
    gz = lax.axis_index("gz")
    lower = gz == 0
    start = slab_start(nz, half)
    slab = layer_map.shape[1]
    cells = jnp.concatenate([layer_map[...], jnp.full((1, LANES - slab), -1, jnp.int32)], axis=1)
    cells = pltpu.roll(jnp.broadcast_to(cells, (8, LANES)), lax.rem(start + LANES - gz * half, LANES), 1)
    lane, row = lane_ids(2 * owned), row_ids(2 * owned)
    inside = (lane >= start) & (lane < start + half)
    cells = jnp.broadcast_to(cells[0:1, :], (2 * owned, LANES))
    ids = lax.rem(row + gz * owned, 2 * owned)
    hot = jnp.where(inside & (cells == ids), 1.0, 0.0).astype(jnp.bfloat16)
    owner = jnp.broadcast_to(layer_map[...], (2 * owned, slab)) == ids[:, :slab]
    share = 1.0 / (3.0 * jnp.sum(jnp.where(owner, 1.0, 0.0), axis=1, keepdims=True))
    middle = jnp.broadcast_to(layer_map[0:1, half - 1 : half], (2 * owned, 1)) == ids[:, 0:1]
    middle_share = jnp.sum(jnp.where(middle, share, 0.0), axis=0, keepdims=True)
    below = zr[...]
    hx_below = [yr[2 * r * nx : (2 * r + 1) * nx, :] - COURANT * first_y[r, 1] for r in range(2)]
    hz_below = [yr[(2 * r + 1) * nx : (2 * r + 2) * nx, :] + COURANT * first_y[r, 0] for r in range(2)]
    dims = (((1,), (1,)), ((), ()))
    group = LANES // ny
    products = []
    for x in range(nx):
        coefficient = update_coefficient(material[x])
        news = []
        for r, (e, h, hz, en) in enumerate(runs):
            at_x, at_y = packed_lane(r, 0, x, nx), packed_lane(r, 1, x, nx)
            hx, hy, hz_here = h[0, x], h[1, x], hz[2, x]
            hy_x, hz_x = (h[1, x - 1], hz[2, x - 1]) if x else (xr[2 * r * ny : (2 * r + 1) * ny, :], xr[(2 * r + 1) * ny : (2 * r + 2) * ny, :])
            hx_y = down_y(hx, hx_below[r][x : x + 1, :])
            hz_y = down_y(hz_here, hz_below[r][x : x + 1, :])
            hx_z = down_z(hx, below, at_x)
            hy_z = down_z(hy, below, at_y)
            ex = e[0, x] + coefficient * ((hz_here - hz_y) - (hy - hy_z))
            ey = e[1, x] + coefficient * ((hx - hx_z) - (hz_here - hz_x))
            ez = e[2, x] + coefficient * ((hy - hy_x) - (hx - hx_y))
            en[0, x] = ex
            en[1, x] = ey
            en[2, x] = ez
            news.append((ex, ey, ez))
        total = spec[0, x]
        for c in range(3):
            f, a = news[0][c], news[1][c]
            total = total + (f * (spec[1 + c, x] + both * a) + a * spec[4 + c, x])
        products.append(total)
        if len(products) == group:
            block = jnp.concatenate(products, axis=0)
            products = []
            sums = jnp.zeros((2 * owned, group * ny), jnp.float32)
            for _ in range(3):
                part = block.astype(jnp.bfloat16)
                block = block - part.astype(jnp.float32)
                sums = sums + lax.dot_general(hot, part, dims, preferred_element_type=jnp.float32)
            sums = sums * share
            where = pl.ds(x // group * owned, owned)
            own[where, :] = sums[:owned]
            other[where, :] = sums[owned:]
    f, a = (pack_open([e[2, x, 0 : 8 if x else ny, :] for x in range(nx)], nz - 1) for e in (efn, ean))
    ratio = COURANT * still[2]
    scaled = ratio * middle_share
    rest = scaled * (still[0] + both * a)
    rest = rest + pltpu.roll(scaled * (still[1] + both * f), nx, 1)
    rest = rest + pltpu.roll(scaled * ratio * both, 2 * nx, 1)
    rest = rest + pltpu.roll(ratio, 3 * nx, 1)
    turned = jnp.concatenate([xr[4 * ny :, :], jnp.zeros((ny - 8, LANES), jnp.float32)], axis=0)
    turned = jnp.transpose(turned)[0:ny, :]
    turned = jnp.concatenate([turned, jnp.zeros((ny, LANES - ny), jnp.float32)], axis=1)
    lane = lane_ids(ny)
    along = jnp.where(lane == 0, turned, jnp.where(lane == nx, move(turned, 1, nx), 0.0))
    along = along + jnp.concatenate([yr[4 * nx : 4 * nx + 8, :], jnp.zeros((ny - 8, LANES), jnp.float32)], axis=0)
    rest = jnp.where(lower, rest, along)
    tile[...] = rest
    other[nx // group * owned :, :] = rest


def electric(ef, ea, hf, ha, hzf, hza, material, xr, yr, zr, first_y, spec, still, freq, layer_map, half, owned):
    _, nx, ny, nz = ef.shape
    field = vmem(3, nx, ny, nz)
    rows = nx * ny // LANES * owned
    return call(
        functools.partial(electric_body, half, owned),
        "electric",
        (field, field, vmem(rows, LANES), vmem(rows + ny, LANES), vmem(ny, LANES)),
        (VMEM,) * 5,
        [VMEM] * 15,
        nbytes=6700000,
    )(ef, ea, hf, ha, hzf, hza, material, xr, yr, zr, first_y, spec, still, freq, layer_map)


def store_body(ef, ea, hf, ha, hzf, hza, after, efn, ean, hfn, han, sems):
    copies = []
    for r, (e, h, hz, en, hn) in enumerate(((ef, hf, hzf, efn, hfn), (ea, ha, hza, ean, han))):
        for c in range(3):
            copies.append(pltpu.make_async_copy(e.at[c], en.at[c], sems.at[r, c]))
            copies.append(pltpu.make_async_copy((h if c < 2 else hz).at[c], hn.at[c], sems.at[r, 3 + c]))
    for copy in copies:
        copy.start()
    for copy in copies:
        copy.wait()


def store(ef, ea, hf, ha, hzf, hza, after):
    field = f32(*ef.shape)
    return call(
        store_body,
        "store",
        (field,) * 4,
        (ANY,) * 4,
        [VMEM] * 6 + [ANY],
        [pltpu.SemaphoreType.DMA((2, 6))],
        nbytes=3000000,
    )(ef, ea, hf, ha, hzf, hza, after)


def gradient_body(ef, ea, own, tile, came, layer_map, _f, _a, out, efn, ean, plane, rows, result, sems):
    owned, nx, ny = out.shape
    nz = ef.shape[3]
    half = layer_map.shape[1] // 2
    gz = lax.axis_index("gz")
    lower = gz == 0
    sums = own.shape[0]
    mine, theirs = tile[...], came[sums:, :]
    change, cells = jnp.where(lower, mine, theirs), jnp.where(lower, theirs, mine)
    cell = [cells, pltpu.roll(cells, LANES - nx, 1)]
    ratio = jnp.where(lower, pltpu.roll(change, LANES - 3 * nx, 1), 0.0)
    copies = []
    for r, (e, en) in enumerate(((ef, efn), (ea, ean))):
        add = ratio * cell[r]
        plane[r] = e[2, 0] + jnp.where(lane_ids(ny) == nz - 1, move(add, 0, nz - 1), 0.0)
        corner = (lane_ids(8) == nz - 1) & (row_ids(8) == 0)
        for x in range(1, nx):
            rows[r, x - 1] = e[2, x, 0:8, :] + jnp.where(corner, move(add[0:8, :], x, nz - 1), 0.0)
        copies.append(pltpu.make_async_copy(plane.at[r], en.at[2, 0], sems.at[r, 0]))
        copies.append(pltpu.make_async_copy(rows.at[r], en.at[2, 1:nx, 0:8], sems.at[r, 1]))
    for copy in copies:
        copy.start()
    by_a, by_both = pltpu.roll(change, LANES - nx, 1), pltpu.roll(change, LANES - 2 * nx, 1)
    missing = change * cell[0] + by_a * cell[1] + by_both * (cell[0] * cell[1])
    missing = jnp.transpose(missing)[0:nx, 0:ny]
    share = own[...] + came[0:sums, :]
    group = nx * owned // sums
    for x in range(nx):
        block = share[x // group * owned : (x // group + 1) * owned]
        at = x % group * ny
        result[:, x, :] = block[:, at : at + ny]
    middle = layer_map[0:1, half - 1 : half]
    for k in range(owned):
        mine = jnp.broadcast_to(middle == gz * owned + k, (nx, ny))
        result[k] = result[k] + jnp.where(mine, missing, 0.0)
    last = pltpu.make_async_copy(result, out, sems.at[0, 2])
    last.start()
    for copy in copies:
        copy.wait()
    last.wait()


def gradient(ef, ea, own, tile, came, layer_map, efn, ean, owned):
    _, nx, ny, nz = ef.shape
    return pl.pallas_call(
        gradient_body,
        out_shape=(f32(owned, nx, ny), f32(*efn.shape), f32(*ean.shape)),
        in_specs=[VMEM] * 6 + [ANY] * 2,
        out_specs=(ANY,) * 3,
        scratch_shapes=[
            pltpu.VMEM((2, ny, nz), jnp.float32),
            pltpu.VMEM((2, nx - 1, 8, nz), jnp.float32),
            pltpu.VMEM((owned, nx, ny), jnp.float32),
            pltpu.SemaphoreType.DMA((2, 3)),
        ],
        input_output_aliases={6: 1, 7: 2},
        compiler_params=pltpu.CompilerParams(vmem_limit_bytes=32 * MIB),
        cost_estimate=pl.CostEstimate(flops=100000, bytes_accessed=400000, transcendentals=0),
        name="gradient",
    )(ef, ea, own, tile, came, layer_map, efn, ean)


def shards(ef, hf, ea, ha, material, df, da, angular_freq, layer_map):
    _, nx, ny, nz = ef.shape
    half = df.shape[3]
    owned = LAYERS // lax.axis_size("gz")
    freq = angular_freq.reshape(1, -1)
    layer_map = layer_map.reshape(1, -1)
    df = jnp.transpose(df, (0, 1, 2, 4, 5, 3))
    da = jnp.transpose(da, (0, 1, 2, 4, 5, 3))
    xs, first_y, ef, ea, hf, ha, along_x, along_y = first_faces(ef, ea, hf, ha)
    yr = ring(first_y, "gy", -1)
    xr = ring(xs, "gx", -1)
    ys = last_y(ef, ea, hf, ha, xr, along_y)
    hf, ha, layer, top = magnetic(ef, ea, hf, ha, xr, ys)
    hf, ha, xs, zs = last_faces(hf, ha, yr, along_x, layer, top)
    yr = ring(ys, "gy", 1)
    xr = ring(xs, "gx", 1)
    zr = ring(zs, "gz", 1)
    spec, still = spectra(df, da, freq, material, zs, nz)
    hxyf, hxya, below = complete(hf, ha, zr, layer)
    ef, ea, own, other, tile = electric(
        ef, ea, hxyf, hxya, hf, ha, material, xr, yr, below, first_y, spec, still, freq, layer_map, half, owned
    )
    came = ring(other, "gz", 1)
    efn, ean, hfn, han = store(ef, ea, hxyf, hxya, hf, ha, own)
    out, efn, ean = gradient(ef, ea, own, tile, came, layer_map, efn, ean, owned)
    return efn, hfn, ean, han, out


def solution(mesh):
    field = P(None, "gx", "gy", "gz")
    dft = P(None, None, None, "gz", "gx", "gy")
    return jax.shard_map(
        shards,
        mesh=mesh,
        in_specs=(field, field, field, field, P("gx", "gy", "gz"), dft, dft, P(), P()),
        out_specs=(field, field, field, field, P("gz", "gx", "gy")),
        check_vma=False,
    )
```

```python
import functools

import jax
import jax.numpy as jnp
from jax import lax
from jax.experimental import pallas as pl
from jax.experimental.pallas import tpu as pltpu
from jax.sharding import PartitionSpec as P

LAYERS = 16
STEP = 40
PERMITTIVITIES = (1.0, 2.1, 4.0, 12.0)
COURANT = 0.5
LANES = 128
MIB = 1024 * 1024
ANY = pl.BlockSpec(memory_space=pl.ANY)
VMEM = pl.BlockSpec(memory_space=pltpu.VMEM)


def f32(*shape):
    return jax.ShapeDtypeStruct(shape, jnp.float32)


def vmem(*shape):
    return pltpu.VMEM(shape, jnp.float32)


def hbm(x):
    return pltpu.with_memory_space_constraint(x, pltpu.HBM)


def ring(x, axis, by):
    peers = lax.axis_size(axis)
    return lax.ppermute(x, axis, [(i, (i + by) % peers) for i in range(peers)])


def call(body, name, outs, out_specs, in_specs, scratch=(), nbytes=100000, limit=32):
    return pl.pallas_call(
        body,
        out_shape=outs,
        in_specs=in_specs,
        out_specs=out_specs,
        scratch_shapes=list(scratch),
        compiler_params=pltpu.CompilerParams(vmem_limit_bytes=limit * MIB),
        cost_estimate=pl.CostEstimate(flops=nbytes, bytes_accessed=nbytes, transcendentals=0),
        name=name,
    )


def lane_ids(rows):
    return lax.broadcasted_iota(jnp.int32, (rows, LANES), 1)


def row_ids(rows):
    return lax.broadcasted_iota(jnp.int32, (rows, LANES), 0)


def move(a, source, target):
    shift = (target - source) % LANES
    return pltpu.roll(a, shift, 1) if shift else a


def up_y(a):
    n = a.shape[0]
    return jnp.where(row_ids(n) == n - 1, 0.0, pltpu.roll(a, n - 1, 0))


def down_y(a, row):
    return jnp.where(row_ids(a.shape[0]) == 0, jnp.broadcast_to(row, a.shape), pltpu.roll(a, 1, 0))


def up_z(a):
    n = a.shape[1]
    return jnp.where(lane_ids(a.shape[0]) == n - 1, 0.0, pltpu.roll(a, n - 1, 1))


def down_z(a, packed, lane):
    return jnp.where(lane_ids(a.shape[0]) == 0, move(packed, lane, 0), pltpu.roll(a, 1, 1))


def first_faces_body(ef, ea, hf, ha, xs, ys, evf, eva, hvf, hva, along_x, along_y, sems):
    fields = (evf, eva)
    _, nx, ny, _ = ef.shape
    copies = {}
    for k, (pair, held) in enumerate((((ef, ea), (evf, eva)), ((hf, ha), (hvf, hva)))):
        for c in range(3):
            for r in range(2):
                copies[k, c, r] = pltpu.make_async_copy(pair[r].at[c], held[r].at[c], sems.at[k, r, c])
                copies[k, c, r].start()
    for c in range(3):
        for r, v in enumerate(fields):
            copies[0, c, r].wait()
            if c != 1:
                for x in range(nx):
                    ys[r, c // 2, x : x + 1, :] = v[c, x, 0:1, :]
            if c:
                xs[r, c - 1] = v[c, 0]
    lane, lane_8 = lane_ids(ny), lane_ids(8)
    by_x = jnp.zeros((ny, LANES), jnp.float32)
    by_y = jnp.zeros((8, LANES), jnp.float32)
    for r, e in enumerate(fields):
        by_x = jnp.where(lane == r, move(e[0, nx - 1], 0, r), by_x)
        for x in range(nx):
            by_y = jnp.where(lane_8 == r * nx + x, move(e[1, x, ny - 8 : ny, :], 0, r * nx + x), by_y)
    turned = jnp.transpose(by_x)[0:8, :]
    along_x[...] = jnp.concatenate([turned, jnp.zeros((8, LANES - ny), jnp.float32)], axis=1)
    along_y[...] = jnp.where(row_ids(8) == 0, pltpu.roll(by_y, 1, 0), 0.0)
    for c in range(3):
        for r in range(2):
            copies[1, c, r].wait()


def first_faces(ef, ea, hf, ha):
    _, nx, ny, nz = ef.shape
    field = vmem(3, nx, ny, nz)
    return call(
        first_faces_body,
        "first_faces",
        (vmem(2, 2, ny, nz), vmem(2, 2, nx, nz)) + (field,) * 4 + (vmem(8, LANES), vmem(8, LANES)),
        (VMEM,) * 8,
        [ANY] * 4,
        [pltpu.SemaphoreType.DMA((2, 2, 3))],
        nbytes=3000000,
    )(hbm(ef), hbm(ea), hbm(hf), hbm(ha))


def magnetic_update(e, h, x, rows, next_x, r):
    nx = e.shape[1]
    ex, ey, ez = e[0, x, rows], e[1, x, rows], e[2, x, rows]
    ey_x, ez_x = (e[1, x + 1, rows], e[2, x + 1, rows]) if x + 1 < nx else (next_x[r, 0, rows], next_x[r, 1, rows])
    ex_y = up_y(ex)
    ez_y = up_y(ez)
    ex_z = up_z(ex)
    ey_z = up_z(ey)
    hx = h[0, x, rows] - COURANT * ((ez_y - ez) - (ey_z - ey))
    hy = h[1, x, rows] - COURANT * ((ex_z - ex) - (ez_x - ez))
    hz = h[2, x, rows] - COURANT * ((ey_x - ey) - (ex_y - ex))
    return hx, hy, hz


def last_y_body(ef, ea, hf, ha, xr, along_y, ys):
    _, nx, ny, _ = ef.shape
    last = slice(ny - 8, ny)
    for r, (e, h) in enumerate(((ef, hf), (ea, ha))):
        for x in range(nx):
            hx, _, hz = magnetic_update(e, h, x, last, xr, r)
            for c, a in enumerate((hx, hz)):
                at = packed_lane(r, c, x, nx)
                ys[at : at + 1, :] = a[7:8, :]
    ys[4 * nx : 4 * nx + 8, :] = along_y[...]
    ys[4 * nx + 8 :, :] = jnp.zeros((ys.shape[0] - 4 * nx - 8, ys.shape[1]), jnp.float32)


def last_y(ef, ea, hf, ha, xr, along_y):
    _, nx, ny, nz = ef.shape
    return call(
        last_y_body,
        "last_y",
        vmem(max(4 * nx, 4 * ny + 8) + 8, nz),
        VMEM,
        [VMEM] * 6,
        nbytes=500000,
    )(ef, ea, hf, ha, xr, along_y)


def magnetic_body(ef, ea, hf, ha, xr, after, hfn, han, layer, top):
    _, nx, ny, nz = ef.shape
    for x in range(nx):
        for r, (e, h, hn) in enumerate(((ef, hf, hfn), (ea, ha, han))):
            hn[0, x], hn[1, x], hn[2, x] = magnetic_update(e, h, x, slice(0, ny), xr, r)
    layer[...] = pack_layer((ef, ea), nx, ny, 0)
    top[...] = pack_layer((hfn, han), nx, ny, nz - 1)


def magnetic(ef, ea, hf, ha, xr, after):
    _, nx, ny, nz = ef.shape
    field = vmem(3, nx, ny, nz)
    return call(
        magnetic_body,
        "magnetic",
        (field, field, vmem(ny, LANES), vmem(ny, LANES)),
        (VMEM,) * 4,
        [VMEM] * 5 + [ANY],
        nbytes=4800000,
    )(ef, ea, hf, ha, xr, after)


def last_faces_body(hf, ha, yr, along_x, layer, top, hfn, han, xs, zs):
    _, nx, ny, nz = hf.shape
    last = slice(ny - 8, ny)
    edge, lane = row_ids(8) == 7, lane_ids(8)
    rows = top[last, :]
    for r, (h, hn) in enumerate(((hf, hfn), (ha, han))):
        for x in range(nx):
            hx = h[0, x, last, :] - COURANT * jnp.where(edge, jnp.broadcast_to(yr[r, 1, x : x + 1, :], (8, nz)), 0.0)
            hz = h[2, x, last, :] + COURANT * jnp.where(edge, jnp.broadcast_to(yr[r, 0, x : x + 1, :], (8, nz)), 0.0)
            hn[0, x, last, :] = hx
            hn[2, x, last, :] = hz
            to = packed_lane(r, 0, x, nx)
            rows = jnp.where(lane == to, move(hx, nz - 1, to), rows)
        at = r * 2 * ny
        xs[at : at + ny, :] = h[1, nx - 1]
        xs[at + ny : at + 2 * ny - 8, :] = h[2, nx - 1, 0 : ny - 8, :]
        xs[at + 2 * ny - 8 : at + 2 * ny, :] = hz
    xs[4 * ny :, :] = along_x[...]
    lower = lax.axis_index("gz") == 0
    zs[...] = jnp.where(lower, top[...], layer[...])
    zs[last, :] = jnp.where(lower, rows, layer[last, :])


def last_faces(hf, ha, yr, along_x, layer, top):
    _, nx, ny, nz = hf.shape
    field = vmem(3, nx, ny, nz)
    return pl.pallas_call(
        last_faces_body,
        out_shape=(field, field, vmem(4 * ny + 8, nz), vmem(ny, LANES)),
        in_specs=[VMEM] * 6,
        out_specs=(VMEM,) * 4,
        input_output_aliases={0: 0, 1: 1},
        compiler_params=pltpu.CompilerParams(vmem_limit_bytes=32 * MIB),
        cost_estimate=pl.CostEstimate(flops=500000, bytes_accessed=500000, transcendentals=0),
        name="last_faces",
    )(hf, ha, yr, along_x, layer, top)


def packed_lane(r, c, x, nx):
    return (r * 2 + c) * nx + x


def pack_layer(fields, nx, ny, z):
    lane = lane_ids(ny)
    total = jnp.zeros((ny, LANES), jnp.float32)
    for r, f in enumerate(fields):
        for c in range(2):
            for x in range(nx):
                to = packed_lane(r, c, x, nx)
                total = jnp.where(lane == to, move(f[c, x], z, to), total)
    return total


def from_layer_above(tile, nx):
    first = lax.rem(lane_ids(tile.shape[0]) // nx, 2) == 0
    return COURANT * jnp.where(first, pltpu.roll(tile, LANES - nx, 1), -pltpu.roll(tile, nx, 1))


def pack_open(planes, z):
    ny = planes[0].shape[0]
    lane_8 = lane_ids(8)
    first = jnp.where(lane_ids(ny) == 0, move(planes[0], z, 0), 0.0)
    top = first[0:8, :]
    for x in range(1, len(planes)):
        top = jnp.where(lane_8 == x, move(planes[x], z, x), top)
    return jnp.concatenate([top, first[8:, :]], axis=0)


def update_coefficient(m):
    return jnp.where(
        m == 0,
        COURANT / PERMITTIVITIES[0],
        jnp.where(
            m == 1,
            COURANT / PERMITTIVITIES[1],
            jnp.where(m == 2, COURANT / PERMITTIVITIES[2], COURANT / PERMITTIVITIES[3]),
        ),
    )


def fold_cells(tile, nx):
    lane = lane_ids(8)
    folded = jnp.where(lane < 4 * nx, tile[0:8, :], 0.0)
    for g in range(1, tile.shape[0] // 8):
        here = (lane >= 4 * nx) & (lax.rem(lane, nx) == g)
        folded = jnp.where(here, pltpu.roll(tile[8 * g : 8 * g + 8, :], 4 * nx + g, 1), folded)
    return folded


def unfold_cells(folded, rows, nx):
    lane = lane_ids(8)
    groups = [jnp.where(lane < 4 * nx, folded, 0.0)]
    for g in range(1, rows // 8):
        here = (lane < 4 * nx) & (lax.rem(lane, nx) == 0)
        groups.append(jnp.where(here, pltpu.roll(folded, LANES - 4 * nx - g, 1), 0.0))
    return jnp.concatenate(groups, axis=0)


def slab_start(nz, half):
    return (1 - lax.axis_index("gz")) * (nz - half)


def spectra_body(half, nz, dfv, dav, freq, material, after, out, still):
    freqs, nx, ny = dfv.shape[0], dfv.shape[3], dfv.shape[4]
    phase = freq[...] * float(STEP)
    cos, sin = jnp.cos(phase), jnp.sin(phase)
    cs = [jnp.broadcast_to(cos[:, f : f + 1], (ny, half)) for f in range(freqs)]
    sn = [jnp.broadcast_to(sin[:, f : f + 1], (ny, half)) for f in range(freqs)]
    shift = slab_start(nz, half)
    blank = jnp.zeros((ny, LANES - half), jnp.float32)

    def place(a):
        return pltpu.roll(jnp.concatenate([a, blank], axis=1), shift, 1)

    for x in range(nx):
        base = jnp.zeros((ny, half), jnp.float32)
        for c in range(3):
            with_forward = jnp.zeros((ny, half), jnp.float32)
            with_adjoint = jnp.zeros((ny, half), jnp.float32)
            for f in range(freqs):
                rf, jf, ra, ja = dfv[f, 0, c, x], dfv[f, 1, c, x], dav[f, 0, c, x], dav[f, 1, c, x]
                base = base + (rf * ra - jf * ja)
                with_forward = with_forward + (cs[f] * ra + sn[f] * ja)
                with_adjoint = with_adjoint + (cs[f] * rf + sn[f] * jf)
            out[1 + c, x] = place(with_forward)
            out[4 + c, x] = place(with_adjoint)
        out[0, x] = place(base)

    def cells(planes):
        return pack_open([planes(x, slice(0, 8 if x else ny)) for x in range(nx)], nz - 1)

    still[0] = cells(lambda x, rows: out[3, x, rows])
    still[1] = cells(lambda x, rows: out[6, x, rows])
    still[2] = cells(lambda x, rows: update_coefficient(material[x, rows]))


def spectra(df, da, freq, material, after, nz):
    _, _, _, nx, ny, half = df.shape
    return call(
        functools.partial(spectra_body, half, nz),
        "spectra",
        (vmem(7, nx, ny, LANES), vmem(3, ny, LANES)),
        (VMEM,) * 2,
        [VMEM] * 4 + [ANY],
        nbytes=11000000,
    )(df, da, freq, material, after)


def complete_body(hf, ha, zr, layer, hfn, han, below):
    _, nx, ny, nz = hf.shape
    lower = lax.axis_index("gz") == 0
    came = zr[...]
    above = jnp.where(lower, from_layer_above(came, nx), 0.0)
    below[...] = jnp.where(lower, 0.0, came + from_layer_above(layer[...], nx))
    top = lane_ids(ny) == nz - 1
    for r, (h, hn) in enumerate(((hf, hfn), (ha, han))):
        for c in range(2):
            for x in range(nx):
                hn[c, x] = h[c, x] + jnp.where(top, move(above, packed_lane(r, c, x, nx), nz - 1), 0.0)


def complete(hf, ha, zr, layer):
    _, nx, ny, nz = hf.shape
    part = vmem(2, nx, ny, nz)
    return call(
        complete_body,
        "complete",
        (part, part, vmem(ny, LANES)),
        (VMEM,) * 3,
        [VMEM] * 4,
        nbytes=2000000,
    )(hf, ha, zr, layer)


def electric_body(
    half, owned, ef, ea, hf, ha, hzf, hza, material, xr, yr, zr, first_y, spec, still, freq, layer_map, efn, ean, own, other, tile
):
    runs = ((ef, hf, hzf, efn), (ea, ha, hza, ean))
    _, nx, ny, nz = ef.shape
    phase = freq[...] * float(STEP)
    cos, sin = jnp.cos(phase), jnp.sin(phase)
    both = jnp.sum(cos * cos - sin * sin, axis=1, keepdims=True)
    gz = lax.axis_index("gz")
    lower = gz == 0
    start = slab_start(nz, half)
    slab = layer_map.shape[1]
    cells = jnp.concatenate([layer_map[...], jnp.full((1, LANES - slab), -1, jnp.int32)], axis=1)
    cells = pltpu.roll(jnp.broadcast_to(cells, (8, LANES)), lax.rem(start + LANES - gz * half, LANES), 1)
    lane, row = lane_ids(2 * owned), row_ids(2 * owned)
    inside = (lane >= start) & (lane < start + half)
    cells = jnp.broadcast_to(cells[0:1, :], (2 * owned, LANES))
    ids = lax.rem(row + gz * owned, 2 * owned)
    hot = jnp.where(inside & (cells == ids), 1.0, 0.0).astype(jnp.bfloat16)
    owner = jnp.broadcast_to(layer_map[...], (2 * owned, slab)) == ids[:, :slab]
    share = 1.0 / (3.0 * jnp.sum(jnp.where(owner, 1.0, 0.0), axis=1, keepdims=True))
    middle = jnp.broadcast_to(layer_map[0:1, half - 1 : half], (2 * owned, 1)) == ids[:, 0:1]
    middle_share = jnp.sum(jnp.where(middle, share, 0.0), axis=0, keepdims=True)
    below = zr[...]
    hx_below = [yr[2 * r * nx : (2 * r + 1) * nx, :] - COURANT * first_y[r, 1] for r in range(2)]
    hz_below = [yr[(2 * r + 1) * nx : (2 * r + 2) * nx, :] + COURANT * first_y[r, 0] for r in range(2)]
    dims = (((1,), (1,)), ((), ()))
    group = LANES // ny
    products = []
    for x in range(nx):
        coefficient = update_coefficient(material[x])
        news = []
        for r, (e, h, hz, en) in enumerate(runs):
            at_x, at_y = packed_lane(r, 0, x, nx), packed_lane(r, 1, x, nx)
            hx, hy, hz_here = h[0, x], h[1, x], hz[2, x]
            hy_x, hz_x = (h[1, x - 1], hz[2, x - 1]) if x else (xr[2 * r * ny : (2 * r + 1) * ny, :], xr[(2 * r + 1) * ny : (2 * r + 2) * ny, :])
            hx_y = down_y(hx, hx_below[r][x : x + 1, :])
            hz_y = down_y(hz_here, hz_below[r][x : x + 1, :])
            hx_z = down_z(hx, below, at_x)
            hy_z = down_z(hy, below, at_y)
            ex = e[0, x] + coefficient * ((hz_here - hz_y) - (hy - hy_z))
            ey = e[1, x] + coefficient * ((hx - hx_z) - (hz_here - hz_x))
            ez = e[2, x] + coefficient * ((hy - hy_x) - (hx - hx_y))
            en[0, x] = ex
            en[1, x] = ey
            en[2, x] = ez
            news.append((ex, ey, ez))
        total = spec[0, x]
        for c in range(3):
            f, a = news[0][c], news[1][c]
            total = total + (f * (spec[1 + c, x] + both * a) + a * spec[4 + c, x])
        products.append(total)
        if len(products) == group:
            block = jnp.concatenate(products, axis=0)
            products = []
            sums = jnp.zeros((2 * owned, group * ny), jnp.float32)
            for _ in range(3):
                part = block.astype(jnp.bfloat16)
                block = block - part.astype(jnp.float32)
                sums = sums + lax.dot_general(hot, part, dims, preferred_element_type=jnp.float32)
            sums = sums * share
            where = pl.ds(x // group * owned, owned)
            own[where, :] = sums[:owned]
            other[where, :] = sums[owned:]
    f, a = (pack_open([e[2, x, 0 : 8 if x else ny, :] for x in range(nx)], nz - 1) for e in (efn, ean))
    ratio = COURANT * still[2]
    scaled = ratio * middle_share
    rest = scaled * (still[0] + both * a)
    rest = rest + pltpu.roll(scaled * (still[1] + both * f), nx, 1)
    rest = rest + pltpu.roll(scaled * ratio * both, 2 * nx, 1)
    rest = rest + pltpu.roll(ratio, 3 * nx, 1)
    turned = jnp.concatenate([xr[4 * ny :, :], jnp.zeros((ny - 8, LANES), jnp.float32)], axis=0)
    turned = jnp.transpose(turned)[0:ny, :]
    turned = jnp.concatenate([turned, jnp.zeros((ny, LANES - ny), jnp.float32)], axis=1)
    lane = lane_ids(ny)
    along = jnp.where(lane == 0, turned, jnp.where(lane == nx, move(turned, 1, nx), 0.0))
    along = along + jnp.concatenate([yr[4 * nx : 4 * nx + 8, :], jnp.zeros((ny - 8, LANES), jnp.float32)], axis=0)
    rest = jnp.where(lower, rest, along)
    tile[...] = rest
    other[nx // group * owned :, :] = fold_cells(rest, nx)


def electric(ef, ea, hf, ha, hzf, hza, material, xr, yr, zr, first_y, spec, still, freq, layer_map, half, owned):
    _, nx, ny, nz = ef.shape
    field = vmem(3, nx, ny, nz)
    rows = nx * ny // LANES * owned
    return call(
        functools.partial(electric_body, half, owned),
        "electric",
        (field, field, vmem(rows, LANES), vmem(rows + 8, LANES), vmem(ny, LANES)),
        (VMEM,) * 5,
        [VMEM] * 15,
        nbytes=6700000,
    )(ef, ea, hf, ha, hzf, hza, material, xr, yr, zr, first_y, spec, still, freq, layer_map)


def store_body(ef, ea, hf, ha, hzf, hza, after, efn, ean, hfn, han, sems):
    copies = []
    for r, (e, h, hz, en, hn) in enumerate(((ef, hf, hzf, efn, hfn), (ea, ha, hza, ean, han))):
        for c in range(3):
            copies.append(pltpu.make_async_copy(e.at[c], en.at[c], sems.at[r, c]))
            copies.append(pltpu.make_async_copy((h if c < 2 else hz).at[c], hn.at[c], sems.at[r, 3 + c]))
    for copy in copies:
        copy.start()
    for copy in copies:
        copy.wait()


def store(ef, ea, hf, ha, hzf, hza, after):
    field = f32(*ef.shape)
    return call(
        store_body,
        "store",
        (field,) * 4,
        (ANY,) * 4,
        [VMEM] * 6 + [ANY],
        [pltpu.SemaphoreType.DMA((2, 6))],
        nbytes=3000000,
    )(ef, ea, hf, ha, hzf, hza, after)


def gradient_body(ef, ea, own, tile, came, layer_map, _f, _a, out, efn, ean, plane, rows, result, sems):
    owned, nx, ny = out.shape
    nz = ef.shape[3]
    half = layer_map.shape[1] // 2
    gz = lax.axis_index("gz")
    lower = gz == 0
    sums = own.shape[0]
    mine, theirs = tile[...], unfold_cells(came[sums:, :], tile.shape[0], nx)
    change, cells = jnp.where(lower, mine, theirs), jnp.where(lower, theirs, mine)
    cell = [cells, pltpu.roll(cells, LANES - nx, 1)]
    ratio = jnp.where(lower, pltpu.roll(change, LANES - 3 * nx, 1), 0.0)
    copies = []
    for r, (e, en) in enumerate(((ef, efn), (ea, ean))):
        add = ratio * cell[r]
        plane[r] = e[2, 0] + jnp.where(lane_ids(ny) == nz - 1, move(add, 0, nz - 1), 0.0)
        corner = (lane_ids(8) == nz - 1) & (row_ids(8) == 0)
        for x in range(1, nx):
            rows[r, x - 1] = e[2, x, 0:8, :] + jnp.where(corner, move(add[0:8, :], x, nz - 1), 0.0)
        copies.append(pltpu.make_async_copy(plane.at[r], en.at[2, 0], sems.at[r, 0]))
        copies.append(pltpu.make_async_copy(rows.at[r], en.at[2, 1:nx, 0:8], sems.at[r, 1]))
    for copy in copies:
        copy.start()
    by_a, by_both = pltpu.roll(change, LANES - nx, 1), pltpu.roll(change, LANES - 2 * nx, 1)
    missing = change * cell[0] + by_a * cell[1] + by_both * (cell[0] * cell[1])
    missing = jnp.transpose(missing)[0:nx, 0:ny]
    share = own[...] + came[0:sums, :]
    group = nx * owned // sums
    for x in range(nx):
        block = share[x // group * owned : (x // group + 1) * owned]
        at = x % group * ny
        result[:, x, :] = block[:, at : at + ny]
    middle = layer_map[0:1, half - 1 : half]
    for k in range(owned):
        mine = jnp.broadcast_to(middle == gz * owned + k, (nx, ny))
        result[k] = result[k] + jnp.where(mine, missing, 0.0)
    last = pltpu.make_async_copy(result, out, sems.at[0, 2])
    last.start()
    for copy in copies:
        copy.wait()
    last.wait()


def gradient(ef, ea, own, tile, came, layer_map, efn, ean, owned):
    _, nx, ny, nz = ef.shape
    return pl.pallas_call(
        gradient_body,
        out_shape=(f32(owned, nx, ny), f32(*efn.shape), f32(*ean.shape)),
        in_specs=[VMEM] * 6 + [ANY] * 2,
        out_specs=(ANY,) * 3,
        scratch_shapes=[
            pltpu.VMEM((2, ny, nz), jnp.float32),
            pltpu.VMEM((2, nx - 1, 8, nz), jnp.float32),
            pltpu.VMEM((owned, nx, ny), jnp.float32),
            pltpu.SemaphoreType.DMA((2, 3)),
        ],
        input_output_aliases={6: 1, 7: 2},
        compiler_params=pltpu.CompilerParams(vmem_limit_bytes=32 * MIB),
        cost_estimate=pl.CostEstimate(flops=100000, bytes_accessed=400000, transcendentals=0),
        name="gradient",
    )(ef, ea, own, tile, came, layer_map, efn, ean)


def shards(ef, hf, ea, ha, material, df, da, angular_freq, layer_map):
    _, nx, ny, nz = ef.shape
    half = df.shape[3]
    owned = LAYERS // lax.axis_size("gz")
    freq = angular_freq.reshape(1, -1)
    layer_map = layer_map.reshape(1, -1)
    df = jnp.transpose(df, (0, 1, 2, 4, 5, 3))
    da = jnp.transpose(da, (0, 1, 2, 4, 5, 3))
    xs, first_y, ef, ea, hf, ha, along_x, along_y = first_faces(ef, ea, hf, ha)
    yr = ring(first_y, "gy", -1)
    xr = ring(xs, "gx", -1)
    ys = last_y(ef, ea, hf, ha, xr, along_y)
    hf, ha, layer, top = magnetic(ef, ea, hf, ha, xr, ys)
    hf, ha, xs, zs = last_faces(hf, ha, yr, along_x, layer, top)
    yr = ring(ys, "gy", 1)
    xr = ring(xs, "gx", 1)
    zr = ring(zs, "gz", 1)
    spec, still = spectra(df, da, freq, material, zs, nz)
    hxyf, hxya, below = complete(hf, ha, zr, layer)
    ef, ea, own, other, tile = electric(
        ef, ea, hxyf, hxya, hf, ha, material, xr, yr, below, first_y, spec, still, freq, layer_map, half, owned
    )
    came = ring(other, "gz", 1)
    efn, ean, hfn, han = store(ef, ea, hxyf, hxya, hf, ha, own)
    out, efn, ean = gradient(ef, ea, own, tile, came, layer_map, efn, ean, owned)
    return efn, hfn, ean, han, out


def solution(mesh):
    field = P(None, "gx", "gy", "gz")
    dft = P(None, None, None, "gz", "gx", "gy")
    return jax.shard_map(
        shards,
        mesh=mesh,
        in_specs=(field, field, field, field, P("gx", "gy", "gz"), dft, dft, P(), P()),
        out_specs=(field, field, field, field, P("gz", "gx", "gy")),
        check_vma=False,
    )
```

```python
import functools

import jax
import jax.numpy as jnp
from jax import lax
from jax.experimental import pallas as pl
from jax.experimental.pallas import tpu as pltpu
from jax.sharding import PartitionSpec as P

LAYERS = 16
STEP = 40
PERMITTIVITIES = (1.0, 2.1, 4.0, 12.0)
COURANT = 0.5
LANES = 128
MIB = 1024 * 1024
ANY = pl.BlockSpec(memory_space=pl.ANY)
VMEM = pl.BlockSpec(memory_space=pltpu.VMEM)


def f32(*shape):
    return jax.ShapeDtypeStruct(shape, jnp.float32)


def vmem(*shape):
    return pltpu.VMEM(shape, jnp.float32)


def hbm(x):
    return pltpu.with_memory_space_constraint(x, pltpu.HBM)


def ring(x, axis, by):
    peers = lax.axis_size(axis)
    return lax.ppermute(x, axis, [(i, (i + by) % peers) for i in range(peers)])


def call(body, name, outs, out_specs, in_specs, scratch=(), nbytes=100000, limit=32):
    return pl.pallas_call(
        body,
        out_shape=outs,
        in_specs=in_specs,
        out_specs=out_specs,
        scratch_shapes=list(scratch),
        compiler_params=pltpu.CompilerParams(vmem_limit_bytes=limit * MIB),
        cost_estimate=pl.CostEstimate(flops=nbytes, bytes_accessed=nbytes, transcendentals=0),
        name=name,
    )


def lane_ids(rows):
    return lax.broadcasted_iota(jnp.int32, (rows, LANES), 1)


def row_ids(rows):
    return lax.broadcasted_iota(jnp.int32, (rows, LANES), 0)


def move(a, source, target):
    shift = (target - source) % LANES
    return pltpu.roll(a, shift, 1) if shift else a


def up_y(a):
    n = a.shape[0]
    return jnp.where(row_ids(n) == n - 1, 0.0, pltpu.roll(a, n - 1, 0))


def down_y(a, row):
    return jnp.where(row_ids(a.shape[0]) == 0, jnp.broadcast_to(row, a.shape), pltpu.roll(a, 1, 0))


def up_z(a):
    n = a.shape[1]
    return jnp.where(lane_ids(a.shape[0]) == n - 1, 0.0, pltpu.roll(a, n - 1, 1))


def down_z(a, packed, lane):
    return jnp.where(lane_ids(a.shape[0]) == 0, move(packed, lane, 0), pltpu.roll(a, 1, 1))


def first_faces_body(ef, ea, hf, ha, xs, ys, evf, eva, hvf, hva, along_x, along_y, sems):
    fields = (evf, eva)
    _, nx, ny, _ = ef.shape
    copies = {}
    for k, (pair, held) in enumerate((((ef, ea), (evf, eva)), ((hf, ha), (hvf, hva)))):
        for c in range(3):
            for r in range(2):
                copies[k, c, r] = pltpu.make_async_copy(pair[r].at[c], held[r].at[c], sems.at[k, r, c])
                copies[k, c, r].start()
    for c in range(3):
        for r, v in enumerate(fields):
            copies[0, c, r].wait()
            if c != 1:
                for x in range(nx):
                    ys[r, c // 2, x : x + 1, :] = v[c, x, 0:1, :]
            if c:
                xs[r, c - 1] = v[c, 0]
    lane, lane_8 = lane_ids(ny), lane_ids(8)
    by_x = jnp.zeros((ny, LANES), jnp.float32)
    by_y = jnp.zeros((8, LANES), jnp.float32)
    for r, e in enumerate(fields):
        by_x = jnp.where(lane == r, move(e[0, nx - 1], 0, r), by_x)
        for x in range(nx):
            by_y = jnp.where(lane_8 == r * nx + x, move(e[1, x, ny - 8 : ny, :], 0, r * nx + x), by_y)
    turned = jnp.transpose(by_x)[0:8, :]
    along_x[...] = jnp.concatenate([turned, jnp.zeros((8, LANES - ny), jnp.float32)], axis=1)
    along_y[...] = jnp.where(row_ids(8) == 0, pltpu.roll(by_y, 1, 0), 0.0)
    for c in range(3):
        for r in range(2):
            copies[1, c, r].wait()


def first_faces(ef, ea, hf, ha):
    _, nx, ny, nz = ef.shape
    field = vmem(3, nx, ny, nz)
    return call(
        first_faces_body,
        "first_faces",
        (vmem(2, 2, ny, nz), vmem(2, 2, nx, nz)) + (field,) * 4 + (vmem(8, LANES), vmem(8, LANES)),
        (VMEM,) * 8,
        [ANY] * 4,
        [pltpu.SemaphoreType.DMA((2, 2, 3))],
        nbytes=3000000,
    )(hbm(ef), hbm(ea), hbm(hf), hbm(ha))


def magnetic_update(e, h, x, rows, next_x, r):
    nx = e.shape[1]
    ex, ey, ez = e[0, x, rows], e[1, x, rows], e[2, x, rows]
    ey_x, ez_x = (e[1, x + 1, rows], e[2, x + 1, rows]) if x + 1 < nx else (next_x[r, 0, rows], next_x[r, 1, rows])
    ex_y = up_y(ex)
    ez_y = up_y(ez)
    ex_z = up_z(ex)
    ey_z = up_z(ey)
    hx = h[0, x, rows] - COURANT * ((ez_y - ez) - (ey_z - ey))
    hy = h[1, x, rows] - COURANT * ((ex_z - ex) - (ez_x - ez))
    hz = h[2, x, rows] - COURANT * ((ey_x - ey) - (ex_y - ex))
    return hx, hy, hz


def last_y_body(ef, ea, hf, ha, xr, along_y, ys):
    _, nx, ny, _ = ef.shape
    last = slice(ny - 8, ny)
    for r, (e, h) in enumerate(((ef, hf), (ea, ha))):
        for x in range(nx):
            hx, _, hz = magnetic_update(e, h, x, last, xr, r)
            for c, a in enumerate((hx, hz)):
                at = packed_lane(r, c, x, nx)
                ys[at : at + 1, :] = a[7:8, :]
    ys[4 * nx : 4 * nx + 8, :] = along_y[...]
    ys[4 * nx + 8 :, :] = jnp.zeros((ys.shape[0] - 4 * nx - 8, ys.shape[1]), jnp.float32)


def last_y(ef, ea, hf, ha, xr, along_y):
    _, nx, ny, nz = ef.shape
    return call(
        last_y_body,
        "last_y",
        vmem(max(4 * nx, 4 * ny + 8) + 8, nz),
        VMEM,
        [VMEM] * 6,
        nbytes=500000,
    )(ef, ea, hf, ha, xr, along_y)


def magnetic_body(ef, ea, hf, ha, xr, after, hfn, han, layer, top):
    _, nx, ny, nz = ef.shape
    for x in range(nx):
        for r, (e, h, hn) in enumerate(((ef, hf, hfn), (ea, ha, han))):
            hn[0, x], hn[1, x], hn[2, x] = magnetic_update(e, h, x, slice(0, ny), xr, r)
    layer[...] = pack_layer((ef, ea), nx, ny, 0)
    top[...] = pack_layer((hfn, han), nx, ny, nz - 1)


def magnetic(ef, ea, hf, ha, xr, after):
    _, nx, ny, nz = ef.shape
    field = vmem(3, nx, ny, nz)
    return call(
        magnetic_body,
        "magnetic",
        (field, field, vmem(ny, LANES), vmem(ny, LANES)),
        (VMEM,) * 4,
        [VMEM] * 5 + [ANY],
        nbytes=4800000,
    )(ef, ea, hf, ha, xr, after)


def last_faces_body(hf, ha, yr, along_x, layer, top, hfn, han, xs, zs):
    _, nx, ny, nz = hf.shape
    last = slice(ny - 8, ny)
    edge, lane = row_ids(8) == 7, lane_ids(8)
    rows = top[last, :]
    for r, (h, hn) in enumerate(((hf, hfn), (ha, han))):
        for x in range(nx):
            hx = h[0, x, last, :] - COURANT * jnp.where(edge, jnp.broadcast_to(yr[r, 1, x : x + 1, :], (8, nz)), 0.0)
            hz = h[2, x, last, :] + COURANT * jnp.where(edge, jnp.broadcast_to(yr[r, 0, x : x + 1, :], (8, nz)), 0.0)
            hn[0, x, last, :] = hx
            hn[2, x, last, :] = hz
            to = packed_lane(r, 0, x, nx)
            rows = jnp.where(lane == to, move(hx, nz - 1, to), rows)
        at = r * 2 * ny
        xs[at : at + ny, :] = h[1, nx - 1]
        xs[at + ny : at + 2 * ny - 8, :] = h[2, nx - 1, 0 : ny - 8, :]
        xs[at + 2 * ny - 8 : at + 2 * ny, :] = hz
    xs[4 * ny :, :] = along_x[...]
    lower = lax.axis_index("gz") == 0
    sent = jnp.where(lower, jnp.concatenate([top[0 : ny - 8, :], rows], axis=0), layer[...])
    zs[...] = sent[0 : ny // 2] + pltpu.roll(sent[ny // 2 :], 4 * nx, 1)


def last_faces(hf, ha, yr, along_x, layer, top):
    _, nx, ny, nz = hf.shape
    field = vmem(3, nx, ny, nz)
    return pl.pallas_call(
        last_faces_body,
        out_shape=(field, field, vmem(4 * ny + 8, nz), vmem(ny // 2, LANES)),
        in_specs=[VMEM] * 6,
        out_specs=(VMEM,) * 4,
        input_output_aliases={0: 0, 1: 1},
        compiler_params=pltpu.CompilerParams(vmem_limit_bytes=32 * MIB),
        cost_estimate=pl.CostEstimate(flops=500000, bytes_accessed=500000, transcendentals=0),
        name="last_faces",
    )(hf, ha, yr, along_x, layer, top)


def packed_lane(r, c, x, nx):
    return (r * 2 + c) * nx + x


def pack_layer(fields, nx, ny, z):
    lane = lane_ids(ny)
    total = jnp.zeros((ny, LANES), jnp.float32)
    for r, f in enumerate(fields):
        for c in range(2):
            for x in range(nx):
                to = packed_lane(r, c, x, nx)
                total = jnp.where(lane == to, move(f[c, x], z, to), total)
    return total


def from_layer_above(tile, nx):
    first = lax.rem(lane_ids(tile.shape[0]) // nx, 2) == 0
    return COURANT * jnp.where(first, pltpu.roll(tile, LANES - nx, 1), -pltpu.roll(tile, nx, 1))


def pack_open(planes, z):
    ny = planes[0].shape[0]
    lane_8 = lane_ids(8)
    first = jnp.where(lane_ids(ny) == 0, move(planes[0], z, 0), 0.0)
    top = first[0:8, :]
    for x in range(1, len(planes)):
        top = jnp.where(lane_8 == x, move(planes[x], z, x), top)
    return jnp.concatenate([top, first[8:, :]], axis=0)


def update_coefficient(m):
    return jnp.where(
        m == 0,
        COURANT / PERMITTIVITIES[0],
        jnp.where(
            m == 1,
            COURANT / PERMITTIVITIES[1],
            jnp.where(m == 2, COURANT / PERMITTIVITIES[2], COURANT / PERMITTIVITIES[3]),
        ),
    )


def fold_cells(tile, nx):
    lane = lane_ids(8)
    folded = jnp.where(lane < 4 * nx, tile[0:8, :], 0.0)
    for g in range(1, tile.shape[0] // 8):
        here = (lane >= 4 * nx) & (lax.rem(lane, nx) == g)
        folded = jnp.where(here, pltpu.roll(tile[8 * g : 8 * g + 8, :], 4 * nx + g, 1), folded)
    return folded


def unfold_cells(folded, rows, nx):
    lane = lane_ids(8)
    groups = [jnp.where(lane < 4 * nx, folded, 0.0)]
    for g in range(1, rows // 8):
        here = (lane < 4 * nx) & (lax.rem(lane, nx) == 0)
        groups.append(jnp.where(here, pltpu.roll(folded, LANES - 4 * nx - g, 1), 0.0))
    return jnp.concatenate(groups, axis=0)


def slab_start(nz, half):
    return (1 - lax.axis_index("gz")) * (nz - half)


def spectra_body(half, nz, dfv, dav, freq, material, after, out, still):
    freqs, nx, ny = dfv.shape[0], dfv.shape[3], dfv.shape[4]
    phase = freq[...] * float(STEP)
    cos, sin = jnp.cos(phase), jnp.sin(phase)
    cs = [jnp.broadcast_to(cos[:, f : f + 1], (ny, half)) for f in range(freqs)]
    sn = [jnp.broadcast_to(sin[:, f : f + 1], (ny, half)) for f in range(freqs)]
    shift = slab_start(nz, half)
    blank = jnp.zeros((ny, LANES - half), jnp.float32)

    def place(a):
        return pltpu.roll(jnp.concatenate([a, blank], axis=1), shift, 1)

    for x in range(nx):
        base = jnp.zeros((ny, half), jnp.float32)
        for c in range(3):
            with_forward = jnp.zeros((ny, half), jnp.float32)
            with_adjoint = jnp.zeros((ny, half), jnp.float32)
            for f in range(freqs):
                rf, jf, ra, ja = dfv[f, 0, c, x], dfv[f, 1, c, x], dav[f, 0, c, x], dav[f, 1, c, x]
                base = base + (rf * ra - jf * ja)
                with_forward = with_forward + (cs[f] * ra + sn[f] * ja)
                with_adjoint = with_adjoint + (cs[f] * rf + sn[f] * jf)
            out[1 + c, x] = place(with_forward)
            out[4 + c, x] = place(with_adjoint)
        out[0, x] = place(base)

    def cells(planes):
        return pack_open([planes(x, slice(0, 8 if x else ny)) for x in range(nx)], nz - 1)

    still[0] = cells(lambda x, rows: out[3, x, rows])
    still[1] = cells(lambda x, rows: out[6, x, rows])
    still[2] = cells(lambda x, rows: update_coefficient(material[x, rows]))


def spectra(df, da, freq, material, after, nz):
    _, _, _, nx, ny, half = df.shape
    return call(
        functools.partial(spectra_body, half, nz),
        "spectra",
        (vmem(7, nx, ny, LANES), vmem(3, ny, LANES)),
        (VMEM,) * 2,
        [VMEM] * 4 + [ANY],
        nbytes=11000000,
    )(df, da, freq, material, after)


def complete_body(hf, ha, zr, layer, hfn, han, below):
    _, nx, ny, nz = hf.shape
    lower = lax.axis_index("gz") == 0
    came = jnp.concatenate([zr[...], pltpu.roll(zr[...], LANES - 4 * nx, 1)], axis=0)
    came = jnp.where(lane_ids(ny) < 4 * nx, came, 0.0)
    above = jnp.where(lower, from_layer_above(came, nx), 0.0)
    below[...] = jnp.where(lower, 0.0, came + from_layer_above(layer[...], nx))
    top = lane_ids(ny) == nz - 1
    for r, (h, hn) in enumerate(((hf, hfn), (ha, han))):
        for c in range(2):
            for x in range(nx):
                hn[c, x] = h[c, x] + jnp.where(top, move(above, packed_lane(r, c, x, nx), nz - 1), 0.0)


def complete(hf, ha, zr, layer):
    _, nx, ny, nz = hf.shape
    part = vmem(2, nx, ny, nz)
    return call(
        complete_body,
        "complete",
        (part, part, vmem(ny, LANES)),
        (VMEM,) * 3,
        [VMEM] * 4,
        nbytes=2000000,
    )(hf, ha, zr, layer)


def electric_body(
    half, owned, ef, ea, hf, ha, hzf, hza, material, xr, yr, zr, first_y, spec, still, freq, layer_map, efn, ean, own, other, tile
):
    runs = ((ef, hf, hzf, efn), (ea, ha, hza, ean))
    _, nx, ny, nz = ef.shape
    phase = freq[...] * float(STEP)
    cos, sin = jnp.cos(phase), jnp.sin(phase)
    both = jnp.sum(cos * cos - sin * sin, axis=1, keepdims=True)
    gz = lax.axis_index("gz")
    lower = gz == 0
    start = slab_start(nz, half)
    slab = layer_map.shape[1]
    cells = jnp.concatenate([layer_map[...], jnp.full((1, LANES - slab), -1, jnp.int32)], axis=1)
    cells = pltpu.roll(jnp.broadcast_to(cells, (8, LANES)), lax.rem(start + LANES - gz * half, LANES), 1)
    lane, row = lane_ids(2 * owned), row_ids(2 * owned)
    inside = (lane >= start) & (lane < start + half)
    cells = jnp.broadcast_to(cells[0:1, :], (2 * owned, LANES))
    ids = lax.rem(row + gz * owned, 2 * owned)
    hot = jnp.where(inside & (cells == ids), 1.0, 0.0).astype(jnp.bfloat16)
    owner = jnp.broadcast_to(layer_map[...], (2 * owned, slab)) == ids[:, :slab]
    share = 1.0 / (3.0 * jnp.sum(jnp.where(owner, 1.0, 0.0), axis=1, keepdims=True))
    middle = jnp.broadcast_to(layer_map[0:1, half - 1 : half], (2 * owned, 1)) == ids[:, 0:1]
    middle_share = jnp.sum(jnp.where(middle, share, 0.0), axis=0, keepdims=True)
    below = zr[...]
    hx_below = [yr[2 * r * nx : (2 * r + 1) * nx, :] - COURANT * first_y[r, 1] for r in range(2)]
    hz_below = [yr[(2 * r + 1) * nx : (2 * r + 2) * nx, :] + COURANT * first_y[r, 0] for r in range(2)]
    dims = (((1,), (1,)), ((), ()))
    group = LANES // ny
    products = []
    for x in range(nx):
        coefficient = update_coefficient(material[x])
        news = []
        for r, (e, h, hz, en) in enumerate(runs):
            at_x, at_y = packed_lane(r, 0, x, nx), packed_lane(r, 1, x, nx)
            hx, hy, hz_here = h[0, x], h[1, x], hz[2, x]
            hy_x, hz_x = (h[1, x - 1], hz[2, x - 1]) if x else (xr[2 * r * ny : (2 * r + 1) * ny, :], xr[(2 * r + 1) * ny : (2 * r + 2) * ny, :])
            hx_y = down_y(hx, hx_below[r][x : x + 1, :])
            hz_y = down_y(hz_here, hz_below[r][x : x + 1, :])
            hx_z = down_z(hx, below, at_x)
            hy_z = down_z(hy, below, at_y)
            ex = e[0, x] + coefficient * ((hz_here - hz_y) - (hy - hy_z))
            ey = e[1, x] + coefficient * ((hx - hx_z) - (hz_here - hz_x))
            ez = e[2, x] + coefficient * ((hy - hy_x) - (hx - hx_y))
            en[0, x] = ex
            en[1, x] = ey
            en[2, x] = ez
            news.append((ex, ey, ez))
        total = spec[0, x]
        for c in range(3):
            f, a = news[0][c], news[1][c]
            total = total + (f * (spec[1 + c, x] + both * a) + a * spec[4 + c, x])
        products.append(total)
        if len(products) == group:
            block = jnp.concatenate(products, axis=0)
            products = []
            sums = jnp.zeros((2 * owned, group * ny), jnp.float32)
            for _ in range(3):
                part = block.astype(jnp.bfloat16)
                block = block - part.astype(jnp.float32)
                sums = sums + lax.dot_general(hot, part, dims, preferred_element_type=jnp.float32)
            sums = sums * share
            where = pl.ds(x // group * owned, owned)
            own[where, :] = sums[:owned]
            other[where, :] = sums[owned:]
    f, a = (pack_open([e[2, x, 0 : 8 if x else ny, :] for x in range(nx)], nz - 1) for e in (efn, ean))
    ratio = COURANT * still[2]
    scaled = ratio * middle_share
    rest = scaled * (still[0] + both * a)
    rest = rest + pltpu.roll(scaled * (still[1] + both * f), nx, 1)
    rest = rest + pltpu.roll(scaled * ratio * both, 2 * nx, 1)
    rest = rest + pltpu.roll(ratio, 3 * nx, 1)
    turned = jnp.concatenate([xr[4 * ny :, :], jnp.zeros((ny - 8, LANES), jnp.float32)], axis=0)
    turned = jnp.transpose(turned)[0:ny, :]
    turned = jnp.concatenate([turned, jnp.zeros((ny, LANES - ny), jnp.float32)], axis=1)
    lane = lane_ids(ny)
    along = jnp.where(lane == 0, turned, jnp.where(lane == nx, move(turned, 1, nx), 0.0))
    along = along + jnp.concatenate([yr[4 * nx : 4 * nx + 8, :], jnp.zeros((ny - 8, LANES), jnp.float32)], axis=0)
    rest = jnp.where(lower, rest, along)
    tile[...] = rest
    other[nx // group * owned :, :] = fold_cells(rest, nx)


def electric(ef, ea, hf, ha, hzf, hza, material, xr, yr, zr, first_y, spec, still, freq, layer_map, half, owned):
    _, nx, ny, nz = ef.shape
    field = vmem(3, nx, ny, nz)
    rows = nx * ny // LANES * owned
    return call(
        functools.partial(electric_body, half, owned),
        "electric",
        (field, field, vmem(rows, LANES), vmem(rows + 8, LANES), vmem(ny, LANES)),
        (VMEM,) * 5,
        [VMEM] * 15,
        nbytes=6700000,
    )(ef, ea, hf, ha, hzf, hza, material, xr, yr, zr, first_y, spec, still, freq, layer_map)


def store_body(ef, ea, hf, ha, hzf, hza, after, efn, ean, hfn, han, sems):
    copies = []
    for r, (e, h, hz, en, hn) in enumerate(((ef, hf, hzf, efn, hfn), (ea, ha, hza, ean, han))):
        for c in range(3):
            copies.append(pltpu.make_async_copy(e.at[c], en.at[c], sems.at[r, c]))
            copies.append(pltpu.make_async_copy((h if c < 2 else hz).at[c], hn.at[c], sems.at[r, 3 + c]))
    for copy in copies:
        copy.start()
    for copy in copies:
        copy.wait()


def store(ef, ea, hf, ha, hzf, hza, after):
    field = f32(*ef.shape)
    return call(
        store_body,
        "store",
        (field,) * 4,
        (ANY,) * 4,
        [VMEM] * 6 + [ANY],
        [pltpu.SemaphoreType.DMA((2, 6))],
        nbytes=3000000,
    )(ef, ea, hf, ha, hzf, hza, after)


def gradient_body(ef, ea, own, tile, came, layer_map, _f, _a, out, efn, ean, plane, rows, result, sems):
    owned, nx, ny = out.shape
    nz = ef.shape[3]
    half = layer_map.shape[1] // 2
    gz = lax.axis_index("gz")
    lower = gz == 0
    sums = own.shape[0]
    mine, theirs = tile[...], unfold_cells(came[sums:, :], tile.shape[0], nx)
    change, cells = jnp.where(lower, mine, theirs), jnp.where(lower, theirs, mine)
    cell = [cells, pltpu.roll(cells, LANES - nx, 1)]
    ratio = jnp.where(lower, pltpu.roll(change, LANES - 3 * nx, 1), 0.0)
    copies = []
    for r, (e, en) in enumerate(((ef, efn), (ea, ean))):
        add = ratio * cell[r]
        plane[r] = e[2, 0] + jnp.where(lane_ids(ny) == nz - 1, move(add, 0, nz - 1), 0.0)
        corner = (lane_ids(8) == nz - 1) & (row_ids(8) == 0)
        for x in range(1, nx):
            rows[r, x - 1] = e[2, x, 0:8, :] + jnp.where(corner, move(add[0:8, :], x, nz - 1), 0.0)
        copies.append(pltpu.make_async_copy(plane.at[r], en.at[2, 0], sems.at[r, 0]))
        copies.append(pltpu.make_async_copy(rows.at[r], en.at[2, 1:nx, 0:8], sems.at[r, 1]))
    for copy in copies:
        copy.start()
    by_a, by_both = pltpu.roll(change, LANES - nx, 1), pltpu.roll(change, LANES - 2 * nx, 1)
    missing = change * cell[0] + by_a * cell[1] + by_both * (cell[0] * cell[1])
    missing = jnp.transpose(missing)[0:nx, 0:ny]
    share = own[...] + came[0:sums, :]
    group = nx * owned // sums
    for x in range(nx):
        block = share[x // group * owned : (x // group + 1) * owned]
        at = x % group * ny
        result[:, x, :] = block[:, at : at + ny]
    middle = layer_map[0:1, half - 1 : half]
    for k in range(owned):
        mine = jnp.broadcast_to(middle == gz * owned + k, (nx, ny))
        result[k] = result[k] + jnp.where(mine, missing, 0.0)
    last = pltpu.make_async_copy(result, out, sems.at[0, 2])
    last.start()
    for copy in copies:
        copy.wait()
    last.wait()


def gradient(ef, ea, own, tile, came, layer_map, efn, ean, owned):
    _, nx, ny, nz = ef.shape
    return pl.pallas_call(
        gradient_body,
        out_shape=(f32(owned, nx, ny), f32(*efn.shape), f32(*ean.shape)),
        in_specs=[VMEM] * 6 + [ANY] * 2,
        out_specs=(ANY,) * 3,
        scratch_shapes=[
            pltpu.VMEM((2, ny, nz), jnp.float32),
            pltpu.VMEM((2, nx - 1, 8, nz), jnp.float32),
            pltpu.VMEM((owned, nx, ny), jnp.float32),
            pltpu.SemaphoreType.DMA((2, 3)),
        ],
        input_output_aliases={6: 1, 7: 2},
        compiler_params=pltpu.CompilerParams(vmem_limit_bytes=32 * MIB),
        cost_estimate=pl.CostEstimate(flops=100000, bytes_accessed=400000, transcendentals=0),
        name="gradient",
    )(ef, ea, own, tile, came, layer_map, efn, ean)


def shards(ef, hf, ea, ha, material, df, da, angular_freq, layer_map):
    _, nx, ny, nz = ef.shape
    half = df.shape[3]
    owned = LAYERS // lax.axis_size("gz")
    freq = angular_freq.reshape(1, -1)
    layer_map = layer_map.reshape(1, -1)
    df = jnp.transpose(df, (0, 1, 2, 4, 5, 3))
    da = jnp.transpose(da, (0, 1, 2, 4, 5, 3))
    xs, first_y, ef, ea, hf, ha, along_x, along_y = first_faces(ef, ea, hf, ha)
    yr = ring(first_y, "gy", -1)
    xr = ring(xs, "gx", -1)
    ys = last_y(ef, ea, hf, ha, xr, along_y)
    hf, ha, layer, top = magnetic(ef, ea, hf, ha, xr, ys)
    hf, ha, xs, zs = last_faces(hf, ha, yr, along_x, layer, top)
    yr = ring(ys, "gy", 1)
    xr = ring(xs, "gx", 1)
    zr = ring(zs, "gz", 1)
    spec, still = spectra(df, da, freq, material, zs, nz)
    hxyf, hxya, below = complete(hf, ha, zr, layer)
    ef, ea, own, other, tile = electric(
        ef, ea, hxyf, hxya, hf, ha, material, xr, yr, below, first_y, spec, still, freq, layer_map, half, owned
    )
    came = ring(other, "gz", 1)
    efn, ean, hfn, han = store(ef, ea, hxyf, hxya, hf, ha, own)
    out, efn, ean = gradient(ef, ea, own, tile, came, layer_map, efn, ean, owned)
    return efn, hfn, ean, han, out


def solution(mesh):
    field = P(None, "gx", "gy", "gz")
    dft = P(None, None, None, "gz", "gx", "gy")
    return jax.shard_map(
        shards,
        mesh=mesh,
        in_specs=(field, field, field, field, P("gx", "gy", "gz"), dft, dft, P(), P()),
        out_specs=(field, field, field, field, P("gz", "gx", "gy")),
        check_vma=False,
    )
```

```python
import functools

import jax
import jax.numpy as jnp
from jax import lax
from jax.experimental import pallas as pl
from jax.experimental.pallas import tpu as pltpu
from jax.sharding import PartitionSpec as P

LAYERS = 16
STEP = 40
PERMITTIVITIES = (1.0, 2.1, 4.0, 12.0)
COURANT = 0.5
LANES = 128
MIB = 1024 * 1024
ANY = pl.BlockSpec(memory_space=pl.ANY)
VMEM = pl.BlockSpec(memory_space=pltpu.VMEM)


def f32(*shape):
    return jax.ShapeDtypeStruct(shape, jnp.float32)


def vmem(*shape):
    return pltpu.VMEM(shape, jnp.float32)


def hbm(x):
    return pltpu.with_memory_space_constraint(x, pltpu.HBM)


def ring(x, axis, by):
    peers = lax.axis_size(axis)
    return lax.ppermute(x, axis, [(i, (i + by) % peers) for i in range(peers)])


def call(body, name, outs, out_specs, in_specs, scratch=(), nbytes=100000, limit=32):
    return pl.pallas_call(
        body,
        out_shape=outs,
        in_specs=in_specs,
        out_specs=out_specs,
        scratch_shapes=list(scratch),
        compiler_params=pltpu.CompilerParams(vmem_limit_bytes=limit * MIB),
        cost_estimate=pl.CostEstimate(flops=nbytes, bytes_accessed=nbytes, transcendentals=0),
        name=name,
    )


def lane_ids(rows):
    return lax.broadcasted_iota(jnp.int32, (rows, LANES), 1)


def row_ids(rows):
    return lax.broadcasted_iota(jnp.int32, (rows, LANES), 0)


def move(a, source, target):
    shift = (target - source) % LANES
    return pltpu.roll(a, shift, 1) if shift else a


def up_y(a):
    n = a.shape[0]
    return jnp.where(row_ids(n) == n - 1, 0.0, pltpu.roll(a, n - 1, 0))


def down_y(a, row):
    return jnp.where(row_ids(a.shape[0]) == 0, jnp.broadcast_to(row, a.shape), pltpu.roll(a, 1, 0))


def up_z(a):
    n = a.shape[1]
    return jnp.where(lane_ids(a.shape[0]) == n - 1, 0.0, pltpu.roll(a, n - 1, 1))


def down_z(a, packed, lane):
    return jnp.where(lane_ids(a.shape[0]) == 0, move(packed, lane, 0), pltpu.roll(a, 1, 1))


def first_faces_body(ef, ea, hf, ha, xs, ys, evf, eva, hvf, hva, along_x, along_y, sems):
    fields = (evf, eva)
    _, nx, ny, _ = ef.shape
    copies = {}
    for k, (pair, held) in enumerate((((ef, ea), (evf, eva)), ((hf, ha), (hvf, hva)))):
        for c in range(3):
            for r in range(2):
                copies[k, c, r] = pltpu.make_async_copy(pair[r].at[c], held[r].at[c], sems.at[k, r, c])
                copies[k, c, r].start()
    for c in range(3):
        for r, v in enumerate(fields):
            copies[0, c, r].wait()
            if c != 1:
                for x in range(nx):
                    ys[r, c // 2, x : x + 1, :] = v[c, x, 0:1, :]
            if c:
                xs[r, c - 1] = v[c, 0]
    lane, lane_8 = lane_ids(ny), lane_ids(8)
    by_x = jnp.zeros((ny, LANES), jnp.float32)
    by_y = jnp.zeros((8, LANES), jnp.float32)
    for r, e in enumerate(fields):
        by_x = jnp.where(lane == r, move(e[0, nx - 1], 0, r), by_x)
        for x in range(nx):
            by_y = jnp.where(lane_8 == r * nx + x, move(e[1, x, ny - 8 : ny, :], 0, r * nx + x), by_y)
    turned = jnp.transpose(by_x)[0:8, :]
    along_x[...] = jnp.concatenate([turned, jnp.zeros((8, LANES - ny), jnp.float32)], axis=1)
    along_y[...] = jnp.where(row_ids(8) == 0, pltpu.roll(by_y, 1, 0), 0.0)
    for c in range(3):
        for r in range(2):
            copies[1, c, r].wait()


def first_faces(ef, ea, hf, ha):
    _, nx, ny, nz = ef.shape
    field = vmem(3, nx, ny, nz)
    return call(
        first_faces_body,
        "first_faces",
        (vmem(2, 2, ny, nz), vmem(2, 2, nx, nz)) + (field,) * 4 + (vmem(8, LANES), vmem(8, LANES)),
        (VMEM,) * 8,
        [ANY] * 4,
        [pltpu.SemaphoreType.DMA((2, 2, 3))],
        nbytes=3000000,
    )(hbm(ef), hbm(ea), hbm(hf), hbm(ha))


def magnetic_update(e, h, x, rows, next_x, r):
    nx = e.shape[1]
    ex, ey, ez = e[0, x, rows], e[1, x, rows], e[2, x, rows]
    ey_x, ez_x = (e[1, x + 1, rows], e[2, x + 1, rows]) if x + 1 < nx else (next_x[r, 0, rows], next_x[r, 1, rows])
    ex_y = up_y(ex)
    ez_y = up_y(ez)
    ex_z = up_z(ex)
    ey_z = up_z(ey)
    hx = h[0, x, rows] - COURANT * ((ez_y - ez) - (ey_z - ey))
    hy = h[1, x, rows] - COURANT * ((ex_z - ex) - (ez_x - ez))
    hz = h[2, x, rows] - COURANT * ((ey_x - ey) - (ex_y - ex))
    return hx, hy, hz


def last_y_body(ef, ea, hf, ha, xr, along_y, ys):
    _, nx, ny, _ = ef.shape
    last = slice(ny - 8, ny)
    for r, (e, h) in enumerate(((ef, hf), (ea, ha))):
        for x in range(nx):
            hx, _, hz = magnetic_update(e, h, x, last, xr, r)
            for c, a in enumerate((hx, hz)):
                at = packed_lane(r, c, x, nx)
                ys[at : at + 1, :] = a[7:8, :]
    ys[4 * nx : 4 * nx + 8, :] = along_y[...]


def last_y(ef, ea, hf, ha, xr, along_y):
    _, nx, ny, nz = ef.shape
    return call(
        last_y_body,
        "last_y",
        vmem(4 * nx + 80, nz),
        VMEM,
        [VMEM] * 6,
        nbytes=500000,
    )(ef, ea, hf, ha, xr, along_y)


def magnetic_body(ef, ea, hf, ha, xr, after, hfn, han, layer, top):
    _, nx, ny, nz = ef.shape
    for x in range(nx):
        for r, (e, h, hn) in enumerate(((ef, hf, hfn), (ea, ha, han))):
            hn[0, x], hn[1, x], hn[2, x] = magnetic_update(e, h, x, slice(0, ny), xr, r)
    layer[...] = pack_layer((ef, ea), nx, ny, 0)
    top[...] = pack_layer((hfn, han), nx, ny, nz - 1)


def magnetic(ef, ea, hf, ha, xr, after):
    _, nx, ny, nz = ef.shape
    field = vmem(3, nx, ny, nz)
    return call(
        magnetic_body,
        "magnetic",
        (field, field, vmem(ny, LANES), vmem(ny, LANES)),
        (VMEM,) * 4,
        [VMEM] * 5 + [ANY],
        nbytes=4800000,
    )(ef, ea, hf, ha, xr, after)


def last_faces_body(hf, ha, yr, along_x, layer, top, hfn, han, xs, zs):
    _, nx, ny, nz = hf.shape
    last = slice(ny - 8, ny)
    edge, lane = row_ids(8) == 7, lane_ids(8)
    rows = top[last, :]
    for r, (h, hn) in enumerate(((hf, hfn), (ha, han))):
        for x in range(nx):
            hx = h[0, x, last, :] - COURANT * jnp.where(edge, jnp.broadcast_to(yr[r, 1, x : x + 1, :], (8, nz)), 0.0)
            hz = h[2, x, last, :] + COURANT * jnp.where(edge, jnp.broadcast_to(yr[r, 0, x : x + 1, :], (8, nz)), 0.0)
            hn[0, x, last, :] = hx
            hn[2, x, last, :] = hz
            to = packed_lane(r, 0, x, nx)
            rows = jnp.where(lane == to, move(hx, nz - 1, to), rows)
        at = r * 2 * ny
        xs[at : at + ny, :] = h[1, nx - 1]
        xs[at + ny : at + 2 * ny - 8, :] = h[2, nx - 1, 0 : ny - 8, :]
        xs[at + 2 * ny - 8 : at + 2 * ny, :] = hz
    xs[4 * ny :, :] = along_x[...]
    lower = lax.axis_index("gz") == 0
    zs[...] = jnp.where(lower, top[...], layer[...])
    zs[last, :] = jnp.where(lower, rows, layer[last, :])


def last_faces(hf, ha, yr, along_x, layer, top):
    _, nx, ny, nz = hf.shape
    field = vmem(3, nx, ny, nz)
    return pl.pallas_call(
        last_faces_body,
        out_shape=(field, field, vmem(4 * ny + 8, nz), vmem(ny, LANES)),
        in_specs=[VMEM] * 6,
        out_specs=(VMEM,) * 4,
        input_output_aliases={0: 0, 1: 1},
        compiler_params=pltpu.CompilerParams(vmem_limit_bytes=32 * MIB),
        cost_estimate=pl.CostEstimate(flops=500000, bytes_accessed=500000, transcendentals=0),
        name="last_faces",
    )(hf, ha, yr, along_x, layer, top)


def packed_lane(r, c, x, nx):
    return (r * 2 + c) * nx + x


def pack_layer(fields, nx, ny, z):
    lane = lane_ids(ny)
    total = jnp.zeros((ny, LANES), jnp.float32)
    for r, f in enumerate(fields):
        for c in range(2):
            for x in range(nx):
                to = packed_lane(r, c, x, nx)
                total = jnp.where(lane == to, move(f[c, x], z, to), total)
    return total


def from_layer_above(tile, nx):
    first = lax.rem(lane_ids(tile.shape[0]) // nx, 2) == 0
    return COURANT * jnp.where(first, pltpu.roll(tile, LANES - nx, 1), -pltpu.roll(tile, nx, 1))


def pack_open(planes, z):
    ny = planes[0].shape[0]
    lane_8 = lane_ids(8)
    first = jnp.where(lane_ids(ny) == 0, move(planes[0], z, 0), 0.0)
    top = first[0:8, :]
    for x in range(1, len(planes)):
        top = jnp.where(lane_8 == x, move(planes[x], z, x), top)
    return jnp.concatenate([top, first[8:, :]], axis=0)


def update_coefficient(m):
    return jnp.where(
        m == 0,
        COURANT / PERMITTIVITIES[0],
        jnp.where(
            m == 1,
            COURANT / PERMITTIVITIES[1],
            jnp.where(m == 2, COURANT / PERMITTIVITIES[2], COURANT / PERMITTIVITIES[3]),
        ),
    )


def slab_start(nz, half):
    return (1 - lax.axis_index("gz")) * (nz - half)


def spectra_body(half, nz, dfv, dav, freq, material, after, out, still):
    freqs, nx, ny = dfv.shape[0], dfv.shape[3], dfv.shape[4]
    phase = freq[...] * float(STEP)
    cos, sin = jnp.cos(phase), jnp.sin(phase)
    cs = [jnp.broadcast_to(cos[:, f : f + 1], (ny, half)) for f in range(freqs)]
    sn = [jnp.broadcast_to(sin[:, f : f + 1], (ny, half)) for f in range(freqs)]
    shift = slab_start(nz, half)
    blank = jnp.zeros((ny, LANES - half), jnp.float32)

    def place(a):
        return pltpu.roll(jnp.concatenate([a, blank], axis=1), shift, 1)

    for x in range(nx):
        base = jnp.zeros((ny, half), jnp.float32)
        for c in range(3):
            with_forward = jnp.zeros((ny, half), jnp.float32)
            with_adjoint = jnp.zeros((ny, half), jnp.float32)
            for f in range(freqs):
                rf, jf, ra, ja = dfv[f, 0, c, x], dfv[f, 1, c, x], dav[f, 0, c, x], dav[f, 1, c, x]
                base = base + (rf * ra - jf * ja)
                with_forward = with_forward + (cs[f] * ra + sn[f] * ja)
                with_adjoint = with_adjoint + (cs[f] * rf + sn[f] * jf)
            out[1 + c, x] = place(with_forward)
            out[4 + c, x] = place(with_adjoint)
        out[0, x] = place(base)

    def cells(planes):
        return pack_open([planes(x, slice(0, 8 if x else ny)) for x in range(nx)], nz - 1)

    still[0] = cells(lambda x, rows: out[3, x, rows])
    still[1] = cells(lambda x, rows: out[6, x, rows])
    still[2] = cells(lambda x, rows: update_coefficient(material[x, rows]))


def spectra(df, da, freq, material, after, nz):
    _, _, _, nx, ny, half = df.shape
    return call(
        functools.partial(spectra_body, half, nz),
        "spectra",
        (vmem(7, nx, ny, LANES), vmem(3, ny, LANES)),
        (VMEM,) * 2,
        [VMEM] * 4 + [ANY],
        nbytes=11000000,
    )(df, da, freq, material, after)


def complete_body(hf, ha, zr, layer, hfn, han, below):
    _, nx, ny, nz = hf.shape
    lower = lax.axis_index("gz") == 0
    came = zr[...]
    above = jnp.where(lower, from_layer_above(came, nx), 0.0)
    below[...] = jnp.where(lower, 0.0, came + from_layer_above(layer[...], nx))
    top = lane_ids(ny) == nz - 1
    for r, (h, hn) in enumerate(((hf, hfn), (ha, han))):
        for c in range(2):
            for x in range(nx):
                hn[c, x] = h[c, x] + jnp.where(top, move(above, packed_lane(r, c, x, nx), nz - 1), 0.0)


def complete(hf, ha, zr, layer):
    _, nx, ny, nz = hf.shape
    part = vmem(2, nx, ny, nz)
    return call(
        complete_body,
        "complete",
        (part, part, vmem(ny, LANES)),
        (VMEM,) * 3,
        [VMEM] * 4,
        nbytes=2000000,
    )(hf, ha, zr, layer)


def electric_body(
    half, owned, ef, ea, hf, ha, hzf, hza, material, xr, yr, zr, first_y, spec, still, freq, layer_map, efn, ean, own, other, tile
):
    runs = ((ef, hf, hzf, efn), (ea, ha, hza, ean))
    _, nx, ny, nz = ef.shape
    phase = freq[...] * float(STEP)
    cos, sin = jnp.cos(phase), jnp.sin(phase)
    both = jnp.sum(cos * cos - sin * sin, axis=1, keepdims=True)
    gz = lax.axis_index("gz")
    lower = gz == 0
    start = slab_start(nz, half)
    slab = layer_map.shape[1]
    cells = jnp.concatenate([layer_map[...], jnp.full((1, LANES - slab), -1, jnp.int32)], axis=1)
    cells = pltpu.roll(jnp.broadcast_to(cells, (8, LANES)), lax.rem(start + LANES - gz * half, LANES), 1)
    lane, row = lane_ids(2 * owned), row_ids(2 * owned)
    inside = (lane >= start) & (lane < start + half)
    cells = jnp.broadcast_to(cells[0:1, :], (2 * owned, LANES))
    ids = lax.rem(row + gz * owned, 2 * owned)
    hot = jnp.where(inside & (cells == ids), 1.0, 0.0).astype(jnp.bfloat16)
    owner = jnp.broadcast_to(layer_map[...], (2 * owned, slab)) == ids[:, :slab]
    share = 1.0 / (3.0 * jnp.sum(jnp.where(owner, 1.0, 0.0), axis=1, keepdims=True))
    middle = jnp.broadcast_to(layer_map[0:1, half - 1 : half], (2 * owned, 1)) == ids[:, 0:1]
    middle_share = jnp.sum(jnp.where(middle, share, 0.0), axis=0, keepdims=True)
    below = zr[...]
    hx_below = [yr[2 * r * nx : (2 * r + 1) * nx, :] - COURANT * first_y[r, 1] for r in range(2)]
    hz_below = [yr[(2 * r + 1) * nx : (2 * r + 2) * nx, :] + COURANT * first_y[r, 0] for r in range(2)]
    dims = (((1,), (1,)), ((), ()))
    group = LANES // ny
    products = []
    for x in range(nx):
        coefficient = update_coefficient(material[x])
        news = []
        for r, (e, h, hz, en) in enumerate(runs):
            at_x, at_y = packed_lane(r, 0, x, nx), packed_lane(r, 1, x, nx)
            hx, hy, hz_here = h[0, x], h[1, x], hz[2, x]
            hy_x, hz_x = (h[1, x - 1], hz[2, x - 1]) if x else (xr[2 * r * ny : (2 * r + 1) * ny, :], xr[(2 * r + 1) * ny : (2 * r + 2) * ny, :])
            hx_y = down_y(hx, hx_below[r][x : x + 1, :])
            hz_y = down_y(hz_here, hz_below[r][x : x + 1, :])
            hx_z = down_z(hx, below, at_x)
            hy_z = down_z(hy, below, at_y)
            ex = e[0, x] + coefficient * ((hz_here - hz_y) - (hy - hy_z))
            ey = e[1, x] + coefficient * ((hx - hx_z) - (hz_here - hz_x))
            ez = e[2, x] + coefficient * ((hy - hy_x) - (hx - hx_y))
            en[0, x] = ex
            en[1, x] = ey
            en[2, x] = ez
            news.append((ex, ey, ez))
        total = spec[0, x]
        for c in range(3):
            f, a = news[0][c], news[1][c]
            total = total + (f * (spec[1 + c, x] + both * a) + a * spec[4 + c, x])
        products.append(total)
        if len(products) == group:
            block = jnp.concatenate(products, axis=0)
            products = []
            sums = jnp.zeros((2 * owned, group * ny), jnp.float32)
            for _ in range(2):
                part = block.astype(jnp.bfloat16)
                block = block - part.astype(jnp.float32)
                sums = sums + lax.dot_general(hot, part, dims, preferred_element_type=jnp.float32)
            sums = sums * share
            where = pl.ds(x // group * owned, owned)
            own[where, :] = sums[:owned]
            other[where, :] = sums[owned:]
    f, a = (pack_open([e[2, x, 0 : 8 if x else ny, :] for x in range(nx)], nz - 1) for e in (efn, ean))
    ratio = COURANT * still[2]
    scaled = ratio * middle_share
    rest = scaled * (still[0] + both * a)
    rest = rest + pltpu.roll(scaled * (still[1] + both * f), nx, 1)
    rest = rest + pltpu.roll(scaled * ratio * both, 2 * nx, 1)
    rest = rest + pltpu.roll(ratio, 3 * nx, 1)
    turned = jnp.concatenate([xr[4 * ny :, :], jnp.zeros((ny - 8, LANES), jnp.float32)], axis=0)
    turned = jnp.transpose(turned)[0:ny, :]
    turned = jnp.concatenate([turned, jnp.zeros((ny, LANES - ny), jnp.float32)], axis=1)
    lane = lane_ids(ny)
    along = jnp.where(lane == 0, turned, jnp.where(lane == nx, move(turned, 1, nx), 0.0))
    along = along + jnp.concatenate([yr[4 * nx : 4 * nx + 8, :], jnp.zeros((ny - 8, LANES), jnp.float32)], axis=0)
    rest = jnp.where(lower, rest, along)
    tile[...] = rest
    other[nx // group * owned :, :] = rest


def electric(ef, ea, hf, ha, hzf, hza, material, xr, yr, zr, first_y, spec, still, freq, layer_map, half, owned):
    _, nx, ny, nz = ef.shape
    field = vmem(3, nx, ny, nz)
    rows = nx * ny // LANES * owned
    return call(
        functools.partial(electric_body, half, owned),
        "electric",
        (field, field, vmem(rows, LANES), vmem(rows + ny, LANES), vmem(ny, LANES)),
        (VMEM,) * 5,
        [VMEM] * 15,
        nbytes=6700000,
    )(ef, ea, hf, ha, hzf, hza, material, xr, yr, zr, first_y, spec, still, freq, layer_map)


def store_body(ef, ea, hf, ha, hzf, hza, after, efn, ean, hfn, han, sems):
    copies = []
    for r, (e, h, hz, en, hn) in enumerate(((ef, hf, hzf, efn, hfn), (ea, ha, hza, ean, han))):
        for c in range(3):
            copies.append(pltpu.make_async_copy(e.at[c], en.at[c], sems.at[r, c]))
            copies.append(pltpu.make_async_copy((h if c < 2 else hz).at[c], hn.at[c], sems.at[r, 3 + c]))
    for copy in copies:
        copy.start()
    for copy in copies:
        copy.wait()


def store(ef, ea, hf, ha, hzf, hza, after):
    field = f32(*ef.shape)
    return call(
        store_body,
        "store",
        (field,) * 4,
        (ANY,) * 4,
        [VMEM] * 6 + [ANY],
        [pltpu.SemaphoreType.DMA((2, 6))],
        nbytes=3000000,
    )(ef, ea, hf, ha, hzf, hza, after)


def gradient_body(ef, ea, own, tile, came, layer_map, _f, _a, out, efn, ean, plane, rows, result, sems):
    owned, nx, ny = out.shape
    nz = ef.shape[3]
    half = layer_map.shape[1] // 2
    gz = lax.axis_index("gz")
    lower = gz == 0
    sums = own.shape[0]
    mine, theirs = tile[...], came[sums:, :]
    change, cells = jnp.where(lower, mine, theirs), jnp.where(lower, theirs, mine)
    cell = [cells, pltpu.roll(cells, LANES - nx, 1)]
    ratio = jnp.where(lower, pltpu.roll(change, LANES - 3 * nx, 1), 0.0)
    copies = []
    for r, (e, en) in enumerate(((ef, efn), (ea, ean))):
        add = ratio * cell[r]
        plane[r] = e[2, 0] + jnp.where(lane_ids(ny) == nz - 1, move(add, 0, nz - 1), 0.0)
        corner = (lane_ids(8) == nz - 1) & (row_ids(8) == 0)
        for x in range(1, nx):
            rows[r, x - 1] = e[2, x, 0:8, :] + jnp.where(corner, move(add[0:8, :], x, nz - 1), 0.0)
        copies.append(pltpu.make_async_copy(plane.at[r], en.at[2, 0], sems.at[r, 0]))
        copies.append(pltpu.make_async_copy(rows.at[r], en.at[2, 1:nx, 0:8], sems.at[r, 1]))
    for copy in copies:
        copy.start()
    by_a, by_both = pltpu.roll(change, LANES - nx, 1), pltpu.roll(change, LANES - 2 * nx, 1)
    missing = change * cell[0] + by_a * cell[1] + by_both * (cell[0] * cell[1])
    missing = jnp.transpose(missing)[0:nx, 0:ny]
    share = own[...] + came[0:sums, :]
    group = nx * owned // sums
    for x in range(nx):
        block = share[x // group * owned : (x // group + 1) * owned]
        at = x % group * ny
        result[:, x, :] = block[:, at : at + ny]
    middle = layer_map[0:1, half - 1 : half]
    for k in range(owned):
        mine = jnp.broadcast_to(middle == gz * owned + k, (nx, ny))
        result[k] = result[k] + jnp.where(mine, missing, 0.0)
    last = pltpu.make_async_copy(result, out, sems.at[0, 2])
    last.start()
    for copy in copies:
        copy.wait()
    last.wait()


def gradient(ef, ea, own, tile, came, layer_map, efn, ean, owned):
    _, nx, ny, nz = ef.shape
    return pl.pallas_call(
        gradient_body,
        out_shape=(f32(owned, nx, ny), f32(*efn.shape), f32(*ean.shape)),
        in_specs=[VMEM] * 6 + [ANY] * 2,
        out_specs=(ANY,) * 3,
        scratch_shapes=[
            pltpu.VMEM((2, ny, nz), jnp.float32),
            pltpu.VMEM((2, nx - 1, 8, nz), jnp.float32),
            pltpu.VMEM((owned, nx, ny), jnp.float32),
            pltpu.SemaphoreType.DMA((2, 3)),
        ],
        input_output_aliases={6: 1, 7: 2},
        compiler_params=pltpu.CompilerParams(vmem_limit_bytes=32 * MIB),
        cost_estimate=pl.CostEstimate(flops=100000, bytes_accessed=400000, transcendentals=0),
        name="gradient",
    )(ef, ea, own, tile, came, layer_map, efn, ean)


def shards(ef, hf, ea, ha, material, df, da, angular_freq, layer_map):
    _, nx, ny, nz = ef.shape
    half = df.shape[3]
    owned = LAYERS // lax.axis_size("gz")
    freq = angular_freq.reshape(1, -1)
    layer_map = layer_map.reshape(1, -1)
    df = jnp.transpose(df, (0, 1, 2, 4, 5, 3))
    da = jnp.transpose(da, (0, 1, 2, 4, 5, 3))
    xs, first_y, ef, ea, hf, ha, along_x, along_y = first_faces(ef, ea, hf, ha)
    yr = ring(first_y, "gy", -1)
    xr = ring(xs, "gx", -1)
    ys = last_y(ef, ea, hf, ha, xr, along_y)
    hf, ha, layer, top = magnetic(ef, ea, hf, ha, xr, ys)
    hf, ha, xs, zs = last_faces(hf, ha, yr, along_x, layer, top)
    yr = ring(ys, "gy", 1)
    xr = ring(xs, "gx", 1)
    zr = ring(zs, "gz", 1)
    spec, still = spectra(df, da, freq, material, zs, nz)
    hxyf, hxya, below = complete(hf, ha, zr, layer)
    ef, ea, own, other, tile = electric(
        ef, ea, hxyf, hxya, hf, ha, material, xr, yr, below, first_y, spec, still, freq, layer_map, half, owned
    )
    came = ring(other, "gz", 1)
    efn, ean, hfn, han = store(ef, ea, hxyf, hxya, hf, ha, own)
    out, efn, ean = gradient(ef, ea, own, tile, came, layer_map, efn, ean, owned)
    return efn, hfn, ean, han, out


def solution(mesh):
    field = P(None, "gx", "gy", "gz")
    dft = P(None, None, None, "gz", "gx", "gy")
    return jax.shard_map(
        shards,
        mesh=mesh,
        in_specs=(field, field, field, field, P("gx", "gy", "gz"), dft, dft, P(), P()),
        out_specs=(field, field, field, field, P("gz", "gx", "gy")),
        check_vma=False,
    )
```
